32 devices in a mesh: groups: 2 (over y), wide: 4 (over z), narrow: 2 (over x), sub: 2 (over core).
Axes of the slice: x: 2, y: 2, z: 4, core: 2. Of those that a mesh axis runs over, the one named last changes fastest.
Arguments:
- tokens: bfloat16 [96, 8192], P(('groups', 'wide'), ('narrow', 'sub')), parts along dimension 0, may hold values from -6 to 6
- gate_weight: bfloat16 [8192, 26624], P(('narrow', 'sub'), 'wide'), may hold values from -0.0625 to 0.0625
- up_weight: bfloat16 [8192, 26624], P(('narrow', 'sub'), 'wide'), may hold values from -0.0625 to 0.0625
- down_weight: bfloat16 [26624, 8192], P('wide', ('narrow', 'sub')), may hold values from -0.0390625 to 0.0390625
Outputs:
- mixed: bfloat16 [96, 8192], P(('groups', 'wide'), ('narrow', 'sub')), parts along dimension 0
The draws below stay inside these ranges and needn't reach their ends.
There are 2 independent parts, one for each index of `groups`. The reference program is written for one: setup_inputs(seed, part) draws one part's arguments, and reference() takes and returns one part's arrays. A program takes and returns all parts, laid end to end along the dimension named above; an argument that names none is the same for every part. Nothing has to cross between parts.
All inputs are finite; a program needn't handle non-finite values.
Results may differ from the reference program's by a relative error of at most 0.0049.
Values may be sent and summed in bfloat16 or wider, within the bound.
No kernel may reach another device: no remote copies, remote signals or barrier semaphores. Data moves between devices by JAX's collectives and lax.ppermute only.
A program may use at most 192 MiB of HBM per device.

```python
import jax
import jax.numpy as jnp

D = 8192
FF = 26624
ROWS = 48


def levels(own_key, dims, pieces, smallest, top_value):
    loudness, own = 1.0, jax.random.fold_in(own_key, 6)
    for position, shards_of in pieces:
        heights = jnp.exp(jax.random.uniform(jax.random.fold_in(own, position), (shards_of,), jnp.float32, smallest / len(pieces), top_value / len(pieces)))
        loudness = loudness * jnp.repeat(heights, dims[position] // shards_of).reshape([-1 if axis == position else 1 for axis in range(len(dims))])
    return loudness


def scatter_about(own_key, extent, width, most, cuts=(), kind=jnp.bfloat16):
    entries = jax.random.normal(own_key, extent, jnp.float32) * width
    if len(cuts) > 0:
        entries = levels(own_key, extent, cuts, -0.22, 0.18) * entries
    return jnp.clip(entries, min=-most, max=most).astype(kind)


def setup_inputs(seed: int = 0, part: int = 0) -> dict:
    key_list = jax.random.split(jax.random.key(seed), 5)
    part_keys = jax.random.split(jax.random.fold_in(key_list[4], part), 5)
    return {
        "tokens": scatter_about(part_keys[0], (ROWS, D), 1.0, 6.0, ((0, 4), (1, 4))),
        "gate_weight": scatter_about(key_list[1], (D, FF), D ** -0.5, 0.0625, ((0, 4), (1, 4))),
        "up_weight": scatter_about(key_list[2], (D, FF), D ** -0.5, 0.0625, ((0, 4), (1, 4))),
        "down_weight": scatter_about(key_list[3], (FF, D), FF ** -0.5, 0.0390625, ((0, 4), (1, 4))),
    }


def reference(tokens, gate_weight, up_weight, down_weight):
    gate_sums = jnp.dot(tokens, gate_weight, preferred_element_type=jnp.float32)
    up_sums = jnp.dot(tokens, up_weight, preferred_element_type=jnp.float32)
    hidden = (jax.nn.silu(gate_sums) * up_sums).astype(jnp.bfloat16)
    return jnp.dot(hidden, down_weight, preferred_element_type=jnp.float32).astype(jnp.bfloat16)
```

```python
import jax
import jax.numpy as jnp
from jax import lax
from jax.sharding import PartitionSpec as P

BF16 = jnp.bfloat16
F32 = jnp.float32


def activate(gate_sums, up_sums):
    return (jax.nn.silu(gate_sums) * up_sums).astype(BF16)


def general(tokens, gate_weight, up_weight, down_weight):
    section = lax.all_gather(tokens, "wide", axis=0, tiled=True)
    gate_part = jnp.dot(section, gate_weight, preferred_element_type=F32)
    up_part = jnp.dot(section, up_weight, preferred_element_type=F32)
    gate_sums = lax.psum(gate_part, ("narrow", "sub"))
    up_sums = lax.psum(up_part, ("narrow", "sub"))
    mixed = lax.psum_scatter(
        jnp.dot(activate(gate_sums, up_sums), down_weight, preferred_element_type=F32),
        "wide",
        scatter_dimension=0,
        tiled=True,
    )
    return mixed.astype(BF16)


def swap(x, axis):
    return lax.ppermute(x, axis, [(0, 1), (1, 0)])


def place(wide, narrow, sub):
    return (wide * 2 + narrow) * 2 + sub


def partner(position, wide, narrow, sub):
    return (wide + (position ^ (2 * sub + narrow))) % 4


def moves(position):
    return [
        (place(w, n, s), place(partner(position, w, n, s), n, s))
        for w in range(4)
        for n in range(2)
        for s in range(2)
    ]


AXES = ("wide", "narrow", "sub")


def shared(tokens, gate_weight, up_weight, down_weight):
    half = gate_weight.shape[1] // 2
    rows = tokens.shape[0]
    group = lax.axis_index("groups")
    pair = jnp.concatenate([tokens, swap(tokens, "groups")], axis=0)
    section = jnp.concatenate(
        [lax.ppermute(pair, AXES, [(owner, device) for device, owner in moves(p)]) for p in range(4)], axis=0
    )
    gate_half = lax.dynamic_slice_in_dim(gate_weight, group * half, half, axis=1)
    up_half = lax.dynamic_slice_in_dim(up_weight, group * half, half, axis=1)
    down_half = lax.dynamic_slice_in_dim(down_weight, group * half, half, axis=0)
    gate_part = jnp.dot(section, gate_half, preferred_element_type=F32)
    up_part = jnp.dot(section, up_half, preferred_element_type=F32)

    own = 4 * rows
    both = jnp.concatenate([gate_part, up_part], axis=1)
    both = both[:own] + swap(both[own:], "sub")
    own = 2 * rows
    sums = both[:own] + swap(both[own:].astype(BF16), "narrow").astype(F32)
    hidden = activate(sums[:, :half], sums[:, half:])
    hidden = jnp.concatenate([hidden, swap(hidden, "narrow")], axis=0)
    hidden = jnp.concatenate([hidden, swap(hidden, "sub")], axis=0)

    mixed = jnp.dot(hidden, down_half, preferred_element_type=F32).reshape(4, 2, rows, -1)
    mixed = mixed[:, 0] + swap(mixed[:, 1].astype(BF16), "groups").astype(F32)
    out = sum(lax.ppermute(mixed[p], AXES, moves(p)) for p in range(4))
    return out.astype(BF16)


def solution(mesh):
    placed = (
        P(("groups", "wide"), ("narrow", "sub")),
        P(("narrow", "sub"), "wide"),
        P(("narrow", "sub"), "wide"),
        P("wide", ("narrow", "sub")),
    )
    sizes = tuple(mesh.shape[axis] for axis in ("groups", "wide", "narrow", "sub"))
    return jax.shard_map(
        shared if sizes == (2, 4, 2, 2) else general,
        mesh=mesh,
        in_specs=placed,
        out_specs=P(("groups", "wide"), ("narrow", "sub")),
        check_vma=False,
    )
```

```python
import jax
import jax.numpy as jnp
from jax import lax
from jax.sharding import PartitionSpec as P

BF16 = jnp.bfloat16
F32 = jnp.float32


def activate(gate_sums, up_sums):
    return (jax.nn.silu(gate_sums) * up_sums).astype(BF16)


def general(tokens, gate_weight, up_weight, down_weight):
    section = lax.all_gather(tokens, "wide", axis=0, tiled=True)
    gate_part = jnp.dot(section, gate_weight, preferred_element_type=F32)
    up_part = jnp.dot(section, up_weight, preferred_element_type=F32)
    gate_sums = lax.psum(gate_part, ("narrow", "sub"))
    up_sums = lax.psum(up_part, ("narrow", "sub"))
    mixed = lax.psum_scatter(
        jnp.dot(activate(gate_sums, up_sums), down_weight, preferred_element_type=F32),
        "wide",
        scatter_dimension=0,
        tiled=True,
    )
    return mixed.astype(BF16)


def swap(x, axis):
    return lax.ppermute(x, axis, [(0, 1), (1, 0)])


PARTS = ("groups", "wide")


def quarters(x, core, chip):
    x = x.reshape(2, 2, -1, x.shape[-1])
    x = jnp.where(core == 0, x, x[::-1])
    x = jnp.where(chip == 0, x, x[:, ::-1])
    return x.reshape(-1, x.shape[-1])


def shared(tokens, gate_weight, up_weight, down_weight):
    half = gate_weight.shape[1] // 2
    rows, features = tokens.shape
    group, chip, core = (lax.axis_index(axis) for axis in ("groups", "narrow", "sub"))
    lined = jnp.broadcast_to(tokens.reshape(1, -1, 128), (8, rows * features // 128, 128))
    section = lax.all_to_all(lined, PARTS, 0, 0, tiled=True).reshape(8 * rows, features)
    section = quarters(section, core, chip)
    gate_half = lax.dynamic_slice_in_dim(gate_weight, group * half, half, axis=1)
    up_half = lax.dynamic_slice_in_dim(up_weight, group * half, half, axis=1)
    down_half = lax.dynamic_slice_in_dim(down_weight, group * half, half, axis=0)
    gate_part = jnp.dot(section, gate_half, preferred_element_type=F32)
    up_part = jnp.dot(section, up_half, preferred_element_type=F32)

    own = 4 * rows
    both = jnp.concatenate([gate_part, up_part], axis=1)
    both = both[:own] + swap(both[own:], "sub")
    own = 2 * rows
    sums = both[:own] + swap(both[own:].astype(BF16), "narrow").astype(F32)
    hidden = activate(sums[:, :half], sums[:, half:])
    hidden = jnp.concatenate([hidden, swap(hidden, "narrow")], axis=0)
    hidden = jnp.concatenate([hidden, swap(hidden, "sub")], axis=0)

    mixed = jnp.dot(hidden, down_half, preferred_element_type=F32)
    mixed = quarters(mixed.astype(BF16), core, chip).reshape(8, -1, 128)
    mixed = lax.all_to_all(mixed, PARTS, 0, 0, tiled=True).astype(F32)
    return jnp.sum(mixed, axis=0).astype(BF16).reshape(rows, features)


def solution(mesh):
    placed = (
        P(("groups", "wide"), ("narrow", "sub")),
        P(("narrow", "sub"), "wide"),
        P(("narrow", "sub"), "wide"),
        P("wide", ("narrow", "sub")),
    )
    sizes = tuple(mesh.shape[axis] for axis in ("groups", "wide", "narrow", "sub"))
    return jax.shard_map(
        shared if sizes == (2, 4, 2, 2) else general,
        mesh=mesh,
        in_specs=placed,
        out_specs=P(("groups", "wide"), ("narrow", "sub")),
        check_vma=False,
    )
```

```python
import functools

import jax
import jax.numpy as jnp
from jax import lax
from jax.experimental import pallas as pl
from jax.experimental.pallas import tpu as pltpu
from jax.sharding import PartitionSpec as P

BF16 = jnp.bfloat16
F32 = jnp.float32


def activate(gate_sums, up_sums):
    return (jax.nn.silu(gate_sums) * up_sums).astype(BF16)


def general(tokens, gate_weight, up_weight, down_weight):
    section = lax.all_gather(tokens, "wide", axis=0, tiled=True)
    gate_part = jnp.dot(section, gate_weight, preferred_element_type=F32)
    up_part = jnp.dot(section, up_weight, preferred_element_type=F32)
    gate_sums = lax.psum(gate_part, ("narrow", "sub"))
    up_sums = lax.psum(up_part, ("narrow", "sub"))
    mixed = lax.psum_scatter(
        jnp.dot(activate(gate_sums, up_sums), down_weight, preferred_element_type=F32),
        "wide",
        scatter_dimension=0,
        tiled=True,
    )
    return mixed.astype(BF16)


def swap(x, axis):
    return lax.ppermute(x, axis, [(0, 1), (1, 0)])


BLOCK = 256
SLOTS = 4
VMEM = pl.BlockSpec(memory_space=pltpu.VMEM)
ANY = pl.BlockSpec(memory_space=pl.ANY)
GRANT = pltpu.CompilerParams(vmem_limit_bytes=32 * 2**20)


def sums_kernel(first, width, tokens, gate, up, send, keep, held, sems):
    core = lax.axis_index("sub")
    half = width // 2
    blocks = half // BLOCK

    def copies(step):
        at_keep = step // blocks
        side = jnp.where(at_keep == 1, core, 1 - core)
        column = first + side * half + (step - at_keep * blocks) * BLOCK
        columns = pl.ds(pl.multiple_of(column, 128), BLOCK)
        slot = lax.rem(step, SLOTS)
        return [
            pltpu.make_async_copy(weight.at[:, columns], held.at[slot, i], sems.at[slot, i])
            for i, weight in enumerate((gate, up))
        ]

    def start(step):
        for copy in copies(step):
            copy.start()

    for step in range(min(SLOTS, 2 * blocks)):
        start(jnp.int32(step))

    for side, out in enumerate((send, keep)):

        @pl.loop(0, blocks)
        def _(block):
            step = side * blocks + block
            slot = lax.rem(step, SLOTS)
            for i, copy in enumerate(copies(step)):
                copy.wait()
                column = pl.multiple_of(i * half + block * BLOCK, 128)
                out[:, pl.ds(column, BLOCK)] = jnp.dot(
                    tokens[...], held[slot, i], preferred_element_type=F32
                ).astype(out.dtype)

            @pl.when(step + SLOTS < 2 * blocks)
            def _():
                start(step + SLOTS)


def sums(tokens, gate, up, first, width):
    rows, depth = tokens.shape
    return pl.pallas_call(
        functools.partial(sums_kernel, first, width),
        out_shape=(jax.ShapeDtypeStruct((rows, width), BF16), jax.ShapeDtypeStruct((rows, width), F32)),
        in_specs=[VMEM, ANY, ANY],
        out_specs=(VMEM, VMEM),
        scratch_shapes=[
            pltpu.VMEM((SLOTS, 2, depth, BLOCK), BF16),
            pltpu.SemaphoreType.DMA((SLOTS, 2)),
        ],
        compiler_params=GRANT,
        cost_estimate=pl.CostEstimate(
            flops=4 * rows * depth * width, bytes_accessed=4 * depth * width, transcendentals=0
        ),
        name="gate_and_up",
    )(tokens, gate, up)


def down_kernel(first, width, mine, other, weight, total, out, held, sems):
    core = lax.axis_index("sub")
    half = width // 2
    blocks = half // BLOCK

    def copy(step):
        at_other = step // blocks
        side = jnp.where(at_other == 1, 1 - core, core)
        row = first + side * half + (step - at_other * blocks) * BLOCK
        slot = lax.rem(step, SLOTS)
        return pltpu.make_async_copy(
            weight.at[pl.ds(pl.multiple_of(row, 128), BLOCK), :], held.at[slot], sems.at[slot]
        )

    for step in range(min(SLOTS, 2 * blocks)):
        copy(jnp.int32(step)).start()
    out[...] = total[...]

    for side, hidden in enumerate((mine, other)):

        @pl.loop(0, blocks)
        def _(block):
            step = side * blocks + block
            copy(step).wait()
            units = pl.ds(pl.multiple_of(block * BLOCK, 128), BLOCK)
            out[...] += jnp.dot(
                hidden[:, units], held[lax.rem(step, SLOTS)], preferred_element_type=F32
            )

            @pl.when(step + SLOTS < 2 * blocks)
            def _():
                copy(step + SLOTS).start()


def down(mine, other, weight, total, first, width):
    rows, features = total.shape
    return pl.pallas_call(
        functools.partial(down_kernel, first, width),
        out_shape=jax.ShapeDtypeStruct(total.shape, F32),
        in_specs=[VMEM, VMEM, ANY, VMEM],
        out_specs=VMEM,
        scratch_shapes=[pltpu.VMEM((SLOTS, BLOCK, features), BF16), pltpu.SemaphoreType.DMA((SLOTS,))],
        compiler_params=GRANT,
        cost_estimate=pl.CostEstimate(
            flops=2 * rows * features * width, bytes_accessed=2 * features * width, transcendentals=0
        ),
        name="down",
    )(mine, other, weight, total)


def halves(x, chip):
    gate, up = jnp.split(x, 2, axis=1)
    quarter = gate.shape[1] // 2

    def of(place):
        return jnp.concatenate(
            [lax.dynamic_slice_in_dim(part, place * quarter, quarter, axis=1) for part in (gate, up)], axis=1
        )

    return of(chip), of(1 - chip)


def split(units):
    lumps = units // 512
    more = (lumps + 1) // 2 * 512
    return ((0, more), (more, units - more))


def chunked(tokens, gate_weight, up_weight, down_weight):
    rows, features = tokens.shape
    chip = lax.axis_index("narrow")
    lined = jnp.broadcast_to(tokens.reshape(1, -1, 128), (4, rows * features // 128, 128))
    section = lax.all_to_all(lined, "wide", 0, 0, tiled=True).reshape(4 * rows, features)
    mixed = jnp.zeros((4 * rows, down_weight.shape[1]), F32)
    for first, width in split(gate_weight.shape[1]):
        send, keep = sums(section, gate_weight, up_weight, first, width)
        own, away = halves(keep + swap(send, "sub").astype(F32), chip)
        gate_up = own + swap(away.astype(BF16), "narrow").astype(F32)
        hidden = activate(*jnp.split(gate_up, 2, axis=1))
        theirs = swap(hidden, "narrow")
        mine = jnp.where(
            chip == 0,
            jnp.concatenate([hidden, theirs], axis=1),
            jnp.concatenate([theirs, hidden], axis=1),
        )
        mixed = down(mine, swap(mine, "sub"), down_weight, mixed, first, width)
    mixed = mixed.astype(BF16).reshape(4, -1, 128)
    mixed = lax.all_to_all(mixed, "wide", 0, 0, tiled=True).astype(F32)
    return jnp.sum(mixed, axis=0).astype(BF16).reshape(rows, features)


def solution(mesh):
    placed = (
        P(("groups", "wide"), ("narrow", "sub")),
        P(("narrow", "sub"), "wide"),
        P(("narrow", "sub"), "wide"),
        P("wide", ("narrow", "sub")),
    )
    sizes = tuple(mesh.shape[axis] for axis in ("groups", "wide", "narrow", "sub"))
    return jax.shard_map(
        chunked if sizes == (2, 4, 2, 2) else general,
        mesh=mesh,
        in_specs=placed,
        out_specs=P(("groups", "wide"), ("narrow", "sub")),
        check_vma=False,
    )
```

```python
import functools

import jax
import jax.numpy as jnp
from jax import lax
from jax.experimental import pallas as pl
from jax.experimental.pallas import tpu as pltpu
from jax.sharding import PartitionSpec as P

BF16 = jnp.bfloat16
F32 = jnp.float32


def activate(gate_sums, up_sums):
    return (jax.nn.silu(gate_sums) * up_sums).astype(BF16)


def general(tokens, gate_weight, up_weight, down_weight):
    section = lax.all_gather(tokens, "wide", axis=0, tiled=True)
    gate_part = jnp.dot(section, gate_weight, preferred_element_type=F32)
    up_part = jnp.dot(section, up_weight, preferred_element_type=F32)
    gate_sums = lax.psum(gate_part, ("narrow", "sub"))
    up_sums = lax.psum(up_part, ("narrow", "sub"))
    mixed = lax.psum_scatter(
        jnp.dot(activate(gate_sums, up_sums), down_weight, preferred_element_type=F32),
        "wide",
        scatter_dimension=0,
        tiled=True,
    )
    return mixed.astype(BF16)


def swap(x, axis):
    return lax.ppermute(x, axis, [(0, 1), (1, 0)])


BLOCK = 256
VMEM = pl.BlockSpec(memory_space=pltpu.VMEM)
ANY = pl.BlockSpec(memory_space=pl.ANY)
HBM = pl.BlockSpec(memory_space=pltpu.HBM)
GRANT = pltpu.CompilerParams(vmem_limit_bytes=6 * 2**20)
STREAM = pltpu.CompilerParams(vmem_limit_bytes=14 * 2**20)
SLOTS = 4


def held_in(x):
    return pltpu.with_memory_space_constraint(x, pltpu.VMEM)


def left_in_hbm(x):
    return pltpu.with_memory_space_constraint(x, pltpu.HBM)


def unit_blocks(first, width, core_first):
    half = width // 2
    core = lax.axis_index("sub")
    for side in (core, 1 - core) if core_first else (1 - core, core):
        for block in range(half // BLOCK):
            yield pl.multiple_of(first + side * half + block * BLOCK, BLOCK)


def sums_fetch(first, width, gate, up, held, sems):
    for step, unit in enumerate(unit_blocks(first, width, False)):
        for i, weight in enumerate((gate, up)):
            yield pltpu.make_async_copy(weight.at[:, pl.ds(unit, BLOCK)], held.at[step, i], sems.at[step, i])


def sums_held(depth, width):
    return (width // BLOCK, 2, depth, BLOCK)


def sums_body(tokens, held, send, keep):
    blocks = held.shape[0] // 2
    for side, out in enumerate((send, keep)):

        @pl.loop(0, blocks)
        def _(block):
            for i in range(2):
                column = pl.multiple_of((i * blocks + block) * BLOCK, BLOCK)
                out[:, pl.ds(column, BLOCK)] = jnp.dot(
                    tokens[...], held[side * blocks + block, i], preferred_element_type=F32
                ).astype(out.dtype)


def load_kernel(first, width, gate, up, held, sems):
    copies = list(sums_fetch(first, width, gate, up, held, sems))
    for copy in copies:
        copy.start()
    for copy in copies:
        copy.wait()


def load(gate, up, first, width):
    shape = sums_held(gate.shape[0], width)
    return pl.pallas_call(
        functools.partial(load_kernel, first, width),
        out_shape=pltpu.VMEM(shape, BF16),
        in_specs=[HBM, HBM],
        out_specs=VMEM,
        scratch_shapes=[pltpu.SemaphoreType.DMA(shape[:2])],
        compiler_params=GRANT,
        cost_estimate=pl.CostEstimate(
            flops=0, bytes_accessed=4 * gate.shape[0] * width, transcendentals=0
        ),
        name="load",
    )(left_in_hbm(gate), left_in_hbm(up))


def first_sums_kernel(tokens, held, send, keep):
    sums_body(tokens, held, send, keep)


def first_sums(tokens, held):
    rows, depth = tokens.shape
    units = held.shape[0] * BLOCK
    return pl.pallas_call(
        first_sums_kernel,
        out_shape=(jax.ShapeDtypeStruct((rows, units), BF16), jax.ShapeDtypeStruct((rows, units), F32)),
        in_specs=[VMEM, VMEM],
        out_specs=(VMEM, VMEM),
        compiler_params=GRANT,
        cost_estimate=pl.CostEstimate(
            flops=4 * rows * depth * units, bytes_accessed=4 * depth * units, transcendentals=0
        ),
        name="first_sums",
    )(tokens, held_in(held))


def sums_kernel(first, width, tokens, gate, up, after, send, keep, held, sems):
    core = lax.axis_index("sub")
    half = width // 2
    blocks = half // BLOCK

    def copies(step):
        at_keep = step // blocks
        side = jnp.where(at_keep == 1, core, 1 - core)
        column = first + side * half + (step - at_keep * blocks) * BLOCK
        columns = pl.ds(pl.multiple_of(column, 128), BLOCK)
        slot = lax.rem(step, SLOTS)
        return [
            pltpu.make_async_copy(weight.at[:, columns], held.at[slot, i], sems.at[slot, i])
            for i, weight in enumerate((gate, up))
        ]

    def start(step):
        for copy in copies(step):
            copy.start()

    for step in range(min(SLOTS, 2 * blocks)):
        start(jnp.int32(step))

    for side, out in enumerate((send, keep)):

        @pl.loop(0, blocks)
        def _(block):
            step = side * blocks + block
            slot = lax.rem(step, SLOTS)
            for i, copy in enumerate(copies(step)):
                copy.wait()
                column = pl.multiple_of(i * half + block * BLOCK, 128)
                out[:, pl.ds(column, BLOCK)] = jnp.dot(
                    tokens[...], held[slot, i], preferred_element_type=F32
                ).astype(out.dtype)

            @pl.when(step + SLOTS < 2 * blocks)
            def _():
                start(step + SLOTS)


def sums(tokens, gate, up, after, first, width):
    rows, depth = tokens.shape
    return pl.pallas_call(
        functools.partial(sums_kernel, first, width),
        out_shape=(jax.ShapeDtypeStruct((rows, width), BF16), jax.ShapeDtypeStruct((rows, width), F32)),
        in_specs=[VMEM, HBM, HBM, ANY],
        out_specs=(VMEM, VMEM),
        scratch_shapes=[
            pltpu.VMEM((SLOTS, 2, depth, BLOCK), BF16),
            pltpu.SemaphoreType.DMA((SLOTS, 2)),
        ],
        compiler_params=STREAM,
        cost_estimate=pl.CostEstimate(
            flops=4 * rows * depth * width, bytes_accessed=4 * depth * width, transcendentals=0
        ),
        name="gate_and_up",
    )(tokens, left_in_hbm(gate), left_in_hbm(up), after)


def down_kernel(first, width, mine, other, weight, total, out, held, sems):
    core = lax.axis_index("sub")
    half = width // 2
    blocks = half // BLOCK

    def copy(step):
        at_other = step // blocks
        side = jnp.where(at_other == 1, 1 - core, core)
        row = first + side * half + (step - at_other * blocks) * BLOCK
        slot = lax.rem(step, SLOTS)
        return pltpu.make_async_copy(
            weight.at[pl.ds(pl.multiple_of(row, 128), BLOCK), :], held.at[slot], sems.at[slot]
        )

    for step in range(min(SLOTS, 2 * blocks)):
        copy(jnp.int32(step)).start()
    out[...] = total[...]

    for side, hidden in enumerate((mine, other)):

        @pl.loop(0, blocks)
        def _(block):
            step = side * blocks + block
            copy(step).wait()
            units = pl.ds(pl.multiple_of(block * BLOCK, 128), BLOCK)
            out[...] += jnp.dot(
                hidden[:, units], held[lax.rem(step, SLOTS)], preferred_element_type=F32
            )

            @pl.when(step + SLOTS < 2 * blocks)
            def _():
                copy(step + SLOTS).start()


def down(mine, other, weight, total, first, width):
    rows, features = total.shape
    return pl.pallas_call(
        functools.partial(down_kernel, first, width),
        out_shape=jax.ShapeDtypeStruct(total.shape, F32),
        in_specs=[VMEM, VMEM, HBM, VMEM],
        out_specs=VMEM,
        scratch_shapes=[pltpu.VMEM((SLOTS, BLOCK, features), BF16), pltpu.SemaphoreType.DMA((SLOTS,))],
        compiler_params=STREAM,
        cost_estimate=pl.CostEstimate(
            flops=2 * rows * features * width, bytes_accessed=2 * features * width, transcendentals=0
        ),
        name="down",
    )(mine, other, left_in_hbm(weight), total)


def halves(x, chip):
    gate, up = jnp.split(x, 2, axis=1)
    quarter = gate.shape[1] // 2

    def of(place):
        return jnp.concatenate(
            [lax.dynamic_slice_in_dim(part, place * quarter, quarter, axis=1) for part in (gate, up)], axis=1
        )

    return of(chip), of(1 - chip)


def split(units):
    more = (units // 512 + 1) // 2 * 512
    return ((0, units - more), (units - more, more))


def across(x, apart):
    return lax.ppermute(x, "wide", [(i, i ^ apart) for i in range(4)])


def chunked(tokens, gate_weight, up_weight, down_weight):
    rows = tokens.shape[0]
    chip = lax.axis_index("narrow")
    chunks = split(gate_weight.shape[1])
    section = jnp.concatenate([tokens] + [across(tokens, apart) for apart in (1, 2, 3)], axis=0)
    held = load(gate_weight, up_weight, *chunks[0])

    def quarters(send, keep):
        own, away = halves(keep + swap(send, "sub").astype(F32), chip)
        return own, away.astype(BF16)

    def hidden_half(own, away):
        gate_up = own + swap(away, "narrow").astype(F32)
        hidden = activate(*jnp.split(gate_up, 2, axis=1))
        theirs = swap(hidden, "narrow")
        return jnp.where(
            chip == 0,
            jnp.concatenate([hidden, theirs], axis=1),
            jnp.concatenate([theirs, hidden], axis=1),
        )

    send, keep = first_sums(section, held)
    own, away = quarters(send, keep)
    send, keep = sums(section, gate_weight, up_weight, away, *chunks[1])
    mixed = jnp.zeros((4 * rows, down_weight.shape[1]), F32)
    for index, chunk in enumerate(chunks):
        if index > 0:
            own, away = quarters(send, keep)
        mine = hidden_half(own, away)
        mixed = down(mine, swap(mine, "sub"), down_weight, mixed, *chunk)
    blocks = mixed.reshape(4, rows, -1)
    out = blocks[0]
    for apart in (1, 2, 3):
        out = out + across(blocks[apart].astype(BF16), apart).astype(F32)
    return out.astype(BF16)


def solution(mesh):
    placed = (
        P(("groups", "wide"), ("narrow", "sub")),
        P(("narrow", "sub"), "wide"),
        P(("narrow", "sub"), "wide"),
        P("wide", ("narrow", "sub")),
    )
    sizes = tuple(mesh.shape[axis] for axis in ("groups", "wide", "narrow", "sub"))
    return jax.shard_map(
        chunked if sizes == (2, 4, 2, 2) else general,
        mesh=mesh,
        in_specs=placed,
        out_specs=P(("groups", "wide"), ("narrow", "sub")),
        check_vma=False,
    )
```

```python
import functools

import jax
import jax.numpy as jnp
from jax import lax
from jax.experimental import pallas as pl
from jax.experimental.pallas import tpu as pltpu
from jax.sharding import PartitionSpec as P

BF16 = jnp.bfloat16
F32 = jnp.float32


def activate(gate_sums, up_sums):
    return (jax.nn.silu(gate_sums) * up_sums).astype(BF16)


def general(tokens, gate_weight, up_weight, down_weight):
    section = lax.all_gather(tokens, "wide", axis=0, tiled=True)
    gate_part = jnp.dot(section, gate_weight, preferred_element_type=F32)
    up_part = jnp.dot(section, up_weight, preferred_element_type=F32)
    gate_sums = lax.psum(gate_part, ("narrow", "sub"))
    up_sums = lax.psum(up_part, ("narrow", "sub"))
    mixed = lax.psum_scatter(
        jnp.dot(activate(gate_sums, up_sums), down_weight, preferred_element_type=F32),
        "wide",
        scatter_dimension=0,
        tiled=True,
    )
    return mixed.astype(BF16)


def swap(x, axis):
    return lax.ppermute(x, axis, [(0, 1), (1, 0)])


BLOCK = 256
VMEM = pl.BlockSpec(memory_space=pltpu.VMEM)
ANY = pl.BlockSpec(memory_space=pl.ANY)
HBM = pl.BlockSpec(memory_space=pltpu.HBM)
GRANT = pltpu.CompilerParams(vmem_limit_bytes=6 * 2**20)


def held_in(x):
    return pltpu.with_memory_space_constraint(x, pltpu.VMEM)


def left_in_hbm(x):
    return pltpu.with_memory_space_constraint(x, pltpu.HBM)


def unit_blocks(first, width, core_first):
    half = width // 2
    core = lax.axis_index("sub")
    for side in (core, 1 - core) if core_first else (1 - core, core):
        for block in range(half // BLOCK):
            yield pl.multiple_of(first + side * half + block * BLOCK, BLOCK)


def sums_fetch(first, width, gate, up, held, sems):
    for step, unit in enumerate(unit_blocks(first, width, False)):
        for i, weight in enumerate((gate, up)):
            yield pltpu.make_async_copy(weight.at[:, pl.ds(unit, BLOCK)], held.at[step, i], sems.at[step, i])


def sums_held(depth, width):
    return (width // BLOCK, 2, depth, BLOCK)


def sums_body(tokens, held, send, keep, copies=()):
    blocks = held.shape[0] // 2

    def block_sums(out, side, block):
        for i in range(2):
            column = i * blocks + block
            if not isinstance(block, int):
                column = pl.multiple_of(column * BLOCK, BLOCK)
            else:
                column = column * BLOCK
            out[:, pl.ds(column, BLOCK)] = jnp.dot(
                tokens[...], held[side * blocks + block, i], preferred_element_type=F32
            ).astype(out.dtype)

    for side, out in enumerate((send, keep)):
        if copies:
            for block in range(blocks):
                step = side * blocks + block
                for copy in copies[2 * step : 2 * step + 2]:
                    copy.wait()
                block_sums(out, side, block)
        else:
            pl.loop(0, blocks)(functools.partial(block_sums, out, side))


def load_kernel(first, width, gate, up, held, sems):
    copies = list(sums_fetch(first, width, gate, up, held, sems))
    for copy in copies:
        copy.start()
    for copy in copies:
        copy.wait()


def load(gate, up, first, width):
    shape = sums_held(gate.shape[0], width)
    return pl.pallas_call(
        functools.partial(load_kernel, first, width),
        out_shape=pltpu.VMEM(shape, BF16),
        in_specs=[HBM, HBM],
        out_specs=VMEM,
        scratch_shapes=[pltpu.SemaphoreType.DMA(shape[:2])],
        compiler_params=GRANT,
        cost_estimate=pl.CostEstimate(
            flops=0, bytes_accessed=4 * gate.shape[0] * width, transcendentals=0
        ),
        name="load",
    )(left_in_hbm(gate), left_in_hbm(up))


def first_sums_kernel(tokens, held, send, keep):
    sums_body(tokens, held, send, keep)


def first_sums(tokens, held):
    rows, depth = tokens.shape
    units = held.shape[0] * BLOCK
    return pl.pallas_call(
        first_sums_kernel,
        out_shape=(jax.ShapeDtypeStruct((rows, units), BF16), jax.ShapeDtypeStruct((rows, units), F32)),
        in_specs=[VMEM, VMEM],
        out_specs=(VMEM, VMEM),
        compiler_params=GRANT,
        cost_estimate=pl.CostEstimate(
            flops=4 * rows * depth * units, bytes_accessed=4 * depth * units, transcendentals=0
        ),
        name="first_sums",
    )(tokens, held_in(held))


def sums_kernel(first, width, tokens, gate, up, after, send, keep, held, sems):
    copies = list(sums_fetch(first, width, gate, up, held, sems))
    for copy in copies:
        copy.start()
    sums_body(tokens, held, send, keep, copies)


def sums(tokens, gate, up, after, first, width):
    rows, depth = tokens.shape
    shape = sums_held(depth, width)
    return pl.pallas_call(
        functools.partial(sums_kernel, first, width),
        out_shape=(jax.ShapeDtypeStruct((rows, width), BF16), jax.ShapeDtypeStruct((rows, width), F32)),
        in_specs=[VMEM, HBM, HBM, ANY],
        out_specs=(VMEM, VMEM),
        scratch_shapes=[pltpu.VMEM(shape, BF16), pltpu.SemaphoreType.DMA(shape[:2])],
        compiler_params=pltpu.CompilerParams(vmem_limit_bytes=4 * depth * width + 4 * 2**20),
        cost_estimate=pl.CostEstimate(
            flops=4 * rows * depth * width, bytes_accessed=4 * depth * width, transcendentals=0
        ),
        name="sums",
    )(tokens, left_in_hbm(gate), left_in_hbm(up), after)


def down_kernel(first, width, mine, other, weight, total, out):
    core = lax.axis_index("sub")
    half = width // 2
    out[...] = total[...]
    for side, hidden in ((core, mine), (1 - core, other)):

        @pl.loop(0, half // BLOCK)
        def _(block):
            units = pl.ds(pl.multiple_of(block * BLOCK, BLOCK), BLOCK)
            rows = pl.ds(pl.multiple_of(first + side * half + block * BLOCK, BLOCK), BLOCK)
            out[...] += jnp.dot(hidden[:, units], weight[rows, :], preferred_element_type=F32)


def down(mine, other, weight, total, first, width):
    rows, features = total.shape
    return pl.pallas_call(
        functools.partial(down_kernel, first, width),
        out_shape=jax.ShapeDtypeStruct(total.shape, F32),
        in_specs=[VMEM] * 4,
        out_specs=VMEM,
        compiler_params=GRANT,
        cost_estimate=pl.CostEstimate(
            flops=2 * rows * features * width, bytes_accessed=2 * features * width, transcendentals=0
        ),
        name="down",
    )(mine, other, held_in(weight), total)


def split(units):
    lumps = units // 512
    ends = [lumps * part // 13 * 512 for part in (0, 6, 10, 13)]
    return [(start, end - start) for start, end in zip(ends, ends[1:])]


def across(x, apart):
    return lax.ppermute(x, "wide", [(i, i ^ apart) for i in range(4)])


def chunked(tokens, gate_weight, up_weight, down_weight):
    rows = tokens.shape[0]
    chunks = split(gate_weight.shape[1])
    section = jnp.concatenate([tokens] + [across(tokens, apart) for apart in (1, 2, 3)], axis=0)
    held = load(gate_weight, up_weight, *chunks[0])

    def core_sums(send, keep):
        total = keep + swap(send, "sub").astype(F32)
        return total, total.astype(BF16)

    def hidden_half(total, sent):
        return activate(*jnp.split(total + swap(sent, "narrow").astype(F32), 2, axis=1))

    parts = [core_sums(*first_sums(section, held))]
    for chunk in chunks[1:]:
        parts.append(core_sums(*sums(section, gate_weight, up_weight, parts[-1][1], *chunk)))
    mixed = jnp.zeros((4 * rows, down_weight.shape[1]), F32)
    for chunk, part in zip(chunks, parts):
        mine = hidden_half(*part)
        mixed = down(mine, swap(mine, "sub"), down_weight, mixed, *chunk)
    blocks = mixed.reshape(4, rows, -1)
    out = blocks[0]
    for apart in (1, 2, 3):
        out = out + across(blocks[apart].astype(BF16), apart).astype(F32)
    return out.astype(BF16)


def solution(mesh):
    placed = (
        P(("groups", "wide"), ("narrow", "sub")),
        P(("narrow", "sub"), "wide"),
        P(("narrow", "sub"), "wide"),
        P("wide", ("narrow", "sub")),
    )
    sizes = tuple(mesh.shape[axis] for axis in ("groups", "wide", "narrow", "sub"))
    return jax.shard_map(
        chunked if sizes == (2, 4, 2, 2) else general,
        mesh=mesh,
        in_specs=placed,
        out_specs=P(("groups", "wide"), ("narrow", "sub")),
        check_vma=False,
    )
```

```python
import functools

import jax
import jax.numpy as jnp
from jax import lax
from jax.experimental import pallas as pl
from jax.experimental.pallas import tpu as pltpu
from jax.sharding import PartitionSpec as P

BF16 = jnp.bfloat16
F32 = jnp.float32


def activate(gate_sums, up_sums):
    return (jax.nn.silu(gate_sums) * up_sums).astype(BF16)


def general(tokens, gate_weight, up_weight, down_weight):
    section = lax.all_gather(tokens, "wide", axis=0, tiled=True)
    gate_part = jnp.dot(section, gate_weight, preferred_element_type=F32)
    up_part = jnp.dot(section, up_weight, preferred_element_type=F32)
    gate_sums = lax.psum(gate_part, ("narrow", "sub"))
    up_sums = lax.psum(up_part, ("narrow", "sub"))
    mixed = lax.psum_scatter(
        jnp.dot(activate(gate_sums, up_sums), down_weight, preferred_element_type=F32),
        "wide",
        scatter_dimension=0,
        tiled=True,
    )
    return mixed.astype(BF16)


def swap(x, axis):
    return lax.ppermute(x, axis, [(0, 1), (1, 0)])


BLOCK = 256
VMEM = pl.BlockSpec(memory_space=pltpu.VMEM)
ANY = pl.BlockSpec(memory_space=pl.ANY)
HBM = pl.BlockSpec(memory_space=pltpu.HBM)
GRANT = pltpu.CompilerParams(vmem_limit_bytes=6 * 2**20)


def held_in(x):
    return pltpu.with_memory_space_constraint(x, pltpu.VMEM)


def left_in_hbm(x):
    return pltpu.with_memory_space_constraint(x, pltpu.HBM)


def unit_blocks(first, width, core_first):
    half = width // 2
    core = lax.axis_index("sub")
    for side in (core, 1 - core) if core_first else (1 - core, core):
        for block in range(half // BLOCK):
            yield pl.multiple_of(first + side * half + block * BLOCK, BLOCK)


def sums_fetch(first, width, gate, up, held, sems):
    for step, unit in enumerate(unit_blocks(first, width, False)):
        for i, weight in enumerate((gate, up)):
            yield pltpu.make_async_copy(weight.at[:, pl.ds(unit, BLOCK)], held.at[step, i], sems.at[step, i])


def sums_held(depth, width):
    return (width // BLOCK, 2, depth, BLOCK)


def sums_body(tokens, held, send, keep, copies=()):
    blocks = held.shape[0] // 2

    def block_sums(out, side, block):
        for i in range(2):
            column = i * blocks + block
            if not isinstance(block, int):
                column = pl.multiple_of(column * BLOCK, BLOCK)
            else:
                column = column * BLOCK
            out[:, pl.ds(column, BLOCK)] = jnp.dot(
                tokens[...], held[side * blocks + block, i], preferred_element_type=F32
            ).astype(out.dtype)

    for side, out in enumerate((send, keep)):
        if copies:
            for block in range(blocks):
                step = side * blocks + block
                for copy in copies[2 * step : 2 * step + 2]:
                    copy.wait()
                block_sums(out, side, block)
        else:
            pl.loop(0, blocks)(functools.partial(block_sums, out, side))


def load_kernel(first, width, gate, up, held, sems):
    copies = list(sums_fetch(first, width, gate, up, held, sems))
    for copy in copies:
        copy.start()
    for copy in copies:
        copy.wait()


def load(gate, up, first, width):
    shape = sums_held(gate.shape[0], width)
    return pl.pallas_call(
        functools.partial(load_kernel, first, width),
        out_shape=pltpu.VMEM(shape, BF16),
        in_specs=[HBM, HBM],
        out_specs=VMEM,
        scratch_shapes=[pltpu.SemaphoreType.DMA(shape[:2])],
        compiler_params=GRANT,
        cost_estimate=pl.CostEstimate(
            flops=0, bytes_accessed=4 * gate.shape[0] * width, transcendentals=0
        ),
        name="load",
    )(left_in_hbm(gate), left_in_hbm(up))


def first_sums_kernel(tokens, held, send, keep):
    sums_body(tokens, held, send, keep)


def first_sums(tokens, held):
    rows, depth = tokens.shape
    units = held.shape[0] * BLOCK
    return pl.pallas_call(
        first_sums_kernel,
        out_shape=(jax.ShapeDtypeStruct((rows, units), BF16), jax.ShapeDtypeStruct((rows, units), F32)),
        in_specs=[VMEM, VMEM],
        out_specs=(VMEM, VMEM),
        compiler_params=GRANT,
        cost_estimate=pl.CostEstimate(
            flops=4 * rows * depth * units, bytes_accessed=4 * depth * units, transcendentals=0
        ),
        name="first_sums",
    )(tokens, held_in(held))


def sums_kernel(first, width, tokens, gate, up, after, send, keep, held, sems):
    copies = list(sums_fetch(first, width, gate, up, held, sems))
    for copy in copies:
        copy.start()
    sums_body(tokens, held, send, keep, copies)


def sums(tokens, gate, up, after, first, width):
    rows, depth = tokens.shape
    shape = sums_held(depth, width)
    return pl.pallas_call(
        functools.partial(sums_kernel, first, width),
        out_shape=(jax.ShapeDtypeStruct((rows, width), BF16), jax.ShapeDtypeStruct((rows, width), F32)),
        in_specs=[VMEM, HBM, HBM, ANY],
        out_specs=(VMEM, VMEM),
        scratch_shapes=[pltpu.VMEM(shape, BF16), pltpu.SemaphoreType.DMA(shape[:2])],
        compiler_params=pltpu.CompilerParams(vmem_limit_bytes=4 * depth * width + 4 * 2**20),
        cost_estimate=pl.CostEstimate(
            flops=4 * rows * depth * width, bytes_accessed=4 * depth * width, transcendentals=0
        ),
        name="sums",
    )(tokens, left_in_hbm(gate), left_in_hbm(up), after)


def down_kernel(first, width, mine, other, weight, total, out):
    core = lax.axis_index("sub")
    half = width // 2
    starts = [pl.multiple_of(first + side * half, BLOCK) for side in (core, 1 - core)]

    @pl.loop(0, out.shape[1] // BLOCK)
    def _(block):
        columns = pl.ds(pl.multiple_of(block * BLOCK, BLOCK), BLOCK)
        part = total[:, columns]
        for start, hidden in zip(starts, (mine, other)):
            part += jnp.dot(hidden[...], weight[pl.ds(start, half), columns], preferred_element_type=F32)
        out[:, columns] = part


def down(mine, other, weight, total, first, width):
    rows, features = total.shape
    return pl.pallas_call(
        functools.partial(down_kernel, first, width),
        out_shape=jax.ShapeDtypeStruct(total.shape, F32),
        in_specs=[VMEM] * 4,
        out_specs=VMEM,
        compiler_params=GRANT,
        cost_estimate=pl.CostEstimate(
            flops=2 * rows * features * width, bytes_accessed=2 * features * width, transcendentals=0
        ),
        name="down",
    )(mine, other, held_in(weight), total)


def split(units):
    lumps = units // 512
    ends = [lumps * part // 13 * 512 for part in (0, 6, 10, 13)]
    return [(start, end - start) for start, end in zip(ends, ends[1:])]


def across(x, apart):
    return lax.ppermute(x, "wide", [(i, i ^ apart) for i in range(4)])


def chunked(tokens, gate_weight, up_weight, down_weight):
    rows = tokens.shape[0]
    chunks = split(gate_weight.shape[1])
    section = jnp.concatenate([tokens] + [across(tokens, apart) for apart in (1, 2, 3)], axis=0)
    held = load(gate_weight, up_weight, *chunks[0])

    def core_sums(send, keep):
        total = keep + swap(send, "sub").astype(F32)
        return total, total.astype(BF16)

    def hidden_half(total, received):
        return activate(*jnp.split(total + received.astype(F32), 2, axis=1))

    def add(mixed, mine, chunk):
        return down(mine, swap(mine, "sub"), down_weight, mixed, *chunk)

    mixed = jnp.zeros((4 * rows, down_weight.shape[1]), F32)
    total, sent = core_sums(*first_sums(section, held))
    send, keep = sums(section, gate_weight, up_weight, sent, *chunks[1])
    received, send = lax.optimization_barrier((swap(sent, "narrow"), send))
    mine = hidden_half(total, received)
    total, sent = core_sums(send, keep)
    send, keep = sums(section, gate_weight, up_weight, sent, *chunks[2])
    mixed = add(mixed, mine, chunks[0])
    received, send = lax.optimization_barrier((swap(sent, "narrow"), send))
    mine = hidden_half(total, received)
    total, sent = core_sums(send, keep)
    mixed = add(mixed, mine, chunks[1])
    received, mixed = lax.optimization_barrier((swap(sent, "narrow"), mixed))
    mixed = add(mixed, hidden_half(total, received), chunks[2])
    blocks = mixed.reshape(4, rows, 2, -1).swapaxes(1, 2).reshape(4, 2 * rows, -1)
    out = blocks[0]
    for received in [across(blocks[apart].astype(BF16), apart) for apart in (3, 2, 1)]:
        out = out + received.astype(F32)
    return out.astype(BF16).reshape(2, rows, -1).swapaxes(0, 1).reshape(rows, -1)


def solution(mesh):
    placed = (
        P(("groups", "wide"), ("narrow", "sub")),
        P(("narrow", "sub"), "wide"),
        P(("narrow", "sub"), "wide"),
        P("wide", ("narrow", "sub")),
    )
    sizes = tuple(mesh.shape[axis] for axis in ("groups", "wide", "narrow", "sub"))
    return jax.shard_map(
        chunked if sizes == (2, 4, 2, 2) else general,
        mesh=mesh,
        in_specs=placed,
        out_specs=P(("groups", "wide"), ("narrow", "sub")),
        check_vma=False,
    )
```

```python
import functools

import jax
import jax.numpy as jnp
from jax import lax
from jax.experimental import pallas as pl
from jax.experimental.pallas import tpu as pltpu
from jax.sharding import PartitionSpec as P

BF16 = jnp.bfloat16
F32 = jnp.float32


def activate(gate_sums, up_sums):
    return (jax.nn.silu(gate_sums) * up_sums).astype(BF16)


def general(tokens, gate_weight, up_weight, down_weight):
    section = lax.all_gather(tokens, "wide", axis=0, tiled=True)
    gate_part = jnp.dot(section, gate_weight, preferred_element_type=F32)
    up_part = jnp.dot(section, up_weight, preferred_element_type=F32)
    gate_sums = lax.psum(gate_part, ("narrow", "sub"))
    up_sums = lax.psum(up_part, ("narrow", "sub"))
    mixed = lax.psum_scatter(
        jnp.dot(activate(gate_sums, up_sums), down_weight, preferred_element_type=F32),
        "wide",
        scatter_dimension=0,
        tiled=True,
    )
    return mixed.astype(BF16)


def swap(x, axis):
    return lax.ppermute(x, axis, [(0, 1), (1, 0)])


BLOCK = 256
VMEM = pl.BlockSpec(memory_space=pltpu.VMEM)
ANY = pl.BlockSpec(memory_space=pl.ANY)
HBM = pl.BlockSpec(memory_space=pltpu.HBM)
GRANT = pltpu.CompilerParams(vmem_limit_bytes=6 * 2**20)


def held_in(x):
    return pltpu.with_memory_space_constraint(x, pltpu.VMEM)


def left_in_hbm(x):
    return pltpu.with_memory_space_constraint(x, pltpu.HBM)


def block_copies(first, half, step, gate, up, dst, sem):
    core = lax.axis_index("sub")
    mine = jnp.int32(step >= half // BLOCK)
    side = jnp.where(mine == 1, core, 1 - core)
    unit = first + side * half + (step - mine * (half // BLOCK)) * BLOCK
    columns = pl.ds(pl.multiple_of(unit, BLOCK), BLOCK)
    return [
        pltpu.make_async_copy(weight.at[:, columns], dst.at[i], sem.at[i]) for i, weight in enumerate((gate, up))
    ]


def load_kernel(first, half, gate, up, held, sems):
    copies = [
        copy
        for step in range(held.shape[0])
        for copy in block_copies(first, half, step, gate, up, held.at[step], sems.at[step])
    ]
    for copy in copies:
        copy.start()
    for copy in copies:
        copy.wait()


def load(gate, up, chunk, steps):
    depth = gate.shape[0]
    return pl.pallas_call(
        functools.partial(load_kernel, chunk[0], chunk[1] // 2),
        out_shape=pltpu.VMEM((steps, 2, depth, BLOCK), BF16),
        in_specs=[HBM, HBM],
        out_specs=VMEM,
        scratch_shapes=[pltpu.SemaphoreType.DMA((steps, 2))],
        compiler_params=GRANT,
        cost_estimate=pl.CostEstimate(
            flops=0, bytes_accessed=4 * steps * depth * BLOCK, transcendentals=0
        ),
        name="load",
    )(left_in_hbm(gate), left_in_hbm(up))


def sums_kernel(first, steps, tokens, gate, up, *refs):
    send, keep, streamed, sems = refs[-4:]
    held = refs[0] if steps else None
    half = send.shape[1] // 2
    blocks = half // BLOCK

    def copies(step):
        at = step - steps
        return block_copies(first, half, step, gate, up, streamed.at[at], sems.at[at])

    for step in range(steps, 2 * blocks):
        for copy in copies(step):
            copy.start()

    def add(out, start, source, block):
        for i in range(2):
            column = pl.multiple_of((i * blocks + block - start) * BLOCK, BLOCK)
            out[:, pl.ds(column, BLOCK)] = jnp.dot(tokens[...], source[i], preferred_element_type=F32).astype(
                out.dtype
            )

    for side, out in enumerate((send, keep)):
        start, end = side * blocks, (side + 1) * blocks

        middle = min(max(steps, start), end)
        if start < middle:

            @pl.loop(start, middle)
            def _(step):
                add(out, start, held.at[step], step)

        if middle < end:

            @pl.loop(middle, end)
            def _(step):
                for copy in copies(step):
                    copy.wait()
                add(out, start, streamed.at[step - steps], step)


def sums(tokens, gate, up, chunk, held=None):
    rows, depth = tokens.shape
    first, width = chunk
    steps = 0 if held is None else held.shape[0]
    shape = (width // BLOCK - steps, 2, depth, BLOCK)
    return pl.pallas_call(
        functools.partial(sums_kernel, first, steps),
        out_shape=(jax.ShapeDtypeStruct((rows, width), BF16), jax.ShapeDtypeStruct((rows, width), F32)),
        in_specs=[VMEM, HBM, HBM] + [VMEM] * (steps > 0),
        out_specs=(VMEM, VMEM),
        scratch_shapes=[pltpu.VMEM(shape, BF16), pltpu.SemaphoreType.DMA(shape[:2])],
        compiler_params=pltpu.CompilerParams(vmem_limit_bytes=4 * shape[0] * depth * BLOCK + 4 * 2**20),
        cost_estimate=pl.CostEstimate(
            flops=4 * rows * depth * width, bytes_accessed=4 * depth * width, transcendentals=0
        ),
        name="sums",
    )(tokens, left_in_hbm(gate), left_in_hbm(up), *([held_in(held)] if steps else []))


def down_kernel(first, width, mine, other, weight, total, out):
    core = lax.axis_index("sub")
    half = width // 2
    starts = [pl.multiple_of(first + side * half, BLOCK) for side in (core, 1 - core)]

    @pl.loop(0, out.shape[1] // BLOCK)
    def _(block):
        columns = pl.ds(pl.multiple_of(block * BLOCK, BLOCK), BLOCK)
        part = total[:, columns]
        for start, hidden in zip(starts, (mine, other)):
            part += jnp.dot(hidden[...], weight[pl.ds(start, half), columns], preferred_element_type=F32)
        out[:, columns] = part


def down(mine, other, weight, total, first, width):
    rows, features = total.shape
    return pl.pallas_call(
        functools.partial(down_kernel, first, width),
        out_shape=jax.ShapeDtypeStruct(total.shape, F32),
        in_specs=[VMEM] * 4,
        out_specs=VMEM,
        compiler_params=GRANT,
        cost_estimate=pl.CostEstimate(
            flops=2 * rows * features * width, bytes_accessed=2 * features * width, transcendentals=0
        ),
        name="down",
    )(mine, other, held_in(weight), total)


def split(units):
    more = units // 512 * 9 // 13 * 512
    return (0, more), (more, units - more)


def across(x, apart):
    return lax.ppermute(x, "wide", [(i, i ^ apart) for i in range(4)])


def chunked(tokens, gate_weight, up_weight, down_weight):
    rows = tokens.shape[0]
    chunks = split(gate_weight.shape[1])
    section = jnp.concatenate([tokens] + [across(tokens, apart) for apart in (1, 2, 3)], axis=0)
    held = load(gate_weight, up_weight, chunks[0], 8)

    def core_sums(send, keep):
        total = keep + swap(send, "sub").astype(F32)
        return total, total.astype(BF16)

    def hidden_half(total, received):
        return activate(*jnp.split(total + received.astype(F32), 2, axis=1))

    def add(mixed, mine, chunk):
        return down(mine, swap(mine, "sub"), down_weight, mixed, *chunk)

    mixed = jnp.zeros((4 * rows, down_weight.shape[1]), F32)
    send, keep = sums(section, gate_weight, up_weight, chunks[0], held)
    total, sent = core_sums(send, keep)
    later, _ = lax.optimization_barrier((section, sent))
    send, keep = sums(later, gate_weight, up_weight, chunks[1])
    received, send = lax.optimization_barrier((swap(sent, "narrow"), send))
    mine = hidden_half(total, received)
    total, sent = core_sums(send, keep)
    mixed = add(mixed, mine, chunks[0])
    received, mixed = lax.optimization_barrier((swap(sent, "narrow"), mixed))
    mixed = add(mixed, hidden_half(total, received), chunks[1])
    blocks = mixed.reshape(4, rows, 2, -1).swapaxes(1, 2).reshape(4, 2 * rows, -1)
    out = blocks[0]
    for received in [across(blocks[apart].astype(BF16), apart) for apart in (3, 2, 1)]:
        out = out + received.astype(F32)
    return out.astype(BF16).reshape(2, rows, -1).swapaxes(0, 1).reshape(rows, -1)


def solution(mesh):
    placed = (
        P(("groups", "wide"), ("narrow", "sub")),
        P(("narrow", "sub"), "wide"),
        P(("narrow", "sub"), "wide"),
        P("wide", ("narrow", "sub")),
    )
    sizes = tuple(mesh.shape[axis] for axis in ("groups", "wide", "narrow", "sub"))
    return jax.shard_map(
        chunked if sizes == (2, 4, 2, 2) else general,
        mesh=mesh,
        in_specs=placed,
        out_specs=P(("groups", "wide"), ("narrow", "sub")),
        check_vma=False,
    )
```

```python
import functools

import jax
import jax.numpy as jnp
from jax import lax
from jax.experimental import pallas as pl
from jax.experimental.pallas import tpu as pltpu
from jax.sharding import PartitionSpec as P

BF16 = jnp.bfloat16
F32 = jnp.float32


def activate(gate_sums, up_sums):
    return (jax.nn.silu(gate_sums) * up_sums).astype(BF16)


def general(tokens, gate_weight, up_weight, down_weight):
    section = lax.all_gather(tokens, "wide", axis=0, tiled=True)
    gate_part = jnp.dot(section, gate_weight, preferred_element_type=F32)
    up_part = jnp.dot(section, up_weight, preferred_element_type=F32)
    gate_sums = lax.psum(gate_part, ("narrow", "sub"))
    up_sums = lax.psum(up_part, ("narrow", "sub"))
    mixed = lax.psum_scatter(
        jnp.dot(activate(gate_sums, up_sums), down_weight, preferred_element_type=F32),
        "wide",
        scatter_dimension=0,
        tiled=True,
    )
    return mixed.astype(BF16)


def swap(x, axis):
    return lax.ppermute(x, axis, [(0, 1), (1, 0)])


BLOCK = 256
VMEM = pl.BlockSpec(memory_space=pltpu.VMEM)
ANY = pl.BlockSpec(memory_space=pl.ANY)
HBM = pl.BlockSpec(memory_space=pltpu.HBM)
GRANT = pltpu.CompilerParams(vmem_limit_bytes=6 * 2**20)


def held_in(x):
    return pltpu.with_memory_space_constraint(x, pltpu.VMEM)


def left_in_hbm(x):
    return pltpu.with_memory_space_constraint(x, pltpu.HBM)


def block_copies(first, half, step, gate, up, dst, sem):
    core = lax.axis_index("sub")
    mine = jnp.int32(step >= half // BLOCK)
    side = jnp.where(mine == 1, core, 1 - core)
    unit = first + side * half + (step - mine * (half // BLOCK)) * BLOCK
    columns = pl.ds(pl.multiple_of(unit, BLOCK), BLOCK)
    return [
        pltpu.make_async_copy(weight.at[:, columns], dst.at[i], sem.at[i]) for i, weight in enumerate((gate, up))
    ]


def load_kernel(first, half, gate, up, held, sems):
    copies = [
        copy
        for step in range(held.shape[0])
        for copy in block_copies(first, half, step, gate, up, held.at[step], sems.at[step])
    ]
    for copy in copies:
        copy.start()
    for copy in copies:
        copy.wait()


def load(gate, up, chunk, steps):
    depth = gate.shape[0]
    return pl.pallas_call(
        functools.partial(load_kernel, chunk[0], chunk[1] // 2),
        out_shape=pltpu.VMEM((steps, 2, depth, BLOCK), BF16),
        in_specs=[HBM, HBM],
        out_specs=VMEM,
        scratch_shapes=[pltpu.SemaphoreType.DMA((steps, 2))],
        compiler_params=GRANT,
        cost_estimate=pl.CostEstimate(
            flops=0, bytes_accessed=4 * steps * depth * BLOCK, transcendentals=0
        ),
        name="load",
    )(left_in_hbm(gate), left_in_hbm(up))


def sums_kernel(first, steps, tokens, gate, up, *refs):
    send, keep, streamed, sems = refs[-4:]
    held = refs[0] if steps else None
    half = send.shape[1] // 2
    blocks = half // BLOCK

    def copies(step):
        at = step - steps
        return block_copies(first, half, step, gate, up, streamed.at[at], sems.at[at])

    for step in range(steps, 2 * blocks):
        for copy in copies(step):
            copy.start()

    def add(out, start, source, block):
        for i in range(2):
            column = pl.multiple_of((i * blocks + block - start) * BLOCK, BLOCK)
            out[:, pl.ds(column, BLOCK)] = jnp.dot(tokens[...], source[i], preferred_element_type=F32).astype(
                out.dtype
            )

    for side, out in enumerate((send, keep)):
        start, end = side * blocks, (side + 1) * blocks

        middle = min(max(steps, start), end)
        if start < middle:

            @pl.loop(start, middle)
            def _(step):
                add(out, start, held.at[step], step)

        if middle < end:

            @pl.loop(middle, end)
            def _(step):
                for copy in copies(step):
                    copy.wait()
                add(out, start, streamed.at[step - steps], step)


def sums(tokens, gate, up, chunk, held=None):
    rows, depth = tokens.shape
    first, width = chunk
    steps = 0 if held is None else held.shape[0]
    shape = (width // BLOCK - steps, 2, depth, BLOCK)
    return pl.pallas_call(
        functools.partial(sums_kernel, first, steps),
        out_shape=(jax.ShapeDtypeStruct((rows, width), BF16), jax.ShapeDtypeStruct((rows, width), F32)),
        in_specs=[VMEM, HBM, HBM] + [VMEM] * (steps > 0),
        out_specs=(VMEM, VMEM),
        scratch_shapes=[pltpu.VMEM(shape, BF16), pltpu.SemaphoreType.DMA(shape[:2])],
        compiler_params=pltpu.CompilerParams(vmem_limit_bytes=4 * shape[0] * depth * BLOCK + 4 * 2**20),
        cost_estimate=pl.CostEstimate(
            flops=4 * rows * depth * width, bytes_accessed=4 * depth * width, transcendentals=0
        ),
        name="sums",
    )(tokens, left_in_hbm(gate), left_in_hbm(up), *([held_in(held)] if steps else []))


def down_kernel(first, width, mine, other, weight, total, out):
    core = lax.axis_index("sub")
    half = width // 2
    starts = [pl.multiple_of(first + side * half, BLOCK) for side in (core, 1 - core)]

    @pl.loop(0, out.shape[1] // BLOCK)
    def _(block):
        columns = pl.ds(pl.multiple_of(block * BLOCK, BLOCK), BLOCK)
        part = total[:, columns]
        for start, hidden in zip(starts, (mine, other)):
            part += jnp.dot(hidden[...], weight[pl.ds(start, half), columns], preferred_element_type=F32)
        out[:, columns] = part


def down(mine, other, weight, total, first, width):
    rows, features = total.shape
    return pl.pallas_call(
        functools.partial(down_kernel, first, width),
        out_shape=jax.ShapeDtypeStruct(total.shape, F32),
        in_specs=[VMEM] * 4,
        out_specs=VMEM,
        compiler_params=GRANT,
        cost_estimate=pl.CostEstimate(
            flops=2 * rows * features * width, bytes_accessed=2 * features * width, transcendentals=0
        ),
        name="down",
    )(mine, other, held_in(weight), total)


def split(units):
    more = units // 512 * 8 // 13 * 512
    return (0, more), (more, units - more)


def across(x, apart):
    return lax.ppermute(x, "wide", [(i, i ^ apart) for i in range(4)])


def chunked(tokens, gate_weight, up_weight, down_weight):
    rows = tokens.shape[0]
    chunks = split(gate_weight.shape[1])
    section = tokens
    for apart in (3, 2, 1):
        section = lax.optimization_barrier(jnp.concatenate([section, across(tokens, apart)], axis=0))
    held = load(gate_weight, up_weight, chunks[0], 8)

    def core_sums(send, keep):
        total = keep + swap(send, "sub").astype(F32)
        return total, total.astype(BF16)

    def hidden_half(total, received):
        return activate(*jnp.split(total + received.astype(F32), 2, axis=1))

    def add(mixed, mine, chunk):
        return down(mine, swap(mine, "sub"), down_weight, mixed, *chunk)

    mixed = jnp.zeros((4 * rows, down_weight.shape[1]), F32)
    send, keep = sums(section, gate_weight, up_weight, chunks[0], held)
    total, sent = core_sums(send, keep)
    later, _ = lax.optimization_barrier((section, sent))
    send, keep = sums(later, gate_weight, up_weight, chunks[1])
    received, keep = lax.optimization_barrier((swap(sent, "narrow"), keep))
    mine = hidden_half(total, received)
    total, sent = core_sums(send, keep)
    mixed = add(mixed, mine, chunks[0])
    received, mixed = lax.optimization_barrier((swap(sent, "narrow"), mixed))
    mixed = add(mixed, hidden_half(total, received), chunks[1])
    blocks = mixed.reshape(4, rows, 2, -1).swapaxes(1, 2).reshape(4, 2 * rows, -1)
    out = blocks[0]
    for place, apart in enumerate((3, 2, 1), 1):
        received = across(blocks[place].astype(BF16), apart)
        out = lax.optimization_barrier(out + received.astype(F32))
    return out.astype(BF16).reshape(2, rows, -1).swapaxes(0, 1).reshape(rows, -1)


def solution(mesh):
    placed = (
        P(("groups", "wide"), ("narrow", "sub")),
        P(("narrow", "sub"), "wide"),
        P(("narrow", "sub"), "wide"),
        P("wide", ("narrow", "sub")),
    )
    sizes = tuple(mesh.shape[axis] for axis in ("groups", "wide", "narrow", "sub"))
    return jax.shard_map(
        chunked if sizes == (2, 4, 2, 2) else general,
        mesh=mesh,
        in_specs=placed,
        out_specs=P(("groups", "wide"), ("narrow", "sub")),
        check_vma=False,
    )
```

```python
import functools

import jax
import jax.numpy as jnp
from jax import lax
from jax.experimental import pallas as pl
from jax.experimental.pallas import tpu as pltpu
from jax.sharding import PartitionSpec as P

BF16 = jnp.bfloat16
F32 = jnp.float32


def activate(gate_sums, up_sums):
    return (jax.nn.silu(gate_sums) * up_sums).astype(BF16)


def general(tokens, gate_weight, up_weight, down_weight):
    section = lax.all_gather(tokens, "wide", axis=0, tiled=True)
    gate_part = jnp.dot(section, gate_weight, preferred_element_type=F32)
    up_part = jnp.dot(section, up_weight, preferred_element_type=F32)
    gate_sums = lax.psum(gate_part, ("narrow", "sub"))
    up_sums = lax.psum(up_part, ("narrow", "sub"))
    mixed = lax.psum_scatter(
        jnp.dot(activate(gate_sums, up_sums), down_weight, preferred_element_type=F32),
        "wide",
        scatter_dimension=0,
        tiled=True,
    )
    return mixed.astype(BF16)


def swap(x, axis):
    return lax.ppermute(x, axis, [(0, 1), (1, 0)])


BLOCK = 256
VMEM = pl.BlockSpec(memory_space=pltpu.VMEM)
ANY = pl.BlockSpec(memory_space=pl.ANY)
HBM = pl.BlockSpec(memory_space=pltpu.HBM)
GRANT = pltpu.CompilerParams(vmem_limit_bytes=6 * 2**20)


def held_in(x):
    return pltpu.with_memory_space_constraint(x, pltpu.VMEM)


def left_in_hbm(x):
    return pltpu.with_memory_space_constraint(x, pltpu.HBM)


def block_copies(first, half, step, gate, up, dst, sem):
    core = lax.axis_index("sub")
    mine = jnp.int32(step >= half // BLOCK)
    side = jnp.where(mine == 1, core, 1 - core)
    unit = first + side * half + (step - mine * (half // BLOCK)) * BLOCK
    columns = pl.ds(pl.multiple_of(unit, BLOCK), BLOCK)
    return [
        pltpu.make_async_copy(weight.at[:, columns], dst.at[:, pl.ds(i * BLOCK, BLOCK)], sem.at[i])
        for i, weight in enumerate((gate, up))
    ]


def pair(ref, at):
    return ref.at[:, pl.ds(pl.multiple_of(at * 2 * BLOCK, 2 * BLOCK), 2 * BLOCK)]


def load_kernel(first, half, gate, up, held, sems):
    copies = [
        copy
        for step in range(sems.shape[0])
        for copy in block_copies(first, half, step, gate, up, pair(held, step), sems.at[step])
    ]
    for copy in copies:
        copy.start()
    for copy in copies:
        copy.wait()


def load(gate, up, chunk, steps):
    depth = gate.shape[0]
    return pl.pallas_call(
        functools.partial(load_kernel, chunk[0], chunk[1] // 2),
        out_shape=pltpu.VMEM((depth, steps * 2 * BLOCK), BF16),
        in_specs=[HBM, HBM],
        out_specs=VMEM,
        scratch_shapes=[pltpu.SemaphoreType.DMA((steps, 2))],
        compiler_params=GRANT,
        cost_estimate=pl.CostEstimate(
            flops=0, bytes_accessed=4 * steps * depth * BLOCK, transcendentals=0
        ),
        name="load",
    )(left_in_hbm(gate), left_in_hbm(up))


def sums_kernel(first, steps, tokens, gate, up, *refs):
    send, keep, streamed, sems = refs[-4:]
    held = refs[0] if steps else None
    half = send.shape[1] // 2
    blocks = half // BLOCK

    def copies(step):
        at = step - steps
        return block_copies(first, half, step, gate, up, pair(streamed, at), sems.at[at])

    for step in range(steps, 2 * blocks):
        for copy in copies(step):
            copy.start()

    def add(out, start, source, block):
        both = jnp.dot(tokens[...], source[...], preferred_element_type=F32).astype(out.dtype)
        for i in range(2):
            column = pl.multiple_of((i * blocks + block - start) * BLOCK, BLOCK)
            out[:, pl.ds(column, BLOCK)] = both[:, i * BLOCK : (i + 1) * BLOCK]

    for side, out in enumerate((send, keep)):
        start, end = side * blocks, (side + 1) * blocks

        middle = min(max(steps, start), end)
        if start < middle:

            @pl.loop(start, middle)
            def _(step):
                add(out, start, pair(held, step), step)

        if middle < end:

            @pl.loop(middle, end)
            def _(step):
                for copy in copies(step):
                    copy.wait()
                add(out, start, pair(streamed, step - steps), step)


def sums(tokens, gate, up, chunk, held=None):
    rows, depth = tokens.shape
    first, width = chunk
    steps = 0 if held is None else held.shape[1] // (2 * BLOCK)
    streamed = width // BLOCK - steps
    return pl.pallas_call(
        functools.partial(sums_kernel, first, steps),
        out_shape=(jax.ShapeDtypeStruct((rows, width), BF16), jax.ShapeDtypeStruct((rows, width), F32)),
        in_specs=[VMEM, HBM, HBM] + [VMEM] * (steps > 0),
        out_specs=(VMEM, VMEM),
        scratch_shapes=[
            pltpu.VMEM((depth, streamed * 2 * BLOCK), BF16),
            pltpu.SemaphoreType.DMA((streamed, 2)),
        ],
        compiler_params=pltpu.CompilerParams(vmem_limit_bytes=4 * streamed * depth * BLOCK + 4 * 2**20),
        cost_estimate=pl.CostEstimate(
            flops=4 * rows * depth * width, bytes_accessed=4 * depth * width, transcendentals=0
        ),
        name="sums",
    )(tokens, left_in_hbm(gate), left_in_hbm(up), *([held_in(held)] if steps else []))


def partial_sums(first, half, sides, hiddens, weight, columns):
    core = lax.axis_index("sub")
    part = 0.0
    for side, hidden in zip(sides, hiddens):
        start = pl.multiple_of(first + jnp.where(core == side, 0, half), BLOCK)
        part += jnp.dot(hidden[...], weight[pl.ds(start, half), columns], preferred_element_type=F32)
    return part


def down_kernel(first, half, sides, weight, *refs):
    hiddens, out = refs[: len(sides)], refs[-1]
    totals = refs[len(sides) : -1]
    wide = 2 * BLOCK

    @pl.loop(0, out.shape[1] // wide)
    def _(block):
        columns = pl.ds(pl.multiple_of(block * wide, wide), wide)
        part = partial_sums(first, half, sides, hiddens, weight, columns)
        for total in totals:
            part += total[:, columns]
        out[:, columns] = part


def last_down_kernel(first, half, sides, weight, hidden, total, own, *sends):
    rows, columns = own.shape[0] // 2, own.shape[1]
    wide = 2 * BLOCK
    for block in range(columns // wide):
        at = block * wide
        parts = []
        for start in (at, columns + at):
            part = partial_sums(first, half, sides, [hidden], weight, pl.ds(start, wide))
            parts.append(part + total[:, pl.ds(start, wide)])
        for place, out in enumerate((own, *sends)):
            pieces = [part[place * rows : (place + 1) * rows] for part in parts]
            out[:, pl.ds(at, wide)] = jnp.concatenate(pieces, axis=0).astype(out.dtype)


def down(weight, chunk, sides, hiddens, total=None, last=False):
    rows, half = hiddens[0].shape
    features = weight.shape[1]
    if last:
        packed = (rows // 2, features // 2)
        out_shape = (jax.ShapeDtypeStruct(packed, F32),) + (jax.ShapeDtypeStruct(packed, BF16),) * 3
        kernel = last_down_kernel
    else:
        out_shape = jax.ShapeDtypeStruct((rows, features), F32)
        kernel = down_kernel
    operands = [held_in(weight), *hiddens] + ([] if total is None else [total])
    return pl.pallas_call(
        functools.partial(kernel, chunk[0], half, sides),
        out_shape=out_shape,
        in_specs=[VMEM] * len(operands),
        out_specs=(VMEM,) * 4 if last else VMEM,
        compiler_params=GRANT,
        cost_estimate=pl.CostEstimate(
            flops=2 * rows * features * half * len(sides),
            bytes_accessed=2 * features * half * len(sides),
            transcendentals=0,
        ),
        name="down",
    )(*operands)


def split(units):
    more = units // 512 * 8 // 13 * 512
    return (0, more), (more, units - more)


def across(x, apart):
    return lax.ppermute(x, "wide", [(i, i ^ apart) for i in range(4)])


def chunked(tokens, gate_weight, up_weight, down_weight):
    rows = tokens.shape[0]
    chunks = split(gate_weight.shape[1])
    section = tokens
    for apart in (3, 2, 1):
        section = lax.optimization_barrier(jnp.concatenate([section, across(tokens, apart)], axis=0))
    held = load(gate_weight, up_weight, chunks[0], 5)

    def core_sums(send, keep):
        total = keep + swap(send, "sub").astype(F32)
        return total, total.astype(BF16)

    def hidden_half(total, received):
        return activate(*jnp.split(total + received.astype(F32), 2, axis=1))

    send, keep = sums(section, gate_weight, up_weight, chunks[0], held)
    total, sent = core_sums(send, keep)
    later, _ = lax.optimization_barrier((section, sent))
    send, keep = sums(later, gate_weight, up_weight, chunks[1])
    received, keep = lax.optimization_barrier((swap(sent, "narrow"), keep))
    mine = hidden_half(total, received)
    total, sent = core_sums(send, keep)
    mixed = down(down_weight, chunks[0], (0, 1), (mine, swap(mine, "sub")))
    received, mixed = lax.optimization_barrier((swap(sent, "narrow"), mixed))
    mine = hidden_half(total, received)
    mixed = down(down_weight, chunks[1], (0,), (mine,), mixed)
    out, *blocks = down(down_weight, chunks[1], (1,), (swap(mine, "sub"),), mixed, last=True)
    for block, apart in zip(blocks, (3, 2, 1)):
        out = lax.optimization_barrier(out + across(block, apart).astype(F32))
    return out.astype(BF16).reshape(2, rows, -1).swapaxes(0, 1).reshape(rows, -1)


def solution(mesh):
    placed = (
        P(("groups", "wide"), ("narrow", "sub")),
        P(("narrow", "sub"), "wide"),
        P(("narrow", "sub"), "wide"),
        P("wide", ("narrow", "sub")),
    )
    sizes = tuple(mesh.shape[axis] for axis in ("groups", "wide", "narrow", "sub"))
    return jax.shard_map(
        chunked if sizes == (2, 4, 2, 2) else general,
        mesh=mesh,
        in_specs=placed,
        out_specs=P(("groups", "wide"), ("narrow", "sub")),
        check_vma=False,
    )
```

```python
import functools

import jax
import jax.numpy as jnp
from jax import lax
from jax.experimental import pallas as pl
from jax.experimental.pallas import tpu as pltpu
from jax.sharding import PartitionSpec as P

BF16 = jnp.bfloat16
F32 = jnp.float32


def activate(gate_sums, up_sums):
    return (jax.nn.silu(gate_sums) * up_sums).astype(BF16)


def general(tokens, gate_weight, up_weight, down_weight):
    section = lax.all_gather(tokens, "wide", axis=0, tiled=True)
    gate_part = jnp.dot(section, gate_weight, preferred_element_type=F32)
    up_part = jnp.dot(section, up_weight, preferred_element_type=F32)
    gate_sums = lax.psum(gate_part, ("narrow", "sub"))
    up_sums = lax.psum(up_part, ("narrow", "sub"))
    mixed = lax.psum_scatter(
        jnp.dot(activate(gate_sums, up_sums), down_weight, preferred_element_type=F32),
        "wide",
        scatter_dimension=0,
        tiled=True,
    )
    return mixed.astype(BF16)


def swap(x, axis):
    return lax.ppermute(x, axis, [(0, 1), (1, 0)])


BLOCK = 256
VMEM = pl.BlockSpec(memory_space=pltpu.VMEM)
ANY = pl.BlockSpec(memory_space=pl.ANY)
HBM = pl.BlockSpec(memory_space=pltpu.HBM)
GRANT = pltpu.CompilerParams(vmem_limit_bytes=6 * 2**20)


def held_in(x):
    return pltpu.with_memory_space_constraint(x, pltpu.VMEM)


def left_in_hbm(x):
    return pltpu.with_memory_space_constraint(x, pltpu.HBM)


def block_copies(first, half, step, gate, up, dst, sem):
    core = lax.axis_index("sub")
    mine = jnp.int32(step >= half // BLOCK)
    side = jnp.where(mine == 1, core, 1 - core)
    unit = first + side * half + (step - mine * (half // BLOCK)) * BLOCK
    columns = pl.ds(pl.multiple_of(unit, BLOCK), BLOCK)
    return [
        pltpu.make_async_copy(weight.at[:, columns], dst.at[:, pl.ds(i * BLOCK, BLOCK)], sem.at[i])
        for i, weight in enumerate((gate, up))
    ]


def pair(ref, at):
    return ref.at[:, pl.ds(pl.multiple_of(at * 2 * BLOCK, 2 * BLOCK), 2 * BLOCK)]


def load_kernel(first, half, gate, up, held, sems):
    copies = [
        copy
        for step in range(sems.shape[0])
        for copy in block_copies(first, half, step, gate, up, pair(held, step), sems.at[step])
    ]
    for copy in copies:
        copy.start()
    for copy in copies:
        copy.wait()


def load(gate, up, chunk, steps):
    depth = gate.shape[0]
    return pl.pallas_call(
        functools.partial(load_kernel, chunk[0], chunk[1] // 2),
        out_shape=pltpu.VMEM((depth, steps * 2 * BLOCK), BF16),
        in_specs=[HBM, HBM],
        out_specs=VMEM,
        scratch_shapes=[pltpu.SemaphoreType.DMA((steps, 2))],
        compiler_params=GRANT,
        cost_estimate=pl.CostEstimate(
            flops=0, bytes_accessed=4 * steps * depth * BLOCK, transcendentals=0
        ),
        name="load",
    )(left_in_hbm(gate), left_in_hbm(up))


def sums_kernel(first, steps, tokens, gate, up, *refs):
    send, keep, streamed, sems = refs[-4:]
    held = refs[0] if steps else None
    half = send.shape[1] // 2
    blocks = half // BLOCK

    def copies(step):
        at = step - steps
        return block_copies(first, half, step, gate, up, pair(streamed, at), sems.at[at])

    for step in range(steps, 2 * blocks):
        for copy in copies(step):
            copy.start()

    def add(out, start, source, block):
        both = jnp.dot(tokens[...], source[...], preferred_element_type=F32).astype(out.dtype)
        for i in range(2):
            column = pl.multiple_of((i * blocks + block - start) * BLOCK, BLOCK)
            out[:, pl.ds(column, BLOCK)] = both[:, i * BLOCK : (i + 1) * BLOCK]

    for side, out in enumerate((send, keep)):
        start, end = side * blocks, (side + 1) * blocks

        middle = min(max(steps, start), end)
        if start < middle:

            @pl.loop(start, middle)
            def _(step):
                add(out, start, pair(held, step), step)

        if middle < end:

            @pl.loop(middle, end)
            def _(step):
                for copy in copies(step):
                    copy.wait()
                add(out, start, pair(streamed, step - steps), step)


def sums(tokens, gate, up, chunk, held=None):
    rows, depth = tokens.shape
    first, width = chunk
    steps = 0 if held is None else held.shape[1] // (2 * BLOCK)
    streamed = width // BLOCK - steps
    return pl.pallas_call(
        functools.partial(sums_kernel, first, steps),
        out_shape=(jax.ShapeDtypeStruct((rows, width), BF16), jax.ShapeDtypeStruct((rows, width), F32)),
        in_specs=[VMEM, HBM, HBM] + [VMEM] * (steps > 0),
        out_specs=(VMEM, VMEM),
        scratch_shapes=[
            pltpu.VMEM((depth, streamed * 2 * BLOCK), BF16),
            pltpu.SemaphoreType.DMA((streamed, 2)),
        ],
        compiler_params=pltpu.CompilerParams(vmem_limit_bytes=4 * streamed * depth * BLOCK + 4 * 2**20),
        cost_estimate=pl.CostEstimate(
            flops=4 * rows * depth * width, bytes_accessed=4 * depth * width, transcendentals=0
        ),
        name="sums",
    )(tokens, left_in_hbm(gate), left_in_hbm(up), *([held_in(held)] if steps else []))


def partial_sums(first, half, sides, hiddens, weight, columns):
    core = lax.axis_index("sub")
    part = 0.0
    for side, hidden in zip(sides, hiddens):
        start = pl.multiple_of(first + jnp.where(core == side, 0, half), BLOCK)
        part += jnp.dot(hidden[...], weight[pl.ds(start, half), columns], preferred_element_type=F32)
    return part


def down_kernel(first, half, sides, weight, *refs):
    hiddens, out = refs[: len(sides)], refs[-1]
    totals = refs[len(sides) : -1]
    wide = 2 * BLOCK

    @pl.loop(0, out.shape[1] // wide)
    def _(block):
        columns = pl.ds(pl.multiple_of(block * wide, wide), wide)
        part = partial_sums(first, half, sides, hiddens, weight, columns)
        for total in totals:
            part += total[:, columns]
        out[:, columns] = part


def last_down_kernel(first, half, sides, weight, hidden, total, own, *sends):
    rows, columns = own.shape[0] // 2, own.shape[1]
    wide = 2 * BLOCK
    for block in range(columns // wide):
        at = block * wide
        parts = []
        for start in (at, columns + at):
            part = partial_sums(first, half, sides, [hidden], weight, pl.ds(start, wide))
            parts.append(part + total[:, pl.ds(start, wide)])
        for place, out in enumerate((own, *sends)):
            pieces = [part[place * rows : (place + 1) * rows] for part in parts]
            out[:, pl.ds(at, wide)] = jnp.concatenate(pieces, axis=0).astype(out.dtype)


def down(weight, chunk, sides, hiddens, total=None, last=False):
    rows, half = hiddens[0].shape
    features = weight.shape[1]
    if last:
        packed = (rows // 2, features // 2)
        out_shape = (jax.ShapeDtypeStruct(packed, F32),) + (jax.ShapeDtypeStruct(packed, BF16),) * 3
        kernel = last_down_kernel
    else:
        out_shape = jax.ShapeDtypeStruct((rows, features), F32)
        kernel = down_kernel
    operands = [held_in(weight), *hiddens] + ([] if total is None else [total])
    return pl.pallas_call(
        functools.partial(kernel, chunk[0], half, sides),
        out_shape=out_shape,
        in_specs=[VMEM] * len(operands),
        out_specs=(VMEM,) * 4 if last else VMEM,
        compiler_params=GRANT,
        cost_estimate=pl.CostEstimate(
            flops=2 * rows * features * half * len(sides),
            bytes_accessed=2 * features * half * len(sides),
            transcendentals=0,
        ),
        name="down",
    )(*operands)


def split(units):
    more = units // 512 * 8 // 13 * 512
    return (0, more), (more, units - more)


def across(x, apart):
    return lax.ppermute(x, "wide", [(i, i ^ apart) for i in range(4)])


def chunked(tokens, gate_weight, up_weight, down_weight):
    rows = tokens.shape[0]
    chunks = split(gate_weight.shape[1])
    section = tokens
    for apart in (3, 2, 1):
        section = lax.optimization_barrier(jnp.concatenate([section, across(tokens, apart)], axis=0))
    held = load(gate_weight, up_weight, chunks[0], 7)

    def core_sums(send, keep):
        total = keep + swap(send, "sub").astype(F32)
        return total, total.astype(BF16)

    def hidden_half(total, received):
        return activate(*jnp.split(total + received.astype(F32), 2, axis=1))

    send, keep = sums(section, gate_weight, up_weight, chunks[0], held)
    total, sent = core_sums(send, keep)
    later, _ = lax.optimization_barrier((section, sent))
    send, keep = sums(later, gate_weight, up_weight, chunks[1])
    received, keep = lax.optimization_barrier((swap(sent, "narrow"), keep))
    mine = hidden_half(total, received)
    total, sent = core_sums(send, keep)
    mixed = down(down_weight, chunks[0], (0, 1), (mine, swap(mine, "sub")))
    received, mixed = lax.optimization_barrier((swap(sent, "narrow"), mixed))
    mine = hidden_half(total, received)
    mixed = down(down_weight, chunks[1], (0,), (mine,), mixed)
    out, *blocks = down(down_weight, chunks[1], (1,), (swap(mine, "sub"),), mixed, last=True)
    for block, apart in zip(blocks, (3, 2, 1)):
        out = lax.optimization_barrier(out + across(block, apart).astype(F32))
    return out.astype(BF16).reshape(2, rows, -1).swapaxes(0, 1).reshape(rows, -1)


def solution(mesh):
    placed = (
        P(("groups", "wide"), ("narrow", "sub")),
        P(("narrow", "sub"), "wide"),
        P(("narrow", "sub"), "wide"),
        P("wide", ("narrow", "sub")),
    )
    sizes = tuple(mesh.shape[axis] for axis in ("groups", "wide", "narrow", "sub"))
    return jax.shard_map(
        chunked if sizes == (2, 4, 2, 2) else general,
        mesh=mesh,
        in_specs=placed,
        out_specs=P(("groups", "wide"), ("narrow", "sub")),
        check_vma=False,
    )
```

```python
import functools

import jax
import jax.numpy as jnp
from jax import lax
from jax.experimental import pallas as pl
from jax.experimental.pallas import tpu as pltpu
from jax.sharding import PartitionSpec as P

BF16 = jnp.bfloat16
F32 = jnp.float32


def activate(gate_sums, up_sums):
    return (jax.nn.silu(gate_sums) * up_sums).astype(BF16)


def general(tokens, gate_weight, up_weight, down_weight):
    section = lax.all_gather(tokens, "wide", axis=0, tiled=True)
    gate_part = jnp.dot(section, gate_weight, preferred_element_type=F32)
    up_part = jnp.dot(section, up_weight, preferred_element_type=F32)
    gate_sums = lax.psum(gate_part, ("narrow", "sub"))
    up_sums = lax.psum(up_part, ("narrow", "sub"))
    mixed = lax.psum_scatter(
        jnp.dot(activate(gate_sums, up_sums), down_weight, preferred_element_type=F32),
        "wide",
        scatter_dimension=0,
        tiled=True,
    )
    return mixed.astype(BF16)


def swap(x, axis):
    return lax.ppermute(x, axis, [(0, 1), (1, 0)])


BLOCK = 256
VMEM = pl.BlockSpec(memory_space=pltpu.VMEM)
ANY = pl.BlockSpec(memory_space=pl.ANY)
HBM = pl.BlockSpec(memory_space=pltpu.HBM)
GRANT = pltpu.CompilerParams(vmem_limit_bytes=6 * 2**20)


def held_in(x):
    return pltpu.with_memory_space_constraint(x, pltpu.VMEM)


def left_in_hbm(x):
    return pltpu.with_memory_space_constraint(x, pltpu.HBM)


SLOTS = 6


def beside_kernel(*refs):
    refs[-1][...] = jnp.zeros_like(refs[-1])


def beside(weight, *operands):
    operands = [left_in_hbm(weight), *operands]
    return pl.pallas_call(
        beside_kernel,
        out_shape=jax.ShapeDtypeStruct((8, 128), F32),
        in_specs=[HBM] + [ANY] * (len(operands) - 1),
        out_specs=VMEM,
        compiler_params=GRANT,
        cost_estimate=pl.CostEstimate(flops=0, bytes_accessed=2 * weight.size, transcendentals=0),
        name="beside",
    )(*operands)


def sums_kernel(first, tokens, gate, up, after, send, keep, slots, sems):
    half = send.shape[1] // 2
    blocks = half // BLOCK
    core = lax.axis_index("sub")

    def columns(step):
        mine = jnp.int32(step >= blocks)
        side = jnp.where(mine == 1, core, 1 - core)
        unit = first + side * half + (step - mine * blocks) * BLOCK
        return pl.ds(pl.multiple_of(unit, BLOCK), BLOCK)

    def slot(step):
        at = lax.rem(step, SLOTS)
        return slots.at[:, pl.ds(pl.multiple_of(at * BLOCK, BLOCK), BLOCK)], sems.at[at]

    def copy(step):
        return pltpu.make_async_copy(up.at[:, columns(step)], *slot(step))

    for step in range(min(SLOTS, 2 * blocks)):
        copy(jnp.int32(step)).start()

    for side, out in enumerate((send, keep)):

        @pl.loop(0, blocks)
        def _(block):
            step = side * blocks + block
            at = pl.multiple_of(block * BLOCK, BLOCK)
            out[:, pl.ds(at, BLOCK)] = jnp.dot(
                tokens[...], gate[:, columns(step)], preferred_element_type=F32
            ).astype(out.dtype)
            copy(step).wait()
            out[:, pl.ds(pl.multiple_of(half + at, BLOCK), BLOCK)] = jnp.dot(
                tokens[...], slot(step)[0][...], preferred_element_type=F32
            ).astype(out.dtype)

            @pl.when(step + SLOTS < 2 * blocks)
            def _():
                copy(step + SLOTS).start()


def sums(tokens, gate, up, chunk, after):
    rows, depth = tokens.shape
    first, width = chunk
    return pl.pallas_call(
        functools.partial(sums_kernel, first),
        out_shape=(jax.ShapeDtypeStruct((rows, width), BF16), jax.ShapeDtypeStruct((rows, width), F32)),
        in_specs=[VMEM, VMEM, HBM, ANY],
        out_specs=(VMEM, VMEM),
        scratch_shapes=[pltpu.VMEM((depth, SLOTS * BLOCK), BF16), pltpu.SemaphoreType.DMA((SLOTS,))],
        compiler_params=pltpu.CompilerParams(vmem_limit_bytes=2 * SLOTS * depth * BLOCK + 2 * 2**20),
        cost_estimate=pl.CostEstimate(
            flops=4 * rows * depth * width, bytes_accessed=4 * depth * width, transcendentals=0
        ),
        name="sums",
    )(tokens, held_in(gate), left_in_hbm(up), after)


def block_copies(first, half, step, gate, up, dst, sem):
    core = lax.axis_index("sub")
    mine = jnp.int32(step >= half // BLOCK)
    side = jnp.where(mine == 1, core, 1 - core)
    unit = first + side * half + (step - mine * (half // BLOCK)) * BLOCK
    columns = pl.ds(pl.multiple_of(unit, BLOCK), BLOCK)
    return [
        pltpu.make_async_copy(weight.at[:, columns], dst.at[:, pl.ds(i * BLOCK, BLOCK)], sem.at[i])
        for i, weight in enumerate((gate, up))
    ]


def pair(ref, at):
    return ref.at[:, pl.ds(pl.multiple_of(at * 2 * BLOCK, 2 * BLOCK), 2 * BLOCK)]


def stream_kernel(first, steps, tokens, gate, up, *refs):
    send, keep, streamed, sems = refs[-4:]
    held = refs[0] if steps else None
    half = send.shape[1] // 2
    blocks = half // BLOCK

    def copies(step):
        at = step - steps
        return block_copies(first, half, step, gate, up, pair(streamed, at), sems.at[at])

    for step in range(steps, 2 * blocks):
        for copy in copies(step):
            copy.start()

    def add(out, start, source, block):
        both = jnp.dot(tokens[...], source[...], preferred_element_type=F32).astype(out.dtype)
        for i in range(2):
            column = pl.multiple_of((i * blocks + block - start) * BLOCK, BLOCK)
            out[:, pl.ds(column, BLOCK)] = both[:, i * BLOCK : (i + 1) * BLOCK]

    for side, out in enumerate((send, keep)):
        start, end = side * blocks, (side + 1) * blocks

        middle = min(max(steps, start), end)
        if start < middle:

            @pl.loop(start, middle)
            def _(step):
                add(out, start, pair(held, step), step)

        if middle < end:

            @pl.loop(middle, end)
            def _(step):
                for copy in copies(step):
                    copy.wait()
                add(out, start, pair(streamed, step - steps), step)


def stream_sums(tokens, gate, up, chunk, held=None):
    rows, depth = tokens.shape
    first, width = chunk
    steps = 0 if held is None else held.shape[1] // (2 * BLOCK)
    streamed = width // BLOCK - steps
    return pl.pallas_call(
        functools.partial(stream_kernel, first, steps),
        out_shape=(jax.ShapeDtypeStruct((rows, width), BF16), jax.ShapeDtypeStruct((rows, width), F32)),
        in_specs=[VMEM, HBM, HBM] + [VMEM] * (steps > 0),
        out_specs=(VMEM, VMEM),
        scratch_shapes=[
            pltpu.VMEM((depth, streamed * 2 * BLOCK), BF16),
            pltpu.SemaphoreType.DMA((streamed, 2)),
        ],
        compiler_params=pltpu.CompilerParams(vmem_limit_bytes=4 * streamed * depth * BLOCK + 4 * 2**20),
        cost_estimate=pl.CostEstimate(
            flops=4 * rows * depth * width, bytes_accessed=4 * depth * width, transcendentals=0
        ),
        name="stream_sums",
    )(tokens, left_in_hbm(gate), left_in_hbm(up), *([held_in(held)] if steps else []))


def partial_sums(first, half, sides, hiddens, weight, columns):
    core = lax.axis_index("sub")
    part = 0.0
    for side, hidden in zip(sides, hiddens):
        start = pl.multiple_of(first + jnp.where(core == side, 0, half), BLOCK)
        part += jnp.dot(hidden[...], weight[pl.ds(start, half), columns], preferred_element_type=F32)
    return part


def down_kernel(first, half, sides, weight, *refs):
    hiddens, out = refs[: len(sides)], refs[-1]
    totals = refs[len(sides) : -1]
    wide = 2 * BLOCK

    @pl.loop(0, out.shape[1] // wide)
    def _(block):
        columns = pl.ds(pl.multiple_of(block * wide, wide), wide)
        part = partial_sums(first, half, sides, hiddens, weight, columns)
        for total in totals:
            part += total[:, columns]
        out[:, columns] = part


def last_down_kernel(first, half, sides, weight, hidden, total, own, *sends):
    rows, columns = own.shape[0] // 2, own.shape[1]
    wide = 2 * BLOCK
    for block in range(columns // wide):
        at = block * wide
        parts = []
        for start in (at, columns + at):
            part = partial_sums(first, half, sides, [hidden], weight, pl.ds(start, wide))
            parts.append(part + total[:, pl.ds(start, wide)])
        for place, out in enumerate((own, *sends)):
            pieces = [part[place * rows : (place + 1) * rows] for part in parts]
            out[:, pl.ds(at, wide)] = jnp.concatenate(pieces, axis=0).astype(out.dtype)


def down(weight, chunk, sides, hiddens, total=None, last=False):
    rows, half = hiddens[0].shape
    features = weight.shape[1]
    if last:
        packed = (rows // 2, features // 2)
        out_shape = (jax.ShapeDtypeStruct(packed, F32),) + (jax.ShapeDtypeStruct(packed, BF16),) * 3
        kernel = last_down_kernel
    else:
        out_shape = jax.ShapeDtypeStruct((rows, features), F32)
        kernel = down_kernel
    operands = [held_in(weight), *hiddens] + ([] if total is None else [total])
    return pl.pallas_call(
        functools.partial(kernel, chunk[0], half, sides),
        out_shape=out_shape,
        in_specs=[VMEM] * len(operands),
        out_specs=(VMEM,) * 4 if last else VMEM,
        compiler_params=GRANT,
        cost_estimate=pl.CostEstimate(
            flops=2 * rows * features * half * len(sides),
            bytes_accessed=2 * features * half * len(sides),
            transcendentals=0,
        ),
        name="down",
    )(*operands)


def split(units):
    more = units // 512 * 8 // 13 * 512
    return (0, more), (more, units - more)


def across(x, apart):
    return lax.ppermute(x, "wide", [(i, i ^ apart) for i in range(4)])


def chunked(tokens, gate_weight, up_weight, down_weight):
    rows = tokens.shape[0]
    chunks = split(gate_weight.shape[1])
    section = tokens
    for apart in (3, 2, 1):
        section = lax.optimization_barrier(jnp.concatenate([section, across(tokens, apart)], axis=0))
    def core_sums(send, keep):
        total = keep + swap(send, "sub").astype(F32)
        return total, total.astype(BF16)

    def hidden_half(total, received):
        return activate(*jnp.split(total + received.astype(F32), 2, axis=1))

    ready = beside(gate_weight)
    send, keep = sums(section, gate_weight, up_weight, chunks[0], ready)
    total, sent = core_sums(send, keep)
    later, _ = lax.optimization_barrier((section, sent))
    send, keep = stream_sums(later, gate_weight, up_weight, chunks[1])
    received, keep = lax.optimization_barrier((swap(sent, "narrow"), keep))
    mine = hidden_half(total, received)
    total, sent = core_sums(send, keep)
    mixed = down(down_weight, chunks[0], (0, 1), (mine, swap(mine, "sub")))
    received, mixed = lax.optimization_barrier((swap(sent, "narrow"), mixed))
    mine = hidden_half(total, received)
    mixed = down(down_weight, chunks[1], (0,), (mine,), mixed)
    out, *blocks = down(down_weight, chunks[1], (1,), (swap(mine, "sub"),), mixed, last=True)
    for block, apart in zip(blocks, (3, 2, 1)):
        out = lax.optimization_barrier(out + across(block, apart).astype(F32))
    return out.astype(BF16).reshape(2, rows, -1).swapaxes(0, 1).reshape(rows, -1)


def solution(mesh):
    placed = (
        P(("groups", "wide"), ("narrow", "sub")),
        P(("narrow", "sub"), "wide"),
        P(("narrow", "sub"), "wide"),
        P("wide", ("narrow", "sub")),
    )
    sizes = tuple(mesh.shape[axis] for axis in ("groups", "wide", "narrow", "sub"))
    return jax.shard_map(
        chunked if sizes == (2, 4, 2, 2) else general,
        mesh=mesh,
        in_specs=placed,
        out_specs=P(("groups", "wide"), ("narrow", "sub")),
        check_vma=False,
    )
```

```python
import functools

import jax
import jax.numpy as jnp
from jax import lax
from jax.experimental import pallas as pl
from jax.experimental.pallas import tpu as pltpu
from jax.sharding import PartitionSpec as P

BF16 = jnp.bfloat16
F32 = jnp.float32


def activate(gate_sums, up_sums):
    return (jax.nn.silu(gate_sums) * up_sums).astype(BF16)


def general(tokens, gate_weight, up_weight, down_weight):
    section = lax.all_gather(tokens, "wide", axis=0, tiled=True)
    gate_part = jnp.dot(section, gate_weight, preferred_element_type=F32)
    up_part = jnp.dot(section, up_weight, preferred_element_type=F32)
    gate_sums = lax.psum(gate_part, ("narrow", "sub"))
    up_sums = lax.psum(up_part, ("narrow", "sub"))
    mixed = lax.psum_scatter(
        jnp.dot(activate(gate_sums, up_sums), down_weight, preferred_element_type=F32),
        "wide",
        scatter_dimension=0,
        tiled=True,
    )
    return mixed.astype(BF16)


def swap(x, axis):
    return lax.ppermute(x, axis, [(0, 1), (1, 0)])


BLOCK = 256
VMEM = pl.BlockSpec(memory_space=pltpu.VMEM)
ANY = pl.BlockSpec(memory_space=pl.ANY)
HBM = pl.BlockSpec(memory_space=pltpu.HBM)
GRANT = pltpu.CompilerParams(vmem_limit_bytes=6 * 2**20)


def held_in(x):
    return pltpu.with_memory_space_constraint(x, pltpu.VMEM)


def left_in_hbm(x):
    return pltpu.with_memory_space_constraint(x, pltpu.HBM)


def beside_kernel(*refs):
    refs[-1][...] = jnp.zeros_like(refs[-1])


def beside(weight, *operands):
    operands = [left_in_hbm(weight), *operands]
    return pl.pallas_call(
        beside_kernel,
        out_shape=jax.ShapeDtypeStruct((8, 128), F32),
        in_specs=[HBM] + [ANY] * (len(operands) - 1),
        out_specs=VMEM,
        compiler_params=GRANT,
        cost_estimate=pl.CostEstimate(flops=0, bytes_accessed=2 * weight.size, transcendentals=0),
        name="beside",
    )(*operands)


def sums_kernel(first, tokens, gate, up, after, send, keep, held, sems):
    half = send.shape[1] // 2
    blocks = half // BLOCK
    core = lax.axis_index("sub")

    def columns(step):
        mine = jnp.int32(step >= blocks)
        side = jnp.where(mine == 1, core, 1 - core)
        unit = first + side * half + (step - mine * blocks) * BLOCK
        return pl.ds(pl.multiple_of(unit, BLOCK), BLOCK)

    def block_of(step):
        return pl.ds(pl.multiple_of(step * BLOCK, BLOCK), BLOCK)

    def copy(step):
        return pltpu.make_async_copy(up.at[:, columns(step)], held.at[:, block_of(step)], sems.at[step])

    for step in range(2 * blocks):
        copy(jnp.int32(step)).start()

    for side, out in enumerate((send, keep)):

        @pl.loop(0, blocks)
        def _(block):
            out[:, block_of(block)] = jnp.dot(
                tokens[...], gate[:, columns(side * blocks + block)], preferred_element_type=F32
            ).astype(out.dtype)

        @pl.loop(0, blocks)
        def _(block):
            step = side * blocks + block
            copy(step).wait()
            out[:, block_of(blocks + block)] = jnp.dot(
                tokens[...], held[:, block_of(step)], preferred_element_type=F32
            ).astype(out.dtype)


def sums(tokens, gate, up, chunk, after):
    rows, depth = tokens.shape
    first, width = chunk
    return pl.pallas_call(
        functools.partial(sums_kernel, first),
        out_shape=(jax.ShapeDtypeStruct((rows, width), BF16), jax.ShapeDtypeStruct((rows, width), F32)),
        in_specs=[VMEM, VMEM, HBM, ANY],
        out_specs=(VMEM, VMEM),
        scratch_shapes=[pltpu.VMEM((depth, width), BF16), pltpu.SemaphoreType.DMA((width // BLOCK,))],
        compiler_params=pltpu.CompilerParams(vmem_limit_bytes=2 * depth * width + 2 * 2**20),
        cost_estimate=pl.CostEstimate(
            flops=4 * rows * depth * width, bytes_accessed=4 * depth * width, transcendentals=0
        ),
        name="sums",
    )(tokens, held_in(gate), left_in_hbm(up), after)


def block_copies(first, half, step, gate, up, dst, sem):
    core = lax.axis_index("sub")
    mine = jnp.int32(step >= half // BLOCK)
    side = jnp.where(mine == 1, core, 1 - core)
    unit = first + side * half + (step - mine * (half // BLOCK)) * BLOCK
    columns = pl.ds(pl.multiple_of(unit, BLOCK), BLOCK)
    return [
        pltpu.make_async_copy(weight.at[:, columns], dst.at[:, pl.ds(i * BLOCK, BLOCK)], sem.at[i])
        for i, weight in enumerate((gate, up))
    ]


def pair(ref, at):
    return ref.at[:, pl.ds(pl.multiple_of(at * 2 * BLOCK, 2 * BLOCK), 2 * BLOCK)]


def stream_kernel(first, steps, tokens, gate, up, *refs):
    send, keep, streamed, sems = refs[-4:]
    held = refs[0] if steps else None
    half = send.shape[1] // 2
    blocks = half // BLOCK

    def copies(step):
        at = step - steps
        return block_copies(first, half, step, gate, up, pair(streamed, at), sems.at[at])

    for step in range(steps, 2 * blocks):
        for copy in copies(step):
            copy.start()

    def add(out, start, source, block):
        both = jnp.dot(tokens[...], source[...], preferred_element_type=F32).astype(out.dtype)
        for i in range(2):
            column = pl.multiple_of((i * blocks + block - start) * BLOCK, BLOCK)
            out[:, pl.ds(column, BLOCK)] = both[:, i * BLOCK : (i + 1) * BLOCK]

    for side, out in enumerate((send, keep)):
        start, end = side * blocks, (side + 1) * blocks

        middle = min(max(steps, start), end)
        if start < middle:

            @pl.loop(start, middle)
            def _(step):
                add(out, start, pair(held, step), step)

        if middle < end:

            @pl.loop(middle, end)
            def _(step):
                for copy in copies(step):
                    copy.wait()
                add(out, start, pair(streamed, step - steps), step)


def stream_sums(tokens, gate, up, chunk, held=None):
    rows, depth = tokens.shape
    first, width = chunk
    steps = 0 if held is None else held.shape[1] // (2 * BLOCK)
    streamed = width // BLOCK - steps
    return pl.pallas_call(
        functools.partial(stream_kernel, first, steps),
        out_shape=(jax.ShapeDtypeStruct((rows, width), BF16), jax.ShapeDtypeStruct((rows, width), F32)),
        in_specs=[VMEM, HBM, HBM] + [VMEM] * (steps > 0),
        out_specs=(VMEM, VMEM),
        scratch_shapes=[
            pltpu.VMEM((depth, streamed * 2 * BLOCK), BF16),
            pltpu.SemaphoreType.DMA((streamed, 2)),
        ],
        compiler_params=pltpu.CompilerParams(vmem_limit_bytes=4 * streamed * depth * BLOCK + 4 * 2**20),
        cost_estimate=pl.CostEstimate(
            flops=4 * rows * depth * width, bytes_accessed=4 * depth * width, transcendentals=0
        ),
        name="stream_sums",
    )(tokens, left_in_hbm(gate), left_in_hbm(up), *([held_in(held)] if steps else []))


def partial_sums(first, half, sides, hiddens, weight, columns):
    core = lax.axis_index("sub")
    part = 0.0
    for side, hidden in zip(sides, hiddens):
        start = pl.multiple_of(first + jnp.where(core == side, 0, half), BLOCK)
        part += jnp.dot(hidden[...], weight[pl.ds(start, half), columns], preferred_element_type=F32)
    return part


def down_kernel(first, half, sides, weight, *refs):
    hiddens, out = refs[: len(sides)], refs[-1]
    totals = refs[len(sides) : -1]
    wide = 2 * BLOCK

    @pl.loop(0, out.shape[1] // wide)
    def _(block):
        columns = pl.ds(pl.multiple_of(block * wide, wide), wide)
        part = partial_sums(first, half, sides, hiddens, weight, columns)
        for total in totals:
            part += total[:, columns]
        out[:, columns] = part


def last_down_kernel(first, half, sides, weight, hidden, total, own, *sends):
    rows, columns = own.shape[0] // 2, own.shape[1]
    wide = 2 * BLOCK
    for block in range(columns // wide):
        at = block * wide
        parts = []
        for start in (at, columns + at):
            part = partial_sums(first, half, sides, [hidden], weight, pl.ds(start, wide))
            parts.append(part + total[:, pl.ds(start, wide)])
        for place, out in enumerate((own, *sends)):
            pieces = [part[place * rows : (place + 1) * rows] for part in parts]
            out[:, pl.ds(at, wide)] = jnp.concatenate(pieces, axis=0).astype(out.dtype)


def down(weight, chunk, sides, hiddens, total=None, last=False):
    rows, half = hiddens[0].shape
    features = weight.shape[1]
    if last:
        packed = (rows // 2, features // 2)
        out_shape = (jax.ShapeDtypeStruct(packed, F32),) + (jax.ShapeDtypeStruct(packed, BF16),) * 3
        kernel = last_down_kernel
    else:
        out_shape = jax.ShapeDtypeStruct((rows, features), F32)
        kernel = down_kernel
    operands = [held_in(weight), *hiddens] + ([] if total is None else [total])
    return pl.pallas_call(
        functools.partial(kernel, chunk[0], half, sides),
        out_shape=out_shape,
        in_specs=[VMEM] * len(operands),
        out_specs=(VMEM,) * 4 if last else VMEM,
        compiler_params=GRANT,
        cost_estimate=pl.CostEstimate(
            flops=2 * rows * features * half * len(sides),
            bytes_accessed=2 * features * half * len(sides),
            transcendentals=0,
        ),
        name="down",
    )(*operands)


def split(units):
    more = units // 512 * 8 // 13 * 512
    return (0, more), (more, units - more)


def across(x, apart):
    return lax.ppermute(x, "wide", [(i, i ^ apart) for i in range(4)])


def chunked(tokens, gate_weight, up_weight, down_weight):
    rows = tokens.shape[0]
    chunks = split(gate_weight.shape[1])
    section = tokens
    for apart in (3, 2, 1):
        section = lax.optimization_barrier(jnp.concatenate([section, across(tokens, apart)], axis=0))
    def core_sums(send, keep):
        total = keep + swap(send, "sub").astype(F32)
        return total, total.astype(BF16)

    def hidden_half(total, received):
        return activate(*jnp.split(total + received.astype(F32), 2, axis=1))

    ready = beside(gate_weight)
    send, keep = sums(section, gate_weight, up_weight, chunks[0], ready)
    total, sent = core_sums(send, keep)
    later, _ = lax.optimization_barrier((section, sent))
    send, keep = stream_sums(later, gate_weight, up_weight, chunks[1])
    received, keep = lax.optimization_barrier((swap(sent, "narrow"), keep))
    mine = hidden_half(total, received)
    total, sent = core_sums(send, keep)
    mixed = down(down_weight, chunks[0], (0, 1), (mine, swap(mine, "sub")))
    received, mixed = lax.optimization_barrier((swap(sent, "narrow"), mixed))
    mine = hidden_half(total, received)
    mixed = down(down_weight, chunks[1], (0,), (mine,), mixed)
    out, *blocks = down(down_weight, chunks[1], (1,), (swap(mine, "sub"),), mixed, last=True)
    for block, apart in zip(blocks, (3, 2, 1)):
        out = lax.optimization_barrier(out + across(block, apart).astype(F32))
    return out.astype(BF16).reshape(2, rows, -1).swapaxes(0, 1).reshape(rows, -1)


def solution(mesh):
    placed = (
        P(("groups", "wide"), ("narrow", "sub")),
        P(("narrow", "sub"), "wide"),
        P(("narrow", "sub"), "wide"),
        P("wide", ("narrow", "sub")),
    )
    sizes = tuple(mesh.shape[axis] for axis in ("groups", "wide", "narrow", "sub"))
    return jax.shard_map(
        chunked if sizes == (2, 4, 2, 2) else general,
        mesh=mesh,
        in_specs=placed,
        out_specs=P(("groups", "wide"), ("narrow", "sub")),
        check_vma=False,
    )
```

```python
import functools

import jax
import jax.numpy as jnp
from jax import lax
from jax.experimental import pallas as pl
from jax.experimental.pallas import tpu as pltpu
from jax.sharding import PartitionSpec as P

BF16 = jnp.bfloat16
F32 = jnp.float32


def activate(gate_sums, up_sums):
    return (jax.nn.silu(gate_sums) * up_sums).astype(BF16)


def general(tokens, gate_weight, up_weight, down_weight):
    section = lax.all_gather(tokens, "wide", axis=0, tiled=True)
    gate_part = jnp.dot(section, gate_weight, preferred_element_type=F32)
    up_part = jnp.dot(section, up_weight, preferred_element_type=F32)
    gate_sums = lax.psum(gate_part, ("narrow", "sub"))
    up_sums = lax.psum(up_part, ("narrow", "sub"))
    mixed = lax.psum_scatter(
        jnp.dot(activate(gate_sums, up_sums), down_weight, preferred_element_type=F32),
        "wide",
        scatter_dimension=0,
        tiled=True,
    )
    return mixed.astype(BF16)


def swap(x, axis):
    return lax.ppermute(x, axis, [(0, 1), (1, 0)])


BLOCK = 256
WIDE = 1024
VMEM = pl.BlockSpec(memory_space=pltpu.VMEM)
ANY = pl.BlockSpec(memory_space=pl.ANY)
HBM = pl.BlockSpec(memory_space=pltpu.HBM)
GRANT = pltpu.CompilerParams(vmem_limit_bytes=6 * 2**20)


def held_in(x):
    return pltpu.with_memory_space_constraint(x, pltpu.VMEM)


def left_in_hbm(x):
    return pltpu.with_memory_space_constraint(x, pltpu.HBM)


def beside_kernel(*refs):
    refs[-1][...] = jnp.zeros_like(refs[-1])


def beside(weight, *operands):
    operands = [left_in_hbm(weight), *operands]
    return pl.pallas_call(
        beside_kernel,
        out_shape=jax.ShapeDtypeStruct((8, 128), F32),
        in_specs=[HBM] + [ANY] * (len(operands) - 1),
        out_specs=VMEM,
        compiler_params=GRANT,
        cost_estimate=pl.CostEstimate(flops=0, bytes_accessed=2 * weight.size, transcendentals=0),
        name="beside",
    )(*operands)


def sums_kernel(first, tokens, gate, up, after, send, keep, held, sems):
    half = send.shape[1] // 2
    core = lax.axis_index("sub")

    def side_of(place):
        return first + jnp.where(core == place, 1, 0) * half

    copies = [
        [
            pltpu.make_async_copy(
                up.at[:, pl.ds(pl.multiple_of(side_of(place) + at, BLOCK), BLOCK)],
                held.at[:, pl.ds(place * half + at, BLOCK)],
                sems.at[place * (half // BLOCK) + at // BLOCK],
            )
            for at in range(0, half, BLOCK)
        ]
        for place in range(2)
    ]
    for copy in copies[0] + copies[1]:
        copy.start()

    for place, out in enumerate((send, keep)):
        for at in range(0, half, WIDE):
            wide = min(WIDE, half - at)
            columns = pl.ds(pl.multiple_of(side_of(place) + at, BLOCK), wide)
            out[:, pl.ds(at, wide)] = jnp.dot(
                tokens[...], gate[:, columns], preferred_element_type=F32
            ).astype(out.dtype)
        for at in range(0, half, WIDE):
            wide = min(WIDE, half - at)
            for copy in copies[place][at // BLOCK : (at + wide) // BLOCK]:
                copy.wait()
            out[:, pl.ds(half + at, wide)] = jnp.dot(
                tokens[...], held[:, pl.ds(place * half + at, wide)], preferred_element_type=F32
            ).astype(out.dtype)


def sums(tokens, gate, up, chunk, after):
    rows, depth = tokens.shape
    first, width = chunk
    return pl.pallas_call(
        functools.partial(sums_kernel, first),
        out_shape=(jax.ShapeDtypeStruct((rows, width), BF16), jax.ShapeDtypeStruct((rows, width), F32)),
        in_specs=[VMEM, VMEM, HBM, ANY],
        out_specs=(VMEM, VMEM),
        scratch_shapes=[pltpu.VMEM((depth, width), BF16), pltpu.SemaphoreType.DMA((width // BLOCK,))],
        compiler_params=pltpu.CompilerParams(vmem_limit_bytes=2 * depth * width + 2 * 2**20),
        cost_estimate=pl.CostEstimate(
            flops=4 * rows * depth * width, bytes_accessed=4 * depth * width, transcendentals=0
        ),
        name="sums",
    )(tokens, held_in(gate), left_in_hbm(up), after)


def block_copies(first, half, step, gate, up, dst, sem):
    core = lax.axis_index("sub")
    mine = jnp.int32(step >= half // BLOCK)
    side = jnp.where(mine == 1, core, 1 - core)
    unit = first + side * half + (step - mine * (half // BLOCK)) * BLOCK
    columns = pl.ds(pl.multiple_of(unit, BLOCK), BLOCK)
    return [
        pltpu.make_async_copy(weight.at[:, columns], dst.at[:, pl.ds(i * BLOCK, BLOCK)], sem.at[i])
        for i, weight in enumerate((gate, up))
    ]


def pair(ref, at):
    return ref.at[:, pl.ds(pl.multiple_of(at * 2 * BLOCK, 2 * BLOCK), 2 * BLOCK)]


def stream_kernel(first, steps, tokens, gate, up, *refs):
    send, keep, streamed, sems = refs[-4:]
    held = refs[0] if steps else None
    half = send.shape[1] // 2
    blocks = half // BLOCK

    def copies(step):
        at = step - steps
        return block_copies(first, half, step, gate, up, pair(streamed, at), sems.at[at])

    for step in range(steps, 2 * blocks):
        for copy in copies(step):
            copy.start()

    def add(out, start, source, block):
        both = jnp.dot(tokens[...], source[...], preferred_element_type=F32).astype(out.dtype)
        for i in range(2):
            column = pl.multiple_of((i * blocks + block - start) * BLOCK, BLOCK)
            out[:, pl.ds(column, BLOCK)] = both[:, i * BLOCK : (i + 1) * BLOCK]

    for side, out in enumerate((send, keep)):
        start, end = side * blocks, (side + 1) * blocks

        middle = min(max(steps, start), end)
        if start < middle:

            @pl.loop(start, middle)
            def _(step):
                add(out, start, pair(held, step), step)

        if middle < end:

            @pl.loop(middle, end)
            def _(step):
                for copy in copies(step):
                    copy.wait()
                add(out, start, pair(streamed, step - steps), step)


def stream_sums(tokens, gate, up, chunk, held=None):
    rows, depth = tokens.shape
    first, width = chunk
    steps = 0 if held is None else held.shape[1] // (2 * BLOCK)
    streamed = width // BLOCK - steps
    return pl.pallas_call(
        functools.partial(stream_kernel, first, steps),
        out_shape=(jax.ShapeDtypeStruct((rows, width), BF16), jax.ShapeDtypeStruct((rows, width), F32)),
        in_specs=[VMEM, HBM, HBM] + [VMEM] * (steps > 0),
        out_specs=(VMEM, VMEM),
        scratch_shapes=[
            pltpu.VMEM((depth, streamed * 2 * BLOCK), BF16),
            pltpu.SemaphoreType.DMA((streamed, 2)),
        ],
        compiler_params=pltpu.CompilerParams(vmem_limit_bytes=4 * streamed * depth * BLOCK + 4 * 2**20),
        cost_estimate=pl.CostEstimate(
            flops=4 * rows * depth * width, bytes_accessed=4 * depth * width, transcendentals=0
        ),
        name="stream_sums",
    )(tokens, left_in_hbm(gate), left_in_hbm(up), *([held_in(held)] if steps else []))


def partial_sums(first, half, sides, hiddens, weight, columns):
    core = lax.axis_index("sub")
    part = 0.0
    for side, hidden in zip(sides, hiddens):
        start = pl.multiple_of(first + jnp.where(core == side, 0, half), BLOCK)
        part += jnp.dot(hidden[...], weight[pl.ds(start, half), columns], preferred_element_type=F32)
    return part


def down_kernel(first, half, sides, weight, *refs):
    hiddens, out = refs[: len(sides)], refs[-1]
    totals = refs[len(sides) : -1]
    wide = 2 * BLOCK

    @pl.loop(0, out.shape[1] // wide)
    def _(block):
        columns = pl.ds(pl.multiple_of(block * wide, wide), wide)
        part = partial_sums(first, half, sides, hiddens, weight, columns)
        for total in totals:
            part += total[:, columns]
        out[:, columns] = part


def last_down_kernel(first, half, sides, weight, hidden, total, own, *sends):
    rows, columns = own.shape[0] // 2, own.shape[1]
    wide = 2 * BLOCK
    for block in range(columns // wide):
        at = block * wide
        parts = []
        for start in (at, columns + at):
            part = partial_sums(first, half, sides, [hidden], weight, pl.ds(start, wide))
            parts.append(part + total[:, pl.ds(start, wide)])
        for place, out in enumerate((own, *sends)):
            pieces = [part[place * rows : (place + 1) * rows] for part in parts]
            out[:, pl.ds(at, wide)] = jnp.concatenate(pieces, axis=0).astype(out.dtype)


def down(weight, chunk, sides, hiddens, total=None, last=False):
    rows, half = hiddens[0].shape
    features = weight.shape[1]
    if last:
        packed = (rows // 2, features // 2)
        out_shape = (jax.ShapeDtypeStruct(packed, F32),) + (jax.ShapeDtypeStruct(packed, BF16),) * 3
        kernel = last_down_kernel
    else:
        out_shape = jax.ShapeDtypeStruct((rows, features), F32)
        kernel = down_kernel
    operands = [held_in(weight), *hiddens] + ([] if total is None else [total])
    return pl.pallas_call(
        functools.partial(kernel, chunk[0], half, sides),
        out_shape=out_shape,
        in_specs=[VMEM] * len(operands),
        out_specs=(VMEM,) * 4 if last else VMEM,
        compiler_params=GRANT,
        cost_estimate=pl.CostEstimate(
            flops=2 * rows * features * half * len(sides),
            bytes_accessed=2 * features * half * len(sides),
            transcendentals=0,
        ),
        name="down",
    )(*operands)


def split(units):
    more = units // 512 * 8 // 13 * 512
    return (0, more), (more, units - more)


def across(x, apart):
    return lax.ppermute(x, "wide", [(i, i ^ apart) for i in range(4)])


def chunked(tokens, gate_weight, up_weight, down_weight):
    rows = tokens.shape[0]
    chunks = split(gate_weight.shape[1])
    section = tokens
    for apart in (3, 2, 1):
        section = lax.optimization_barrier(jnp.concatenate([section, across(tokens, apart)], axis=0))
    def core_sums(send, keep):
        total = keep + swap(send, "sub").astype(F32)
        return total, total.astype(BF16)

    def hidden_half(total, received):
        return activate(*jnp.split(total + received.astype(F32), 2, axis=1))

    ready = beside(gate_weight)
    send, keep = sums(section, gate_weight, up_weight, chunks[0], ready)
    total, sent = core_sums(send, keep)
    later, _ = lax.optimization_barrier((section, sent))
    send, keep = stream_sums(later, gate_weight, up_weight, chunks[1])
    received, keep = lax.optimization_barrier((swap(sent, "narrow"), keep))
    mine = hidden_half(total, received)
    total, sent = core_sums(send, keep)
    mixed = down(down_weight, chunks[0], (0, 1), (mine, swap(mine, "sub")))
    received, mixed = lax.optimization_barrier((swap(sent, "narrow"), mixed))
    mine = hidden_half(total, received)
    mixed = down(down_weight, chunks[1], (0,), (mine,), mixed)
    out, *blocks = down(down_weight, chunks[1], (1,), (swap(mine, "sub"),), mixed, last=True)
    for block, apart in zip(blocks, (3, 2, 1)):
        out = lax.optimization_barrier(out + across(block, apart).astype(F32))
    return out.astype(BF16).reshape(2, rows, -1).swapaxes(0, 1).reshape(rows, -1)


def solution(mesh):
    placed = (
        P(("groups", "wide"), ("narrow", "sub")),
        P(("narrow", "sub"), "wide"),
        P(("narrow", "sub"), "wide"),
        P("wide", ("narrow", "sub")),
    )
    sizes = tuple(mesh.shape[axis] for axis in ("groups", "wide", "narrow", "sub"))
    return jax.shard_map(
        chunked if sizes == (2, 4, 2, 2) else general,
        mesh=mesh,
        in_specs=placed,
        out_specs=P(("groups", "wide"), ("narrow", "sub")),
        check_vma=False,
    )
```

```python
import functools

import jax
import jax.numpy as jnp
from jax import lax
from jax.experimental import pallas as pl
from jax.experimental.pallas import tpu as pltpu
from jax.sharding import PartitionSpec as P

BF16 = jnp.bfloat16
F32 = jnp.float32


def activate(gate_sums, up_sums):
    return (jax.nn.silu(gate_sums) * up_sums).astype(BF16)


def general(tokens, gate_weight, up_weight, down_weight):
    section = lax.all_gather(tokens, "wide", axis=0, tiled=True)
    gate_part = jnp.dot(section, gate_weight, preferred_element_type=F32)
    up_part = jnp.dot(section, up_weight, preferred_element_type=F32)
    gate_sums = lax.psum(gate_part, ("narrow", "sub"))
    up_sums = lax.psum(up_part, ("narrow", "sub"))
    mixed = lax.psum_scatter(
        jnp.dot(activate(gate_sums, up_sums), down_weight, preferred_element_type=F32),
        "wide",
        scatter_dimension=0,
        tiled=True,
    )
    return mixed.astype(BF16)


def swap(x, axis):
    return lax.ppermute(x, axis, [(0, 1), (1, 0)])


BLOCK = 256
WIDE = 512
VMEM = pl.BlockSpec(memory_space=pltpu.VMEM)
ANY = pl.BlockSpec(memory_space=pl.ANY)
HBM = pl.BlockSpec(memory_space=pltpu.HBM)
GRANT = pltpu.CompilerParams(vmem_limit_bytes=6 * 2**20)


def held_in(x):
    return pltpu.with_memory_space_constraint(x, pltpu.VMEM)


def left_in_hbm(x):
    return pltpu.with_memory_space_constraint(x, pltpu.HBM)


def beside_kernel(*refs):
    refs[-1][...] = jnp.zeros_like(refs[-1])


def beside(weight, *operands):
    operands = [left_in_hbm(weight), *operands]
    return pl.pallas_call(
        beside_kernel,
        out_shape=jax.ShapeDtypeStruct((8, 128), F32),
        in_specs=[HBM] + [ANY] * (len(operands) - 1),
        out_specs=VMEM,
        compiler_params=GRANT,
        cost_estimate=pl.CostEstimate(flops=0, bytes_accessed=2 * weight.size, transcendentals=0),
        name="beside",
    )(*operands)


def sums_kernel(first, tokens, gate, up, after, send, keep, held, sems):
    half = send.shape[1] // 2
    core = lax.axis_index("sub")

    def side_of(place):
        return first + jnp.where(core == place, 1, 0) * half

    copies = [
        [
            pltpu.make_async_copy(
                up.at[:, pl.ds(pl.multiple_of(side_of(place) + at, BLOCK), BLOCK)],
                held.at[:, pl.ds(place * half + at, BLOCK)],
                sems.at[place * (half // BLOCK) + at // BLOCK],
            )
            for at in range(0, half, BLOCK)
        ]
        for place in range(2)
    ]
    for copy in copies[0] + copies[1]:
        copy.start()

    for place, out in enumerate((send, keep)):
        for at in range(0, half, WIDE):
            wide = min(WIDE, half - at)
            columns = pl.ds(pl.multiple_of(side_of(place) + at, BLOCK), wide)
            out[:, pl.ds(at, wide)] = jnp.dot(
                tokens[...], gate[:, columns], preferred_element_type=F32
            ).astype(out.dtype)
        for at in range(0, half, WIDE):
            wide = min(WIDE, half - at)
            for copy in copies[place][at // BLOCK : (at + wide) // BLOCK]:
                copy.wait()
            out[:, pl.ds(half + at, wide)] = jnp.dot(
                tokens[...], held[:, pl.ds(place * half + at, wide)], preferred_element_type=F32
            ).astype(out.dtype)


def sums(tokens, gate, up, chunk, after):
    rows, depth = tokens.shape
    first, width = chunk
    return pl.pallas_call(
        functools.partial(sums_kernel, first),
        out_shape=(jax.ShapeDtypeStruct((rows, width), BF16), jax.ShapeDtypeStruct((rows, width), F32)),
        in_specs=[VMEM, VMEM, HBM, ANY],
        out_specs=(VMEM, VMEM),
        scratch_shapes=[pltpu.VMEM((depth, width), BF16), pltpu.SemaphoreType.DMA((width // BLOCK,))],
        compiler_params=pltpu.CompilerParams(vmem_limit_bytes=2 * depth * width + 2 * 2**20),
        cost_estimate=pl.CostEstimate(
            flops=4 * rows * depth * width, bytes_accessed=4 * depth * width, transcendentals=0
        ),
        name="sums",
    )(tokens, held_in(gate), left_in_hbm(up), after)


def block_copies(first, half, step, gate, up, dst, sem):
    core = lax.axis_index("sub")
    mine = jnp.int32(step >= half // BLOCK)
    side = jnp.where(mine == 1, core, 1 - core)
    unit = first + side * half + (step - mine * (half // BLOCK)) * BLOCK
    columns = pl.ds(pl.multiple_of(unit, BLOCK), BLOCK)
    return [
        pltpu.make_async_copy(weight.at[:, columns], dst.at[:, pl.ds(i * BLOCK, BLOCK)], sem.at[i])
        for i, weight in enumerate((gate, up))
    ]


def pair(ref, at):
    return ref.at[:, pl.ds(pl.multiple_of(at * 2 * BLOCK, 2 * BLOCK), 2 * BLOCK)]


def stream_kernel(first, steps, tokens, gate, up, *refs):
    send, keep, streamed, sems = refs[-4:]
    held = refs[0] if steps else None
    half = send.shape[1] // 2
    blocks = half // BLOCK

    def copies(step):
        at = step - steps
        return block_copies(first, half, step, gate, up, pair(streamed, at), sems.at[at])

    for step in range(steps, 2 * blocks):
        for copy in copies(step):
            copy.start()

    def add(out, start, source, block):
        both = jnp.dot(tokens[...], source[...], preferred_element_type=F32).astype(out.dtype)
        for i in range(2):
            column = pl.multiple_of((i * blocks + block - start) * BLOCK, BLOCK)
            out[:, pl.ds(column, BLOCK)] = both[:, i * BLOCK : (i + 1) * BLOCK]

    for side, out in enumerate((send, keep)):
        start, end = side * blocks, (side + 1) * blocks

        middle = min(max(steps, start), end)
        if start < middle:

            @pl.loop(start, middle)
            def _(step):
                add(out, start, pair(held, step), step)

        if middle < end:

            @pl.loop(middle, end)
            def _(step):
                for copy in copies(step):
                    copy.wait()
                add(out, start, pair(streamed, step - steps), step)


def stream_sums(tokens, gate, up, chunk, held=None):
    rows, depth = tokens.shape
    first, width = chunk
    steps = 0 if held is None else held.shape[1] // (2 * BLOCK)
    streamed = width // BLOCK - steps
    return pl.pallas_call(
        functools.partial(stream_kernel, first, steps),
        out_shape=(jax.ShapeDtypeStruct((rows, width), BF16), jax.ShapeDtypeStruct((rows, width), F32)),
        in_specs=[VMEM, HBM, HBM] + [VMEM] * (steps > 0),
        out_specs=(VMEM, VMEM),
        scratch_shapes=[
            pltpu.VMEM((depth, streamed * 2 * BLOCK), BF16),
            pltpu.SemaphoreType.DMA((streamed, 2)),
        ],
        compiler_params=pltpu.CompilerParams(vmem_limit_bytes=4 * streamed * depth * BLOCK + 4 * 2**20),
        cost_estimate=pl.CostEstimate(
            flops=4 * rows * depth * width, bytes_accessed=4 * depth * width, transcendentals=0
        ),
        name="stream_sums",
    )(tokens, left_in_hbm(gate), left_in_hbm(up), *([held_in(held)] if steps else []))


def partial_sums(first, half, sides, hiddens, weight, columns):
    core = lax.axis_index("sub")
    part = 0.0
    for side, hidden in zip(sides, hiddens):
        start = pl.multiple_of(first + jnp.where(core == side, 0, half), BLOCK)
        part += jnp.dot(hidden[...], weight[pl.ds(start, half), columns], preferred_element_type=F32)
    return part


def down_kernel(first, half, sides, weight, *refs):
    hiddens, out = refs[: len(sides)], refs[-1]
    totals = refs[len(sides) : -1]
    for at in range(0, out.shape[1], WIDE):
        columns = pl.ds(at, WIDE)
        part = partial_sums(first, half, sides, hiddens, weight, columns)
        for total in totals:
            part += total[:, columns]
        out[:, columns] = part


def last_down_kernel(first, half, sides, weight, hidden, total, own, *sends):
    rows, columns = own.shape[0] // 2, own.shape[1]
    for at in range(0, columns, WIDE):
        parts = []
        for start in (at, columns + at):
            part = partial_sums(first, half, sides, [hidden], weight, pl.ds(start, WIDE))
            parts.append(part + total[:, pl.ds(start, WIDE)])
        for place, out in enumerate((own, *sends)):
            pieces = [part[place * rows : (place + 1) * rows] for part in parts]
            out[:, pl.ds(at, WIDE)] = jnp.concatenate(pieces, axis=0).astype(out.dtype)


def down(weight, chunk, sides, hiddens, total=None, last=False):
    rows, half = hiddens[0].shape
    features = weight.shape[1]
    if last:
        packed = (rows // 2, features // 2)
        out_shape = (jax.ShapeDtypeStruct(packed, F32),) + (jax.ShapeDtypeStruct(packed, BF16),) * 3
        kernel = last_down_kernel
    else:
        out_shape = jax.ShapeDtypeStruct((rows, features), F32)
        kernel = down_kernel
    operands = [held_in(weight), *hiddens] + ([] if total is None else [total])
    return pl.pallas_call(
        functools.partial(kernel, chunk[0], half, sides),
        out_shape=out_shape,
        in_specs=[VMEM] * len(operands),
        out_specs=(VMEM,) * 4 if last else VMEM,
        compiler_params=GRANT,
        cost_estimate=pl.CostEstimate(
            flops=2 * rows * features * half * len(sides),
            bytes_accessed=2 * features * half * len(sides),
            transcendentals=0,
        ),
        name="down",
    )(*operands)


def split(units):
    more = units // 512 * 8 // 13 * 512
    return (0, more), (more, units - more)


def across(x, apart):
    return lax.ppermute(x, "wide", [(i, i ^ apart) for i in range(4)])


def chunked(tokens, gate_weight, up_weight, down_weight):
    rows = tokens.shape[0]
    chunks = split(gate_weight.shape[1])
    section = tokens
    for apart in (3, 2, 1):
        section = lax.optimization_barrier(jnp.concatenate([section, across(tokens, apart)], axis=0))
    def core_sums(send, keep):
        total = keep + swap(send, "sub").astype(F32)
        return total, total.astype(BF16)

    def hidden_half(total, received):
        return activate(*jnp.split(total + received.astype(F32), 2, axis=1))

    ready = beside(gate_weight)
    send, keep = sums(section, gate_weight, up_weight, chunks[0], ready)
    total, sent = core_sums(send, keep)
    later, _ = lax.optimization_barrier((section, sent))
    send, keep = stream_sums(later, gate_weight, up_weight, chunks[1])
    received, keep = lax.optimization_barrier((swap(sent, "narrow"), keep))
    mine = hidden_half(total, received)
    total, sent = core_sums(send, keep)
    mixed = down(down_weight, chunks[0], (0, 1), (mine, swap(mine, "sub")))
    received, mixed = lax.optimization_barrier((swap(sent, "narrow"), mixed))
    mine = hidden_half(total, received)
    mixed = down(down_weight, chunks[1], (0,), (mine,), mixed)
    out, *blocks = down(down_weight, chunks[1], (1,), (swap(mine, "sub"),), mixed, last=True)
    for block, apart in zip(blocks, (3, 2, 1)):
        out = lax.optimization_barrier(out + across(block, apart).astype(F32))
    return out.astype(BF16).reshape(2, rows, -1).swapaxes(0, 1).reshape(rows, -1)


def solution(mesh):
    placed = (
        P(("groups", "wide"), ("narrow", "sub")),
        P(("narrow", "sub"), "wide"),
        P(("narrow", "sub"), "wide"),
        P("wide", ("narrow", "sub")),
    )
    sizes = tuple(mesh.shape[axis] for axis in ("groups", "wide", "narrow", "sub"))
    return jax.shard_map(
        chunked if sizes == (2, 4, 2, 2) else general,
        mesh=mesh,
        in_specs=placed,
        out_specs=P(("groups", "wide"), ("narrow", "sub")),
        check_vma=False,
    )
```

```python
import functools

import jax
import jax.numpy as jnp
from jax import lax
from jax.experimental import pallas as pl
from jax.experimental.pallas import tpu as pltpu
from jax.sharding import PartitionSpec as P

BF16 = jnp.bfloat16
F32 = jnp.float32


def activate(gate_sums, up_sums):
    return (jax.nn.silu(gate_sums) * up_sums).astype(BF16)


def general(tokens, gate_weight, up_weight, down_weight):
    section = lax.all_gather(tokens, "wide", axis=0, tiled=True)
    gate_part = jnp.dot(section, gate_weight, preferred_element_type=F32)
    up_part = jnp.dot(section, up_weight, preferred_element_type=F32)
    gate_sums = lax.psum(gate_part, ("narrow", "sub"))
    up_sums = lax.psum(up_part, ("narrow", "sub"))
    mixed = lax.psum_scatter(
        jnp.dot(activate(gate_sums, up_sums), down_weight, preferred_element_type=F32),
        "wide",
        scatter_dimension=0,
        tiled=True,
    )
    return mixed.astype(BF16)


def swap(x, axis):
    return lax.ppermute(x, axis, [(0, 1), (1, 0)])


BLOCK = 256
WIDE = 512
VMEM = pl.BlockSpec(memory_space=pltpu.VMEM)
ANY = pl.BlockSpec(memory_space=pl.ANY)
HBM = pl.BlockSpec(memory_space=pltpu.HBM)
GRANT = pltpu.CompilerParams(vmem_limit_bytes=6 * 2**20)


def held_in(x):
    return pltpu.with_memory_space_constraint(x, pltpu.VMEM)


def left_in_hbm(x):
    return pltpu.with_memory_space_constraint(x, pltpu.HBM)


def beside_kernel(*refs):
    refs[-1][...] = jnp.zeros_like(refs[-1])


def beside(weight, *operands):
    operands = [left_in_hbm(weight), *operands]
    return pl.pallas_call(
        beside_kernel,
        out_shape=jax.ShapeDtypeStruct((8, 128), F32),
        in_specs=[HBM] + [ANY] * (len(operands) - 1),
        out_specs=VMEM,
        compiler_params=GRANT,
        cost_estimate=pl.CostEstimate(flops=0, bytes_accessed=2 * weight.size, transcendentals=0),
        name="beside",
    )(*operands)


def sums_kernel(first, tokens, gate, up, after, send, keep, held, sems):
    half = send.shape[1] // 2
    core = lax.axis_index("sub")

    def side_of(place):
        return first + jnp.where(core == place, 1, 0) * half

    copies = [
        [
            pltpu.make_async_copy(
                up.at[:, pl.ds(pl.multiple_of(side_of(place) + at, BLOCK), BLOCK)],
                held.at[:, pl.ds(place * half + at, BLOCK)],
                sems.at[place * (half // BLOCK) + at // BLOCK],
            )
            for at in range(0, half, BLOCK)
        ]
        for place in range(2)
    ]
    for copy in copies[0] + copies[1]:
        copy.start()

    pieces = [
        (place, out, at, min(WIDE, half - at))
        for place, out in enumerate((send, keep))
        for at in range(0, half, WIDE)
    ]
    for place, out, at, wide in pieces:
        columns = pl.ds(pl.multiple_of(side_of(place) + at, BLOCK), wide)
        out[:, pl.ds(at, wide)] = jnp.dot(tokens[...], gate[:, columns], preferred_element_type=F32).astype(
            out.dtype
        )
    for place, out, at, wide in pieces:
        for copy in copies[place][at // BLOCK : (at + wide) // BLOCK]:
            copy.wait()
        out[:, pl.ds(half + at, wide)] = jnp.dot(
            tokens[...], held[:, pl.ds(place * half + at, wide)], preferred_element_type=F32
        ).astype(out.dtype)


def sums(tokens, gate, up, chunk, after):
    rows, depth = tokens.shape
    first, width = chunk
    return pl.pallas_call(
        functools.partial(sums_kernel, first),
        out_shape=(jax.ShapeDtypeStruct((rows, width), BF16), jax.ShapeDtypeStruct((rows, width), F32)),
        in_specs=[VMEM, VMEM, HBM, ANY],
        out_specs=(VMEM, VMEM),
        scratch_shapes=[pltpu.VMEM((depth, width), BF16), pltpu.SemaphoreType.DMA((width // BLOCK,))],
        compiler_params=pltpu.CompilerParams(vmem_limit_bytes=2 * depth * width + 2 * 2**20),
        cost_estimate=pl.CostEstimate(
            flops=4 * rows * depth * width, bytes_accessed=4 * depth * width, transcendentals=0
        ),
        name="sums",
    )(tokens, held_in(gate), left_in_hbm(up), after)


def block_copies(first, half, step, gate, up, dst, sem):
    core = lax.axis_index("sub")
    mine = jnp.int32(step >= half // BLOCK)
    side = jnp.where(mine == 1, core, 1 - core)
    unit = first + side * half + (step - mine * (half // BLOCK)) * BLOCK
    columns = pl.ds(pl.multiple_of(unit, BLOCK), BLOCK)
    return [
        pltpu.make_async_copy(weight.at[:, columns], dst.at[:, pl.ds(i * BLOCK, BLOCK)], sem.at[i])
        for i, weight in enumerate((gate, up))
    ]


def pair(ref, at):
    return ref.at[:, pl.ds(pl.multiple_of(at * 2 * BLOCK, 2 * BLOCK), 2 * BLOCK)]


def stream_kernel(first, steps, tokens, gate, up, *refs):
    send, keep, streamed, sems = refs[-4:]
    held = refs[0] if steps else None
    half = send.shape[1] // 2
    blocks = half // BLOCK

    def copies(step):
        at = step - steps
        return block_copies(first, half, step, gate, up, pair(streamed, at), sems.at[at])

    for step in range(steps, 2 * blocks):
        for copy in copies(step):
            copy.start()

    def add(out, start, source, block):
        both = jnp.dot(tokens[...], source[...], preferred_element_type=F32).astype(out.dtype)
        for i in range(2):
            column = pl.multiple_of((i * blocks + block - start) * BLOCK, BLOCK)
            out[:, pl.ds(column, BLOCK)] = both[:, i * BLOCK : (i + 1) * BLOCK]

    for side, out in enumerate((send, keep)):
        start, end = side * blocks, (side + 1) * blocks

        middle = min(max(steps, start), end)
        if start < middle:

            @pl.loop(start, middle)
            def _(step):
                add(out, start, pair(held, step), step)

        if middle < end:

            @pl.loop(middle, end)
            def _(step):
                for copy in copies(step):
                    copy.wait()
                add(out, start, pair(streamed, step - steps), step)


def stream_sums(tokens, gate, up, chunk, held=None):
    rows, depth = tokens.shape
    first, width = chunk
    steps = 0 if held is None else held.shape[1] // (2 * BLOCK)
    streamed = width // BLOCK - steps
    return pl.pallas_call(
        functools.partial(stream_kernel, first, steps),
        out_shape=(jax.ShapeDtypeStruct((rows, width), BF16), jax.ShapeDtypeStruct((rows, width), F32)),
        in_specs=[VMEM, HBM, HBM] + [VMEM] * (steps > 0),
        out_specs=(VMEM, VMEM),
        scratch_shapes=[
            pltpu.VMEM((depth, streamed * 2 * BLOCK), BF16),
            pltpu.SemaphoreType.DMA((streamed, 2)),
        ],
        compiler_params=pltpu.CompilerParams(vmem_limit_bytes=4 * streamed * depth * BLOCK + 4 * 2**20),
        cost_estimate=pl.CostEstimate(
            flops=4 * rows * depth * width, bytes_accessed=4 * depth * width, transcendentals=0
        ),
        name="stream_sums",
    )(tokens, left_in_hbm(gate), left_in_hbm(up), *([held_in(held)] if steps else []))


def partial_sums(first, half, sides, hiddens, weight, columns):
    core = lax.axis_index("sub")
    part = 0.0
    for side, hidden in zip(sides, hiddens):
        start = pl.multiple_of(first + jnp.where(core == side, 0, half), BLOCK)
        part += jnp.dot(hidden[...], weight[pl.ds(start, half), columns], preferred_element_type=F32)
    return part


def down_kernel(first, half, sides, weight, *refs):
    hiddens, out = refs[: len(sides)], refs[-1]
    totals = refs[len(sides) : -1]
    for at in range(0, out.shape[1], WIDE):
        columns = pl.ds(at, WIDE)
        part = partial_sums(first, half, sides, hiddens, weight, columns)
        for total in totals:
            part += total[:, columns]
        out[:, columns] = part


def last_down_kernel(first, half, sides, weight, hidden, total, own, *sends):
    rows, columns = own.shape[0] // 2, own.shape[1]
    for at in range(0, columns, WIDE):
        parts = []
        for start in (at, columns + at):
            part = partial_sums(first, half, sides, [hidden], weight, pl.ds(start, WIDE))
            parts.append(part + total[:, pl.ds(start, WIDE)])
        for place, out in enumerate((own, *sends)):
            pieces = [part[place * rows : (place + 1) * rows] for part in parts]
            out[:, pl.ds(at, WIDE)] = jnp.concatenate(pieces, axis=0).astype(out.dtype)


def down(weight, chunk, sides, hiddens, total=None, last=False):
    rows, half = hiddens[0].shape
    features = weight.shape[1]
    if last:
        packed = (rows // 2, features // 2)
        out_shape = (jax.ShapeDtypeStruct(packed, F32),) + (jax.ShapeDtypeStruct(packed, BF16),) * 3
        kernel = last_down_kernel
    else:
        out_shape = jax.ShapeDtypeStruct((rows, features), F32)
        kernel = down_kernel
    operands = [held_in(weight), *hiddens] + ([] if total is None else [total])
    return pl.pallas_call(
        functools.partial(kernel, chunk[0], half, sides),
        out_shape=out_shape,
        in_specs=[VMEM] * len(operands),
        out_specs=(VMEM,) * 4 if last else VMEM,
        compiler_params=GRANT,
        cost_estimate=pl.CostEstimate(
            flops=2 * rows * features * half * len(sides),
            bytes_accessed=2 * features * half * len(sides),
            transcendentals=0,
        ),
        name="down",
    )(*operands)


def split(units):
    more = units // 512 * 8 // 13 * 512
    return (0, more), (more, units - more)


def across(x, apart):
    return lax.ppermute(x, "wide", [(i, i ^ apart) for i in range(4)])


def chunked(tokens, gate_weight, up_weight, down_weight):
    rows = tokens.shape[0]
    chunks = split(gate_weight.shape[1])
    section = tokens
    for apart in (3, 2, 1):
        section = lax.optimization_barrier(jnp.concatenate([section, across(tokens, apart)], axis=0))
    def core_sums(send, keep):
        total = keep + swap(send, "sub").astype(F32)
        return total, total.astype(BF16)

    def hidden_half(total, received):
        return activate(*jnp.split(total + received.astype(F32), 2, axis=1))

    ready = beside(gate_weight)
    send, keep = sums(section, gate_weight, up_weight, chunks[0], ready)
    total, sent = core_sums(send, keep)
    later, _ = lax.optimization_barrier((section, sent))
    send, keep = stream_sums(later, gate_weight, up_weight, chunks[1])
    received, keep = lax.optimization_barrier((swap(sent, "narrow"), keep))
    mine = hidden_half(total, received)
    total, sent = core_sums(send, keep)
    mixed = down(down_weight, chunks[0], (0, 1), (mine, swap(mine, "sub")))
    received, mixed = lax.optimization_barrier((swap(sent, "narrow"), mixed))
    mine = hidden_half(total, received)
    mixed = down(down_weight, chunks[1], (0,), (mine,), mixed)
    out, *blocks = down(down_weight, chunks[1], (1,), (swap(mine, "sub"),), mixed, last=True)
    for block, apart in zip(blocks, (3, 2, 1)):
        out = lax.optimization_barrier(out + across(block, apart).astype(F32))
    return out.astype(BF16).reshape(2, rows, -1).swapaxes(0, 1).reshape(rows, -1)


def solution(mesh):
    placed = (
        P(("groups", "wide"), ("narrow", "sub")),
        P(("narrow", "sub"), "wide"),
        P(("narrow", "sub"), "wide"),
        P("wide", ("narrow", "sub")),
    )
    sizes = tuple(mesh.shape[axis] for axis in ("groups", "wide", "narrow", "sub"))
    return jax.shard_map(
        chunked if sizes == (2, 4, 2, 2) else general,
        mesh=mesh,
        in_specs=placed,
        out_specs=P(("groups", "wide"), ("narrow", "sub")),
        check_vma=False,
    )
```

```python
import functools

import jax
import jax.numpy as jnp
from jax import lax
from jax.experimental import pallas as pl
from jax.experimental.pallas import tpu as pltpu
from jax.sharding import PartitionSpec as P

BF16 = jnp.bfloat16
F32 = jnp.float32


def activate(gate_sums, up_sums):
    return (jax.nn.silu(gate_sums) * up_sums).astype(BF16)


def general(tokens, gate_weight, up_weight, down_weight):
    section = lax.all_gather(tokens, "wide", axis=0, tiled=True)
    gate_part = jnp.dot(section, gate_weight, preferred_element_type=F32)
    up_part = jnp.dot(section, up_weight, preferred_element_type=F32)
    gate_sums = lax.psum(gate_part, ("narrow", "sub"))
    up_sums = lax.psum(up_part, ("narrow", "sub"))
    mixed = lax.psum_scatter(
        jnp.dot(activate(gate_sums, up_sums), down_weight, preferred_element_type=F32),
        "wide",
        scatter_dimension=0,
        tiled=True,
    )
    return mixed.astype(BF16)


def swap(x, axis):
    return lax.ppermute(x, axis, [(0, 1), (1, 0)])


BLOCK = 256
WIDE = 512
HELD = 8
VMEM = pl.BlockSpec(memory_space=pltpu.VMEM)
ANY = pl.BlockSpec(memory_space=pl.ANY)
HBM = pl.BlockSpec(memory_space=pltpu.HBM)
GRANT = pltpu.CompilerParams(vmem_limit_bytes=6 * 2**20)


def held_in(x):
    return pltpu.with_memory_space_constraint(x, pltpu.VMEM)


def left_in_hbm(x):
    return pltpu.with_memory_space_constraint(x, pltpu.HBM)


def block_copies(first, half, step, gate, up, dst, sem):
    core = lax.axis_index("sub")
    mine, block = divmod(step, half // BLOCK)
    side = core if mine else 1 - core
    unit = first + side * half + block * BLOCK
    columns = pl.ds(pl.multiple_of(unit, BLOCK), BLOCK)
    return [
        pltpu.make_async_copy(weight.at[:, columns], dst.at[i], sem.at[i]) for i, weight in enumerate((gate, up))
    ]


def load_kernel(first, half, gate, up, held, sems):
    copies = [
        copy
        for step in range(held.shape[0])
        for copy in block_copies(first, half, step, gate, up, held.at[step], sems.at[step])
    ]
    for copy in copies:
        copy.start()
    for copy in copies:
        copy.wait()


def load(gate, up, chunk, steps):
    depth = gate.shape[0]
    return pl.pallas_call(
        functools.partial(load_kernel, chunk[0], chunk[1] // 2),
        out_shape=pltpu.VMEM((steps, 2, depth, BLOCK), BF16),
        in_specs=[HBM, HBM],
        out_specs=VMEM,
        scratch_shapes=[pltpu.SemaphoreType.DMA((steps, 2))],
        compiler_params=GRANT,
        cost_estimate=pl.CostEstimate(
            flops=0, bytes_accessed=4 * steps * depth * BLOCK, transcendentals=0
        ),
        name="load",
    )(left_in_hbm(gate), left_in_hbm(up))


def sums_kernel(first, steps, tokens, gate, up, *refs):
    send, keep, streamed, sems = refs[-4:]
    held = refs[0] if steps else None
    half = send.shape[1] // 2
    blocks = half // BLOCK

    def copies(step):
        at = step - steps
        return block_copies(first, half, step, gate, up, streamed.at[at], sems.at[at])

    for step in range(steps, 2 * blocks):
        for copy in copies(step):
            copy.start()

    for step in range(2 * blocks):
        out, block = (send, step) if step < blocks else (keep, step - blocks)
        source = held.at[step] if step < steps else streamed.at[step - steps]
        if step >= steps:
            for copy in copies(step):
                copy.wait()
        for i in range(2):
            out[:, pl.ds((i * blocks + block) * BLOCK, BLOCK)] = jnp.dot(
                tokens[...], source[i], preferred_element_type=F32
            ).astype(out.dtype)


def sums(tokens, gate, up, chunk, held=None):
    rows, depth = tokens.shape
    first, width = chunk
    steps = 0 if held is None else held.shape[0]
    shape = (width // BLOCK - steps, 2, depth, BLOCK)
    return pl.pallas_call(
        functools.partial(sums_kernel, first, steps),
        out_shape=(jax.ShapeDtypeStruct((rows, width), BF16), jax.ShapeDtypeStruct((rows, width), F32)),
        in_specs=[VMEM, HBM, HBM] + [VMEM] * (steps > 0),
        out_specs=(VMEM, VMEM),
        scratch_shapes=[pltpu.VMEM(shape, BF16), pltpu.SemaphoreType.DMA(shape[:2])],
        compiler_params=pltpu.CompilerParams(vmem_limit_bytes=4 * shape[0] * depth * BLOCK + 4 * 2**20),
        cost_estimate=pl.CostEstimate(
            flops=4 * rows * depth * width, bytes_accessed=4 * depth * width, transcendentals=0
        ),
        name="sums",
    )(tokens, left_in_hbm(gate), left_in_hbm(up), *([held_in(held)] if steps else []))


def partial_sums(first, half, sides, hiddens, weight, columns):
    core = lax.axis_index("sub")
    part = 0.0
    for side, hidden in zip(sides, hiddens):
        start = pl.multiple_of(first + jnp.where(core == side, 0, half), BLOCK)
        part += jnp.dot(hidden[...], weight[pl.ds(start, half), columns], preferred_element_type=F32)
    return part


def down_kernel(first, half, sides, weight, *refs):
    hiddens, out = refs[: len(sides)], refs[-1]
    totals = refs[len(sides) : -1]
    for at in range(0, out.shape[1], WIDE):
        columns = pl.ds(at, WIDE)
        part = partial_sums(first, half, sides, hiddens, weight, columns)
        for total in totals:
            part += total[:, columns]
        out[:, columns] = part


def last_down_kernel(first, half, sides, weight, hidden, total, own, *sends):
    rows, columns = own.shape[0] // 2, own.shape[1]
    for at in range(0, columns, WIDE):
        parts = []
        for start in (at, columns + at):
            part = partial_sums(first, half, sides, [hidden], weight, pl.ds(start, WIDE))
            parts.append(part + total[:, pl.ds(start, WIDE)])
        for place, out in enumerate((own, *sends)):
            pieces = [part[place * rows : (place + 1) * rows] for part in parts]
            out[:, pl.ds(at, WIDE)] = jnp.concatenate(pieces, axis=0).astype(out.dtype)


def down(weight, chunk, sides, hiddens, total=None, last=False):
    rows, half = hiddens[0].shape
    features = weight.shape[1]
    if last:
        packed = (rows // 2, features // 2)
        out_shape = (jax.ShapeDtypeStruct(packed, F32),) + (jax.ShapeDtypeStruct(packed, BF16),) * 3
        kernel = last_down_kernel
    else:
        out_shape = jax.ShapeDtypeStruct((rows, features), F32)
        kernel = down_kernel
    operands = [held_in(weight), *hiddens] + ([] if total is None else [total])
    return pl.pallas_call(
        functools.partial(kernel, chunk[0], half, sides),
        out_shape=out_shape,
        in_specs=[VMEM] * len(operands),
        out_specs=(VMEM,) * 4 if last else VMEM,
        compiler_params=GRANT,
        cost_estimate=pl.CostEstimate(
            flops=2 * rows * features * half * len(sides),
            bytes_accessed=2 * features * half * len(sides),
            transcendentals=0,
        ),
        name="down",
    )(*operands)


def split(units):
    more = units // 512 * 8 // 13 * 512
    return (0, more), (more, units - more)


def across(x, apart):
    return lax.ppermute(x, "wide", [(i, i ^ apart) for i in range(4)])


def chunked(tokens, gate_weight, up_weight, down_weight):
    rows = tokens.shape[0]
    chunks = split(gate_weight.shape[1])
    section = tokens
    for apart in (3, 2, 1):
        section = lax.optimization_barrier(jnp.concatenate([section, across(tokens, apart)], axis=0))
    held = load(gate_weight, up_weight, chunks[0], HELD)

    def core_sums(send, keep):
        total = keep + swap(send, "sub").astype(F32)
        return total, total.astype(BF16)

    def hidden_half(total, received):
        return activate(*jnp.split(total + received.astype(F32), 2, axis=1))

    send, keep = sums(section, gate_weight, up_weight, chunks[0], held)
    total, sent = core_sums(send, keep)
    later, _ = lax.optimization_barrier((section, sent))
    send, keep = sums(later, gate_weight, up_weight, chunks[1])
    received, keep = lax.optimization_barrier((swap(sent, "narrow"), keep))
    mine = hidden_half(total, received)
    total, sent = core_sums(send, keep)
    mixed = down(down_weight, chunks[0], (0, 1), (mine, swap(mine, "sub")))
    received, mixed = lax.optimization_barrier((swap(sent, "narrow"), mixed))
    mine = hidden_half(total, received)
    mixed = down(down_weight, chunks[1], (0,), (mine,), mixed)
    out, *blocks = down(down_weight, chunks[1], (1,), (swap(mine, "sub"),), mixed, last=True)
    for block, apart in zip(blocks, (3, 2, 1)):
        out = lax.optimization_barrier(out + across(block, apart).astype(F32))
    return out.astype(BF16).reshape(2, rows, -1).swapaxes(0, 1).reshape(rows, -1)


def solution(mesh):
    placed = (
        P(("groups", "wide"), ("narrow", "sub")),
        P(("narrow", "sub"), "wide"),
        P(("narrow", "sub"), "wide"),
        P("wide", ("narrow", "sub")),
    )
    sizes = tuple(mesh.shape[axis] for axis in ("groups", "wide", "narrow", "sub"))
    return jax.shard_map(
        chunked if sizes == (2, 4, 2, 2) else general,
        mesh=mesh,
        in_specs=placed,
        out_specs=P(("groups", "wide"), ("narrow", "sub")),
        check_vma=False,
    )
```

```python
import functools

import jax
import jax.numpy as jnp
from jax import lax
from jax.experimental import pallas as pl
from jax.experimental.pallas import tpu as pltpu
from jax.sharding import PartitionSpec as P

BF16 = jnp.bfloat16
F32 = jnp.float32


def activate(gate_sums, up_sums):
    return (jax.nn.silu(gate_sums) * up_sums).astype(BF16)


def general(tokens, gate_weight, up_weight, down_weight):
    section = lax.all_gather(tokens, "wide", axis=0, tiled=True)
    gate_part = jnp.dot(section, gate_weight, preferred_element_type=F32)
    up_part = jnp.dot(section, up_weight, preferred_element_type=F32)
    gate_sums = lax.psum(gate_part, ("narrow", "sub"))
    up_sums = lax.psum(up_part, ("narrow", "sub"))
    mixed = lax.psum_scatter(
        jnp.dot(activate(gate_sums, up_sums), down_weight, preferred_element_type=F32),
        "wide",
        scatter_dimension=0,
        tiled=True,
    )
    return mixed.astype(BF16)


def swap(x, axis):
    return lax.ppermute(x, axis, [(0, 1), (1, 0)])


BLOCK = 256
WIDE = 512
VMEM = pl.BlockSpec(memory_space=pltpu.VMEM)
ANY = pl.BlockSpec(memory_space=pl.ANY)
HBM = pl.BlockSpec(memory_space=pltpu.HBM)
GRANT = pltpu.CompilerParams(vmem_limit_bytes=6 * 2**20)


def held_in(x):
    return pltpu.with_memory_space_constraint(x, pltpu.VMEM)


def left_in_hbm(x):
    return pltpu.with_memory_space_constraint(x, pltpu.HBM)


def beside_kernel(*refs):
    refs[-1][...] = jnp.zeros_like(refs[-1])


def beside(weight, *operands):
    operands = [left_in_hbm(weight), *operands]
    return pl.pallas_call(
        beside_kernel,
        out_shape=jax.ShapeDtypeStruct((8, 128), F32),
        in_specs=[HBM] + [ANY] * (len(operands) - 1),
        out_specs=VMEM,
        compiler_params=GRANT,
        cost_estimate=pl.CostEstimate(flops=0, bytes_accessed=2 * weight.size, transcendentals=0),
        name="beside",
    )(*operands)


def sums_kernel(first, tokens, gate, up, after, send, keep, held, sems):
    half = send.shape[1] // 2
    core = lax.axis_index("sub")

    def side_of(place):
        return first + jnp.where(core == place, 1, 0) * half

    def copy(place, block):
        at = pl.multiple_of(block * BLOCK, BLOCK)
        return pltpu.make_async_copy(
            up.at[:, pl.ds(pl.multiple_of(side_of(place) + at, BLOCK), BLOCK)],
            held.at[:, pl.ds(pl.multiple_of(place * half + at, BLOCK), BLOCK)],
            sems.at[place * (half // BLOCK) + block],
        )

    for place in range(2):
        for block in range(half // BLOCK):
            copy(place, block).start()

    for place, out in enumerate((send, keep)):

        def steps(body):
            pl.loop(0, half // WIDE)(lambda step: body(pl.multiple_of(step * WIDE, WIDE), WIDE))
            if half % WIDE:
                body(half - half % WIDE, half % WIDE)

        def gate_sums(at, wide):
            columns = pl.ds(pl.multiple_of(side_of(place) + at, BLOCK), wide)
            out[:, pl.ds(at, wide)] = jnp.dot(
                tokens[...], gate[:, columns], preferred_element_type=F32
            ).astype(out.dtype)

        def up_sums(at, wide):
            for block in range(wide // BLOCK):
                copy(place, at // BLOCK + block).wait()
            out[:, pl.ds(half + at, wide)] = jnp.dot(
                tokens[...], held[:, pl.ds(place * half + at, wide)], preferred_element_type=F32
            ).astype(out.dtype)

        steps(gate_sums)
        steps(up_sums)


def sums(tokens, gate, up, chunk, after):
    rows, depth = tokens.shape
    first, width = chunk
    return pl.pallas_call(
        functools.partial(sums_kernel, first),
        out_shape=(jax.ShapeDtypeStruct((rows, width), BF16), jax.ShapeDtypeStruct((rows, width), F32)),
        in_specs=[VMEM, VMEM, HBM, ANY],
        out_specs=(VMEM, VMEM),
        scratch_shapes=[pltpu.VMEM((depth, width), BF16), pltpu.SemaphoreType.DMA((width // BLOCK,))],
        compiler_params=pltpu.CompilerParams(vmem_limit_bytes=2 * depth * width + 2 * 2**20),
        cost_estimate=pl.CostEstimate(
            flops=4 * rows * depth * width, bytes_accessed=4 * depth * width, transcendentals=0
        ),
        name="sums",
    )(tokens, held_in(gate), left_in_hbm(up), after)


def block_copies(first, half, step, gate, up, dst, sem):
    core = lax.axis_index("sub")
    mine = jnp.int32(step >= half // BLOCK)
    side = jnp.where(mine == 1, core, 1 - core)
    unit = first + side * half + (step - mine * (half // BLOCK)) * BLOCK
    columns = pl.ds(pl.multiple_of(unit, BLOCK), BLOCK)
    return [
        pltpu.make_async_copy(weight.at[:, columns], dst.at[:, pl.ds(i * BLOCK, BLOCK)], sem.at[i])
        for i, weight in enumerate((gate, up))
    ]


def pair(ref, at):
    return ref.at[:, pl.ds(pl.multiple_of(at * 2 * BLOCK, 2 * BLOCK), 2 * BLOCK)]


def stream_kernel(first, steps, tokens, gate, up, *refs):
    send, keep, streamed, sems = refs[-4:]
    held = refs[0] if steps else None
    half = send.shape[1] // 2
    blocks = half // BLOCK

    def copies(step):
        at = step - steps
        return block_copies(first, half, step, gate, up, pair(streamed, at), sems.at[at])

    for step in range(steps, 2 * blocks):
        for copy in copies(step):
            copy.start()

    def add(out, start, source, block):
        both = jnp.dot(tokens[...], source[...], preferred_element_type=F32).astype(out.dtype)
        for i in range(2):
            column = pl.multiple_of((i * blocks + block - start) * BLOCK, BLOCK)
            out[:, pl.ds(column, BLOCK)] = both[:, i * BLOCK : (i + 1) * BLOCK]

    for side, out in enumerate((send, keep)):
        start, end = side * blocks, (side + 1) * blocks

        middle = min(max(steps, start), end)
        if start < middle:

            @pl.loop(start, middle)
            def _(step):
                add(out, start, pair(held, step), step)

        if middle < end:

            @pl.loop(middle, end)
            def _(step):
                for copy in copies(step):
                    copy.wait()
                add(out, start, pair(streamed, step - steps), step)


def stream_sums(tokens, gate, up, chunk, held=None):
    rows, depth = tokens.shape
    first, width = chunk
    steps = 0 if held is None else held.shape[1] // (2 * BLOCK)
    streamed = width // BLOCK - steps
    return pl.pallas_call(
        functools.partial(stream_kernel, first, steps),
        out_shape=(jax.ShapeDtypeStruct((rows, width), BF16), jax.ShapeDtypeStruct((rows, width), F32)),
        in_specs=[VMEM, HBM, HBM] + [VMEM] * (steps > 0),
        out_specs=(VMEM, VMEM),
        scratch_shapes=[
            pltpu.VMEM((depth, streamed * 2 * BLOCK), BF16),
            pltpu.SemaphoreType.DMA((streamed, 2)),
        ],
        compiler_params=pltpu.CompilerParams(vmem_limit_bytes=4 * streamed * depth * BLOCK + 4 * 2**20),
        cost_estimate=pl.CostEstimate(
            flops=4 * rows * depth * width, bytes_accessed=4 * depth * width, transcendentals=0
        ),
        name="stream_sums",
    )(tokens, left_in_hbm(gate), left_in_hbm(up), *([held_in(held)] if steps else []))


def partial_sums(first, half, sides, hiddens, weight, columns):
    core = lax.axis_index("sub")
    part = 0.0
    for side, hidden in zip(sides, hiddens):
        start = pl.multiple_of(first + jnp.where(core == side, 0, half), BLOCK)
        part += jnp.dot(hidden[...], weight[pl.ds(start, half), columns], preferred_element_type=F32)
    return part


def down_kernel(first, half, sides, weight, *refs):
    hiddens, out = refs[: len(sides)], refs[-1]
    totals = refs[len(sides) : -1]
    for at in range(0, out.shape[1], WIDE):
        columns = pl.ds(at, WIDE)
        part = partial_sums(first, half, sides, hiddens, weight, columns)
        for total in totals:
            part += total[:, columns]
        out[:, columns] = part


def last_down_kernel(first, half, sides, weight, hidden, total, own, *sends):
    rows, columns = own.shape[0] // 2, own.shape[1]
    for at in range(0, columns, WIDE):
        parts = []
        for start in (at, columns + at):
            part = partial_sums(first, half, sides, [hidden], weight, pl.ds(start, WIDE))
            parts.append(part + total[:, pl.ds(start, WIDE)])
        for place, out in enumerate((own, *sends)):
            pieces = [part[place * rows : (place + 1) * rows] for part in parts]
            out[:, pl.ds(at, WIDE)] = jnp.concatenate(pieces, axis=0).astype(out.dtype)


def down(weight, chunk, sides, hiddens, total=None, last=False):
    rows, half = hiddens[0].shape
    features = weight.shape[1]
    if last:
        packed = (rows // 2, features // 2)
        out_shape = (jax.ShapeDtypeStruct(packed, F32),) + (jax.ShapeDtypeStruct(packed, BF16),) * 3
        kernel = last_down_kernel
    else:
        out_shape = jax.ShapeDtypeStruct((rows, features), F32)
        kernel = down_kernel
    operands = [held_in(weight), *hiddens] + ([] if total is None else [total])
    return pl.pallas_call(
        functools.partial(kernel, chunk[0], half, sides),
        out_shape=out_shape,
        in_specs=[VMEM] * len(operands),
        out_specs=(VMEM,) * 4 if last else VMEM,
        compiler_params=GRANT,
        cost_estimate=pl.CostEstimate(
            flops=2 * rows * features * half * len(sides),
            bytes_accessed=2 * features * half * len(sides),
            transcendentals=0,
        ),
        name="down",
    )(*operands)


def split(units):
    more = units // 512 * 8 // 13 * 512
    return (0, more), (more, units - more)


def across(x, apart):
    return lax.ppermute(x, "wide", [(i, i ^ apart) for i in range(4)])


def chunked(tokens, gate_weight, up_weight, down_weight):
    rows = tokens.shape[0]
    chunks = split(gate_weight.shape[1])
    section = tokens
    for apart in (3, 2, 1):
        section = lax.optimization_barrier(jnp.concatenate([section, across(tokens, apart)], axis=0))
    def core_sums(send, keep):
        total = keep + swap(send, "sub").astype(F32)
        return total, total.astype(BF16)

    def hidden_half(total, received):
        return activate(*jnp.split(total + received.astype(F32), 2, axis=1))

    ready = beside(gate_weight)
    send, keep = sums(section, gate_weight, up_weight, chunks[0], ready)
    total, sent = core_sums(send, keep)
    later, _ = lax.optimization_barrier((section, sent))
    send, keep = stream_sums(later, gate_weight, up_weight, chunks[1])
    received, keep = lax.optimization_barrier((swap(sent, "narrow"), keep))
    mine = hidden_half(total, received)
    total, sent = core_sums(send, keep)
    mixed = down(down_weight, chunks[0], (0, 1), (mine, swap(mine, "sub")))
    received, mixed = lax.optimization_barrier((swap(sent, "narrow"), mixed))
    mine = hidden_half(total, received)
    mixed = down(down_weight, chunks[1], (0,), (mine,), mixed)
    out, *blocks = down(down_weight, chunks[1], (1,), (swap(mine, "sub"),), mixed, last=True)
    for block, apart in zip(blocks, (3, 2, 1)):
        out = lax.optimization_barrier(out + across(block, apart).astype(F32))
    return out.astype(BF16).reshape(2, rows, -1).swapaxes(0, 1).reshape(rows, -1)


def solution(mesh):
    placed = (
        P(("groups", "wide"), ("narrow", "sub")),
        P(("narrow", "sub"), "wide"),
        P(("narrow", "sub"), "wide"),
        P("wide", ("narrow", "sub")),
    )
    sizes = tuple(mesh.shape[axis] for axis in ("groups", "wide", "narrow", "sub"))
    return jax.shard_map(
        chunked if sizes == (2, 4, 2, 2) else general,
        mesh=mesh,
        in_specs=placed,
        out_specs=P(("groups", "wide"), ("narrow", "sub")),
        check_vma=False,
    )
```

```python
import functools

import jax
import jax.numpy as jnp
from jax import lax
from jax.experimental import pallas as pl
from jax.experimental.pallas import tpu as pltpu
from jax.sharding import PartitionSpec as P

BF16 = jnp.bfloat16
F32 = jnp.float32


def activate(gate_sums, up_sums):
    return (jax.nn.silu(gate_sums) * up_sums).astype(BF16)


def general(tokens, gate_weight, up_weight, down_weight):
    section = lax.all_gather(tokens, "wide", axis=0, tiled=True)
    gate_part = jnp.dot(section, gate_weight, preferred_element_type=F32)
    up_part = jnp.dot(section, up_weight, preferred_element_type=F32)
    gate_sums = lax.psum(gate_part, ("narrow", "sub"))
    up_sums = lax.psum(up_part, ("narrow", "sub"))
    mixed = lax.psum_scatter(
        jnp.dot(activate(gate_sums, up_sums), down_weight, preferred_element_type=F32),
        "wide",
        scatter_dimension=0,
        tiled=True,
    )
    return mixed.astype(BF16)


def swap(x, axis):
    return lax.ppermute(x, axis, [(0, 1), (1, 0)])


BLOCK = 256
WIDE = 512
VMEM = pl.BlockSpec(memory_space=pltpu.VMEM)
ANY = pl.BlockSpec(memory_space=pl.ANY)
HBM = pl.BlockSpec(memory_space=pltpu.HBM)
GRANT = pltpu.CompilerParams(vmem_limit_bytes=6 * 2**20)


def held_in(x):
    return pltpu.with_memory_space_constraint(x, pltpu.VMEM)


def left_in_hbm(x):
    return pltpu.with_memory_space_constraint(x, pltpu.HBM)


def beside_kernel(*refs):
    refs[-1][...] = jnp.zeros_like(refs[-1])


def beside(weight, *operands):
    operands = [left_in_hbm(weight), *operands]
    return pl.pallas_call(
        beside_kernel,
        out_shape=jax.ShapeDtypeStruct((8, 128), F32),
        in_specs=[HBM] + [ANY] * (len(operands) - 1),
        out_specs=VMEM,
        compiler_params=GRANT,
        cost_estimate=pl.CostEstimate(flops=0, bytes_accessed=2 * weight.size, transcendentals=0),
        name="beside",
    )(*operands)


def half_sums_kernel(first, half, mine, tokens, gate, up, after, out, held, sems):
    core = lax.axis_index("sub")
    start = first + jnp.where(core == mine, 1, 0) * half

    def copy(block):
        at = pl.multiple_of(block * BLOCK, BLOCK)
        return pltpu.make_async_copy(
            up.at[:, pl.ds(pl.multiple_of(start + at, BLOCK), BLOCK)], held.at[:, pl.ds(at, BLOCK)], sems.at[block]
        )

    for block in range(half // BLOCK):
        copy(block).start()

    def steps(body):
        pl.loop(0, half // WIDE)(lambda step: body(pl.multiple_of(step * WIDE, WIDE), WIDE))
        if half % WIDE:
            body(half - half % WIDE, half % WIDE)

    def gate_sums(at, wide):
        columns = pl.ds(pl.multiple_of(start + at, BLOCK), wide)
        out[:, pl.ds(at, wide)] = jnp.dot(tokens[...], gate[:, columns], preferred_element_type=F32).astype(
            out.dtype
        )

    def up_sums(at, wide):
        for block in range(wide // BLOCK):
            copy(at // BLOCK + block).wait()
        out[:, pl.ds(half + at, wide)] = jnp.dot(
            tokens[...], held[:, pl.ds(at, wide)], preferred_element_type=F32
        ).astype(out.dtype)

    steps(gate_sums)
    steps(up_sums)


def half_sums(tokens, gate, up, chunk, mine, after):
    rows, depth = tokens.shape
    first, width = chunk
    half = width // 2
    return pl.pallas_call(
        functools.partial(half_sums_kernel, first, half, mine),
        out_shape=jax.ShapeDtypeStruct((rows, width), F32 if mine else BF16),
        in_specs=[VMEM, VMEM, HBM, ANY],
        out_specs=VMEM,
        scratch_shapes=[pltpu.VMEM((depth, half), BF16), pltpu.SemaphoreType.DMA((half // BLOCK,))],
        compiler_params=pltpu.CompilerParams(vmem_limit_bytes=2 * depth * half + 2 * 2**20),
        cost_estimate=pl.CostEstimate(
            flops=2 * rows * depth * width, bytes_accessed=2 * depth * width, transcendentals=0
        ),
        name="half_sums",
    )(tokens, held_in(gate), left_in_hbm(up), after)


def block_copies(first, half, step, gate, up, dst, sem):
    core = lax.axis_index("sub")
    mine = jnp.int32(step >= half // BLOCK)
    side = jnp.where(mine == 1, core, 1 - core)
    unit = first + side * half + (step - mine * (half // BLOCK)) * BLOCK
    columns = pl.ds(pl.multiple_of(unit, BLOCK), BLOCK)
    return [
        pltpu.make_async_copy(weight.at[:, columns], dst.at[:, pl.ds(i * BLOCK, BLOCK)], sem.at[i])
        for i, weight in enumerate((gate, up))
    ]


def pair(ref, at):
    return ref.at[:, pl.ds(pl.multiple_of(at * 2 * BLOCK, 2 * BLOCK), 2 * BLOCK)]


def stream_kernel(first, steps, tokens, gate, up, *refs):
    send, keep, streamed, sems = refs[-4:]
    held = refs[0] if steps else None
    half = send.shape[1] // 2
    blocks = half // BLOCK

    def copies(step):
        at = step - steps
        return block_copies(first, half, step, gate, up, pair(streamed, at), sems.at[at])

    for step in range(steps, 2 * blocks):
        for copy in copies(step):
            copy.start()

    def add(out, start, source, block):
        both = jnp.dot(tokens[...], source[...], preferred_element_type=F32).astype(out.dtype)
        for i in range(2):
            column = pl.multiple_of((i * blocks + block - start) * BLOCK, BLOCK)
            out[:, pl.ds(column, BLOCK)] = both[:, i * BLOCK : (i + 1) * BLOCK]

    for side, out in enumerate((send, keep)):
        start, end = side * blocks, (side + 1) * blocks

        middle = min(max(steps, start), end)
        if start < middle:

            @pl.loop(start, middle)
            def _(step):
                add(out, start, pair(held, step), step)

        if middle < end:

            @pl.loop(middle, end)
            def _(step):
                for copy in copies(step):
                    copy.wait()
                add(out, start, pair(streamed, step - steps), step)


def stream_sums(tokens, gate, up, chunk, held=None):
    rows, depth = tokens.shape
    first, width = chunk
    steps = 0 if held is None else held.shape[1] // (2 * BLOCK)
    streamed = width // BLOCK - steps
    return pl.pallas_call(
        functools.partial(stream_kernel, first, steps),
        out_shape=(jax.ShapeDtypeStruct((rows, width), BF16), jax.ShapeDtypeStruct((rows, width), F32)),
        in_specs=[VMEM, HBM, HBM] + [VMEM] * (steps > 0),
        out_specs=(VMEM, VMEM),
        scratch_shapes=[
            pltpu.VMEM((depth, streamed * 2 * BLOCK), BF16),
            pltpu.SemaphoreType.DMA((streamed, 2)),
        ],
        compiler_params=pltpu.CompilerParams(vmem_limit_bytes=4 * streamed * depth * BLOCK + 4 * 2**20),
        cost_estimate=pl.CostEstimate(
            flops=4 * rows * depth * width, bytes_accessed=4 * depth * width, transcendentals=0
        ),
        name="stream_sums",
    )(tokens, left_in_hbm(gate), left_in_hbm(up), *([held_in(held)] if steps else []))


def partial_sums(first, half, sides, hiddens, weight, columns):
    core = lax.axis_index("sub")
    part = 0.0
    for side, hidden in zip(sides, hiddens):
        start = pl.multiple_of(first + jnp.where(core == side, 0, half), BLOCK)
        part += jnp.dot(hidden[...], weight[pl.ds(start, half), columns], preferred_element_type=F32)
    return part


def down_kernel(first, half, sides, weight, *refs):
    hiddens, out = refs[: len(sides)], refs[-1]
    totals = refs[len(sides) : -1]
    for at in range(0, out.shape[1], WIDE):
        columns = pl.ds(at, WIDE)
        part = partial_sums(first, half, sides, hiddens, weight, columns)
        for total in totals:
            part += total[:, columns]
        out[:, columns] = part


def last_down_kernel(first, half, sides, weight, hidden, total, own, *sends):
    rows, columns = own.shape[0] // 2, own.shape[1]
    for at in range(0, columns, WIDE):
        parts = []
        for start in (at, columns + at):
            part = partial_sums(first, half, sides, [hidden], weight, pl.ds(start, WIDE))
            parts.append(part + total[:, pl.ds(start, WIDE)])
        for place, out in enumerate((own, *sends)):
            pieces = [part[place * rows : (place + 1) * rows] for part in parts]
            out[:, pl.ds(at, WIDE)] = jnp.concatenate(pieces, axis=0).astype(out.dtype)


def down(weight, chunk, sides, hiddens, total=None, last=False):
    rows, half = hiddens[0].shape
    features = weight.shape[1]
    if last:
        packed = (rows // 2, features // 2)
        out_shape = (jax.ShapeDtypeStruct(packed, F32),) + (jax.ShapeDtypeStruct(packed, BF16),) * 3
        kernel = last_down_kernel
    else:
        out_shape = jax.ShapeDtypeStruct((rows, features), F32)
        kernel = down_kernel
    operands = [held_in(weight), *hiddens] + ([] if total is None else [total])
    return pl.pallas_call(
        functools.partial(kernel, chunk[0], half, sides),
        out_shape=out_shape,
        in_specs=[VMEM] * len(operands),
        out_specs=(VMEM,) * 4 if last else VMEM,
        compiler_params=GRANT,
        cost_estimate=pl.CostEstimate(
            flops=2 * rows * features * half * len(sides),
            bytes_accessed=2 * features * half * len(sides),
            transcendentals=0,
        ),
        name="down",
    )(*operands)


def split(units):
    more = units // 512 * 8 // 13 * 512
    return (0, more), (more, units - more)


def across(x, apart):
    return lax.ppermute(x, "wide", [(i, i ^ apart) for i in range(4)])


def chunked(tokens, gate_weight, up_weight, down_weight):
    rows = tokens.shape[0]
    chunks = split(gate_weight.shape[1])
    section = tokens
    for apart in (3, 2, 1):
        section = lax.optimization_barrier(jnp.concatenate([section, across(tokens, apart)], axis=0))
    def core_sums(send, keep):
        total = keep + swap(send, "sub").astype(F32)
        return total, total.astype(BF16)

    def hidden_half(total, received):
        return activate(*jnp.split(total + received.astype(F32), 2, axis=1))

    ready = beside(gate_weight)
    send = half_sums(section, gate_weight, up_weight, chunks[0], 0, ready)
    keep = half_sums(section, gate_weight, up_weight, chunks[0], 1, send)
    total, sent = core_sums(send, keep)
    later, _ = lax.optimization_barrier((section, sent))
    send, keep = stream_sums(later, gate_weight, up_weight, chunks[1])
    received, keep = lax.optimization_barrier((swap(sent, "narrow"), keep))
    mine = hidden_half(total, received)
    total, sent = core_sums(send, keep)
    mixed = down(down_weight, chunks[0], (0, 1), (mine, swap(mine, "sub")))
    received, mixed = lax.optimization_barrier((swap(sent, "narrow"), mixed))
    mine = hidden_half(total, received)
    mixed = down(down_weight, chunks[1], (0,), (mine,), mixed)
    out, *blocks = down(down_weight, chunks[1], (1,), (swap(mine, "sub"),), mixed, last=True)
    for block, apart in zip(blocks, (3, 2, 1)):
        out = lax.optimization_barrier(out + across(block, apart).astype(F32))
    return out.astype(BF16).reshape(2, rows, -1).swapaxes(0, 1).reshape(rows, -1)


def solution(mesh):
    placed = (
        P(("groups", "wide"), ("narrow", "sub")),
        P(("narrow", "sub"), "wide"),
        P(("narrow", "sub"), "wide"),
        P("wide", ("narrow", "sub")),
    )
    sizes = tuple(mesh.shape[axis] for axis in ("groups", "wide", "narrow", "sub"))
    return jax.shard_map(
        chunked if sizes == (2, 4, 2, 2) else general,
        mesh=mesh,
        in_specs=placed,
        out_specs=P(("groups", "wide"), ("narrow", "sub")),
        check_vma=False,
    )
```

```python
import functools

import jax
import jax.numpy as jnp
from jax import lax
from jax.experimental import pallas as pl
from jax.experimental.pallas import tpu as pltpu
from jax.sharding import PartitionSpec as P

BF16 = jnp.bfloat16
F32 = jnp.float32


def activate(gate_sums, up_sums):
    return (jax.nn.silu(gate_sums) * up_sums).astype(BF16)


def general(tokens, gate_weight, up_weight, down_weight):
    section = lax.all_gather(tokens, "wide", axis=0, tiled=True)
    gate_part = jnp.dot(section, gate_weight, preferred_element_type=F32)
    up_part = jnp.dot(section, up_weight, preferred_element_type=F32)
    gate_sums = lax.psum(gate_part, ("narrow", "sub"))
    up_sums = lax.psum(up_part, ("narrow", "sub"))
    mixed = lax.psum_scatter(
        jnp.dot(activate(gate_sums, up_sums), down_weight, preferred_element_type=F32),
        "wide",
        scatter_dimension=0,
        tiled=True,
    )
    return mixed.astype(BF16)


def swap(x, axis):
    return lax.ppermute(x, axis, [(0, 1), (1, 0)])


BLOCK = 256
WIDE = 512
VMEM = pl.BlockSpec(memory_space=pltpu.VMEM)
ANY = pl.BlockSpec(memory_space=pl.ANY)
HBM = pl.BlockSpec(memory_space=pltpu.HBM)
GRANT = pltpu.CompilerParams(vmem_limit_bytes=6 * 2**20)


def held_in(x):
    return pltpu.with_memory_space_constraint(x, pltpu.VMEM)


def left_in_hbm(x):
    return pltpu.with_memory_space_constraint(x, pltpu.HBM)


def beside_kernel(*refs):
    refs[-1][...] = jnp.zeros_like(refs[-1])


def beside(weight, *operands):
    operands = [left_in_hbm(weight), *operands]
    return pl.pallas_call(
        beside_kernel,
        out_shape=jax.ShapeDtypeStruct((8, 128), F32),
        in_specs=[HBM] + [ANY] * (len(operands) - 1),
        out_specs=VMEM,
        compiler_params=GRANT,
        cost_estimate=pl.CostEstimate(flops=0, bytes_accessed=2 * weight.size, transcendentals=0),
        name="beside",
    )(*operands)


def half_sums_kernel(first, half, mine, tokens, gate, up, after, out, held, sems):
    core = lax.axis_index("sub")
    start = first + jnp.where(core == mine, 1, 0) * half

    def copy(block):
        at = pl.multiple_of(block * BLOCK, BLOCK)
        return pltpu.make_async_copy(
            up.at[:, pl.ds(pl.multiple_of(start + at, BLOCK), BLOCK)], held.at[:, pl.ds(at, BLOCK)], sems.at[block]
        )

    for block in range(half // BLOCK):
        copy(block).start()

    def steps(body):
        pl.loop(0, half // WIDE, unroll=2)(lambda step: body(pl.multiple_of(step * WIDE, WIDE), WIDE))
        if half % WIDE:
            body(half - half % WIDE, half % WIDE)

    def gate_sums(at, wide):
        columns = pl.ds(pl.multiple_of(start + at, BLOCK), wide)
        out[:, pl.ds(at, wide)] = jnp.dot(tokens[...], gate[:, columns], preferred_element_type=F32).astype(
            out.dtype
        )

    def up_sums(at, wide):
        for block in range(wide // BLOCK):
            copy(at // BLOCK + block).wait()
        out[:, pl.ds(half + at, wide)] = jnp.dot(
            tokens[...], held[:, pl.ds(at, wide)], preferred_element_type=F32
        ).astype(out.dtype)

    steps(gate_sums)
    steps(up_sums)


def half_sums(tokens, gate, up, chunk, mine, after):
    rows, depth = tokens.shape
    first, width = chunk
    half = width // 2
    return pl.pallas_call(
        functools.partial(half_sums_kernel, first, half, mine),
        out_shape=jax.ShapeDtypeStruct((rows, width), F32 if mine else BF16),
        in_specs=[VMEM, VMEM, HBM, ANY],
        out_specs=VMEM,
        scratch_shapes=[pltpu.VMEM((depth, half), BF16), pltpu.SemaphoreType.DMA((half // BLOCK,))],
        compiler_params=pltpu.CompilerParams(vmem_limit_bytes=2 * depth * half + 2 * 2**20),
        cost_estimate=pl.CostEstimate(
            flops=2 * rows * depth * width, bytes_accessed=2 * depth * width, transcendentals=0
        ),
        name="half_sums",
    )(tokens, held_in(gate), left_in_hbm(up), after)


def block_copies(first, half, step, gate, up, dst, sem):
    core = lax.axis_index("sub")
    mine = jnp.int32(step >= half // BLOCK)
    side = jnp.where(mine == 1, core, 1 - core)
    unit = first + side * half + (step - mine * (half // BLOCK)) * BLOCK
    columns = pl.ds(pl.multiple_of(unit, BLOCK), BLOCK)
    return [
        pltpu.make_async_copy(weight.at[:, columns], dst.at[:, pl.ds(i * BLOCK, BLOCK)], sem.at[i])
        for i, weight in enumerate((gate, up))
    ]


def pair(ref, at):
    return ref.at[:, pl.ds(pl.multiple_of(at * 2 * BLOCK, 2 * BLOCK), 2 * BLOCK)]


def stream_kernel(first, steps, tokens, gate, up, *refs):
    send, keep, streamed, sems = refs[-4:]
    held = refs[0] if steps else None
    half = send.shape[1] // 2
    blocks = half // BLOCK

    def copies(step):
        at = step - steps
        return block_copies(first, half, step, gate, up, pair(streamed, at), sems.at[at])

    for step in range(steps, 2 * blocks):
        for copy in copies(step):
            copy.start()

    def add(out, start, source, block):
        both = jnp.dot(tokens[...], source[...], preferred_element_type=F32).astype(out.dtype)
        for i in range(2):
            column = pl.multiple_of((i * blocks + block - start) * BLOCK, BLOCK)
            out[:, pl.ds(column, BLOCK)] = both[:, i * BLOCK : (i + 1) * BLOCK]

    for side, out in enumerate((send, keep)):
        start, end = side * blocks, (side + 1) * blocks

        middle = min(max(steps, start), end)
        if start < middle:

            @pl.loop(start, middle)
            def _(step):
                add(out, start, pair(held, step), step)

        if middle < end:

            @pl.loop(middle, end)
            def _(step):
                for copy in copies(step):
                    copy.wait()
                add(out, start, pair(streamed, step - steps), step)


def stream_sums(tokens, gate, up, chunk, held=None):
    rows, depth = tokens.shape
    first, width = chunk
    steps = 0 if held is None else held.shape[1] // (2 * BLOCK)
    streamed = width // BLOCK - steps
    return pl.pallas_call(
        functools.partial(stream_kernel, first, steps),
        out_shape=(jax.ShapeDtypeStruct((rows, width), BF16), jax.ShapeDtypeStruct((rows, width), F32)),
        in_specs=[VMEM, HBM, HBM] + [VMEM] * (steps > 0),
        out_specs=(VMEM, VMEM),
        scratch_shapes=[
            pltpu.VMEM((depth, streamed * 2 * BLOCK), BF16),
            pltpu.SemaphoreType.DMA((streamed, 2)),
        ],
        compiler_params=pltpu.CompilerParams(vmem_limit_bytes=4 * streamed * depth * BLOCK + 4 * 2**20),
        cost_estimate=pl.CostEstimate(
            flops=4 * rows * depth * width, bytes_accessed=4 * depth * width, transcendentals=0
        ),
        name="stream_sums",
    )(tokens, left_in_hbm(gate), left_in_hbm(up), *([held_in(held)] if steps else []))


def partial_sums(first, half, sides, hiddens, weight, columns):
    core = lax.axis_index("sub")
    part = 0.0
    for side, hidden in zip(sides, hiddens):
        start = pl.multiple_of(first + jnp.where(core == side, 0, half), BLOCK)
        part += jnp.dot(hidden[...], weight[pl.ds(start, half), columns], preferred_element_type=F32)
    return part


def down_kernel(first, half, sides, weight, *refs):
    hiddens, out = refs[: len(sides)], refs[-1]
    totals = refs[len(sides) : -1]
    for at in range(0, out.shape[1], WIDE):
        columns = pl.ds(at, WIDE)
        part = partial_sums(first, half, sides, hiddens, weight, columns)
        for total in totals:
            part += total[:, columns]
        out[:, columns] = part


def last_down_kernel(first, half, sides, weight, hidden, total, own, *sends):
    rows, columns = own.shape[0] // 2, own.shape[1]
    for at in range(0, columns, WIDE):
        parts = []
        for start in (at, columns + at):
            part = partial_sums(first, half, sides, [hidden], weight, pl.ds(start, WIDE))
            parts.append(part + total[:, pl.ds(start, WIDE)])
        for place, out in enumerate((own, *sends)):
            pieces = [part[place * rows : (place + 1) * rows] for part in parts]
            out[:, pl.ds(at, WIDE)] = jnp.concatenate(pieces, axis=0).astype(out.dtype)


def down(weight, chunk, sides, hiddens, total=None, last=False):
    rows, half = hiddens[0].shape
    features = weight.shape[1]
    if last:
        packed = (rows // 2, features // 2)
        out_shape = (jax.ShapeDtypeStruct(packed, F32),) + (jax.ShapeDtypeStruct(packed, BF16),) * 3
        kernel = last_down_kernel
    else:
        out_shape = jax.ShapeDtypeStruct((rows, features), F32)
        kernel = down_kernel
    operands = [held_in(weight), *hiddens] + ([] if total is None else [total])
    return pl.pallas_call(
        functools.partial(kernel, chunk[0], half, sides),
        out_shape=out_shape,
        in_specs=[VMEM] * len(operands),
        out_specs=(VMEM,) * 4 if last else VMEM,
        compiler_params=GRANT,
        cost_estimate=pl.CostEstimate(
            flops=2 * rows * features * half * len(sides),
            bytes_accessed=2 * features * half * len(sides),
            transcendentals=0,
        ),
        name="down",
    )(*operands)


def split(units):
    more = units // 512 * 8 // 13 * 512
    return (0, more), (more, units - more)


def across(x, apart):
    return lax.ppermute(x, "wide", [(i, i ^ apart) for i in range(4)])


def chunked(tokens, gate_weight, up_weight, down_weight):
    rows = tokens.shape[0]
    chunks = split(gate_weight.shape[1])
    section = tokens
    for apart in (3, 2, 1):
        section = lax.optimization_barrier(jnp.concatenate([section, across(tokens, apart)], axis=0))
    def core_sums(send, keep):
        total = keep + swap(send, "sub").astype(F32)
        return total, total.astype(BF16)

    def hidden_half(total, received):
        return activate(*jnp.split(total + received.astype(F32), 2, axis=1))

    ready = beside(gate_weight)
    send = half_sums(section, gate_weight, up_weight, chunks[0], 0, ready)
    keep = half_sums(section, gate_weight, up_weight, chunks[0], 1, send)
    total, sent = core_sums(send, keep)
    later, _ = lax.optimization_barrier((section, sent))
    send, keep = stream_sums(later, gate_weight, up_weight, chunks[1])
    received, keep = lax.optimization_barrier((swap(sent, "narrow"), keep))
    mine = hidden_half(total, received)
    total, sent = core_sums(send, keep)
    mixed = down(down_weight, chunks[0], (0, 1), (mine, swap(mine, "sub")))
    received, mixed = lax.optimization_barrier((swap(sent, "narrow"), mixed))
    mine = hidden_half(total, received)
    mixed = down(down_weight, chunks[1], (0,), (mine,), mixed)
    out, *blocks = down(down_weight, chunks[1], (1,), (swap(mine, "sub"),), mixed, last=True)
    for block, apart in zip(blocks, (3, 2, 1)):
        out = lax.optimization_barrier(out + across(block, apart).astype(F32))
    return out.astype(BF16).reshape(2, rows, -1).swapaxes(0, 1).reshape(rows, -1)


def solution(mesh):
    placed = (
        P(("groups", "wide"), ("narrow", "sub")),
        P(("narrow", "sub"), "wide"),
        P(("narrow", "sub"), "wide"),
        P("wide", ("narrow", "sub")),
    )
    sizes = tuple(mesh.shape[axis] for axis in ("groups", "wide", "narrow", "sub"))
    return jax.shard_map(
        chunked if sizes == (2, 4, 2, 2) else general,
        mesh=mesh,
        in_specs=placed,
        out_specs=P(("groups", "wide"), ("narrow", "sub")),
        check_vma=False,
    )
```

```python
import functools

import jax
import jax.numpy as jnp
from jax import lax
from jax.experimental import pallas as pl
from jax.experimental.pallas import tpu as pltpu
from jax.sharding import PartitionSpec as P

BF16 = jnp.bfloat16
F32 = jnp.float32


def activate(gate_sums, up_sums):
    return (jax.nn.silu(gate_sums) * up_sums).astype(BF16)


def general(tokens, gate_weight, up_weight, down_weight):
    section = lax.all_gather(tokens, "wide", axis=0, tiled=True)
    gate_part = jnp.dot(section, gate_weight, preferred_element_type=F32)
    up_part = jnp.dot(section, up_weight, preferred_element_type=F32)
    gate_sums = lax.psum(gate_part, ("narrow", "sub"))
    up_sums = lax.psum(up_part, ("narrow", "sub"))
    mixed = lax.psum_scatter(
        jnp.dot(activate(gate_sums, up_sums), down_weight, preferred_element_type=F32),
        "wide",
        scatter_dimension=0,
        tiled=True,
    )
    return mixed.astype(BF16)


def swap(x, axis):
    return lax.ppermute(x, axis, [(0, 1), (1, 0)])


BLOCK = 256
WIDE = 512
VMEM = pl.BlockSpec(memory_space=pltpu.VMEM)
ANY = pl.BlockSpec(memory_space=pl.ANY)
HBM = pl.BlockSpec(memory_space=pltpu.HBM)
GRANT = pltpu.CompilerParams(vmem_limit_bytes=6 * 2**20)


def held_in(x):
    return pltpu.with_memory_space_constraint(x, pltpu.VMEM)


def left_in_hbm(x):
    return pltpu.with_memory_space_constraint(x, pltpu.HBM)


def beside_kernel(*refs):
    refs[-1][...] = jnp.zeros_like(refs[-1])


def beside(weight, *operands):
    operands = [left_in_hbm(weight), *operands]
    return pl.pallas_call(
        beside_kernel,
        out_shape=jax.ShapeDtypeStruct((8, 128), F32),
        in_specs=[HBM] + [ANY] * (len(operands) - 1),
        out_specs=VMEM,
        compiler_params=GRANT,
        cost_estimate=pl.CostEstimate(flops=0, bytes_accessed=2 * weight.size, transcendentals=0),
        name="beside",
    )(*operands)


def half_sums_kernel(first, half, mine, tokens, gate, up, after, out, held, sems):
    core = lax.axis_index("sub")
    start = first + jnp.where(core == mine, 1, 0) * half

    def copy(block):
        at = pl.multiple_of(block * BLOCK, BLOCK)
        return pltpu.make_async_copy(
            up.at[:, pl.ds(pl.multiple_of(start + at, BLOCK), BLOCK)], held.at[:, pl.ds(at, BLOCK)], sems.at[block]
        )

    for block in range(half // BLOCK):
        copy(block).start()

    def steps(body):
        pl.loop(0, half // WIDE)(lambda step: body(pl.multiple_of(step * WIDE, WIDE), WIDE))
        if half % WIDE:
            body(half - half % WIDE, half % WIDE)

    def gate_sums(at, wide):
        columns = pl.ds(pl.multiple_of(start + at, BLOCK), wide)
        out[:, pl.ds(at, wide)] = jnp.dot(tokens[...], gate[:, columns], preferred_element_type=F32).astype(
            out.dtype
        )

    def up_sums(at, wide):
        for block in range(wide // BLOCK):
            copy(at // BLOCK + block).wait()
        out[:, pl.ds(half + at, wide)] = jnp.dot(
            tokens[...], held[:, pl.ds(at, wide)], preferred_element_type=F32
        ).astype(out.dtype)

    steps(gate_sums)
    steps(up_sums)


def half_sums(tokens, gate, up, chunk, mine, after):
    rows, depth = tokens.shape
    first, width = chunk
    half = width // 2
    return pl.pallas_call(
        functools.partial(half_sums_kernel, first, half, mine),
        out_shape=jax.ShapeDtypeStruct((rows, width), F32 if mine else BF16),
        in_specs=[VMEM, VMEM, HBM, ANY],
        out_specs=VMEM,
        scratch_shapes=[pltpu.VMEM((depth, half), BF16), pltpu.SemaphoreType.DMA((half // BLOCK,))],
        compiler_params=pltpu.CompilerParams(vmem_limit_bytes=2 * depth * half + 2 * 2**20),
        cost_estimate=pl.CostEstimate(
            flops=2 * rows * depth * width, bytes_accessed=2 * depth * width, transcendentals=0
        ),
        name="half_sums",
    )(tokens, held_in(gate), left_in_hbm(up), after)


def block_copies(first, half, step, gate, up, dst, sem):
    core = lax.axis_index("sub")
    mine = jnp.int32(step >= half // BLOCK)
    side = jnp.where(mine == 1, core, 1 - core)
    unit = first + side * half + (step - mine * (half // BLOCK)) * BLOCK
    columns = pl.ds(pl.multiple_of(unit, BLOCK), BLOCK)
    return [
        pltpu.make_async_copy(weight.at[:, columns], dst.at[:, pl.ds(i * BLOCK, BLOCK)], sem.at[i])
        for i, weight in enumerate((gate, up))
    ]


def pair(ref, at):
    return ref.at[:, pl.ds(pl.multiple_of(at * 2 * BLOCK, 2 * BLOCK), 2 * BLOCK)]


def stream_kernel(first, steps, tokens, gate, up, *refs):
    send, keep, streamed, sems = refs[-4:]
    held = refs[0] if steps else None
    half = send.shape[1] // 2
    blocks = half // BLOCK

    def copies(step):
        at = step - steps
        return block_copies(first, half, step, gate, up, pair(streamed, at), sems.at[at])

    for step in range(steps, 2 * blocks):
        for copy in copies(step):
            copy.start()

    def add(out, start, source, block):
        both = jnp.dot(tokens[...], source[...], preferred_element_type=F32).astype(out.dtype)
        for i in range(2):
            column = pl.multiple_of((i * blocks + block - start) * BLOCK, BLOCK)
            out[:, pl.ds(column, BLOCK)] = both[:, i * BLOCK : (i + 1) * BLOCK]

    for side, out in enumerate((send, keep)):
        start, end = side * blocks, (side + 1) * blocks

        middle = min(max(steps, start), end)
        if start < middle:

            @pl.loop(start, middle)
            def _(step):
                add(out, start, pair(held, step), step)

        if middle < end:

            @pl.loop(middle, end)
            def _(step):
                for copy in copies(step):
                    copy.wait()
                add(out, start, pair(streamed, step - steps), step)


def stream_sums(tokens, gate, up, chunk, held=None):
    rows, depth = tokens.shape
    first, width = chunk
    steps = 0 if held is None else held.shape[1] // (2 * BLOCK)
    streamed = width // BLOCK - steps
    return pl.pallas_call(
        functools.partial(stream_kernel, first, steps),
        out_shape=(jax.ShapeDtypeStruct((rows, width), BF16), jax.ShapeDtypeStruct((rows, width), F32)),
        in_specs=[VMEM, HBM, HBM] + [VMEM] * (steps > 0),
        out_specs=(VMEM, VMEM),
        scratch_shapes=[
            pltpu.VMEM((depth, streamed * 2 * BLOCK), BF16),
            pltpu.SemaphoreType.DMA((streamed, 2)),
        ],
        compiler_params=pltpu.CompilerParams(vmem_limit_bytes=4 * streamed * depth * BLOCK + 4 * 2**20),
        cost_estimate=pl.CostEstimate(
            flops=4 * rows * depth * width, bytes_accessed=4 * depth * width, transcendentals=0
        ),
        name="stream_sums",
    )(tokens, left_in_hbm(gate), left_in_hbm(up), *([held_in(held)] if steps else []))


def partial_sums(first, half, sides, hiddens, weight, columns):
    core = lax.axis_index("sub")
    part = 0.0
    for side, hidden in zip(sides, hiddens):
        start = pl.multiple_of(first + jnp.where(core == side, 0, half), BLOCK)
        part += jnp.dot(hidden[...], weight[pl.ds(start, half), columns], preferred_element_type=F32)
    return part


def down_kernel(first, half, sides, weight, *refs):
    hiddens, out = refs[: len(sides)], refs[-1]
    totals = refs[len(sides) : -1]
    for at in range(0, out.shape[1], WIDE):
        columns = pl.ds(at, WIDE)
        part = partial_sums(first, half, sides, hiddens, weight, columns)
        for total in totals:
            part += total[:, columns]
        out[:, columns] = part


def last_down_kernel(first, half, sides, weight, hidden, total, own, *sends):
    rows, columns = own.shape[0] // 2, own.shape[1]
    for at in range(0, columns, WIDE):
        parts = []
        for start in (at, columns + at):
            part = partial_sums(first, half, sides, [hidden], weight, pl.ds(start, WIDE))
            parts.append(part + total[:, pl.ds(start, WIDE)])
        for place, out in enumerate((own, *sends)):
            pieces = [part[place * rows : (place + 1) * rows] for part in parts]
            out[:, pl.ds(at, WIDE)] = jnp.concatenate(pieces, axis=0).astype(out.dtype)


def down(weight, chunk, sides, hiddens, total=None, last=False):
    rows, half = hiddens[0].shape
    features = weight.shape[1]
    if last:
        packed = (rows // 2, features // 2)
        out_shape = (jax.ShapeDtypeStruct(packed, F32),) + (jax.ShapeDtypeStruct(packed, BF16),) * 3
        kernel = last_down_kernel
    else:
        out_shape = jax.ShapeDtypeStruct((rows, features), F32)
        kernel = down_kernel
    operands = [held_in(weight), *hiddens] + ([] if total is None else [total])
    return pl.pallas_call(
        functools.partial(kernel, chunk[0], half, sides),
        out_shape=out_shape,
        in_specs=[VMEM] * len(operands),
        out_specs=(VMEM,) * 4 if last else VMEM,
        compiler_params=GRANT,
        cost_estimate=pl.CostEstimate(
            flops=2 * rows * features * half * len(sides),
            bytes_accessed=2 * features * half * len(sides),
            transcendentals=0,
        ),
        name="down",
    )(*operands)


def split(units):
    more = units // 512 * 8 // 13 * 512
    return (0, more), (more, units - more)


def across(x, apart):
    return lax.ppermute(x, "wide", [(i, i ^ apart) for i in range(4)])


def chunked(tokens, gate_weight, up_weight, down_weight):
    rows = tokens.shape[0]
    chunks = split(gate_weight.shape[1])
    apart_by = (3, 1, 2)
    section = tokens
    for apart in apart_by:
        section = lax.optimization_barrier(jnp.concatenate([section, across(tokens, apart)], axis=0))

    def core_sums(send, keep):
        total = keep + swap(send, "sub").astype(F32)
        return total, total.astype(BF16)

    def hidden_half(total, received):
        return activate(*jnp.split(total + received.astype(F32), 2, axis=1))

    ready = beside(gate_weight)
    send = half_sums(section, gate_weight, up_weight, chunks[0], 0, ready)
    keep = half_sums(section, gate_weight, up_weight, chunks[0], 1, send)
    total, sent = core_sums(send, keep)
    later, _ = lax.optimization_barrier((section, sent))
    send, keep = stream_sums(later, gate_weight, up_weight, chunks[1])
    received, keep = lax.optimization_barrier((swap(sent, "narrow"), keep))
    mine = hidden_half(total, received)
    total, sent = core_sums(send, keep)
    mixed = down(down_weight, chunks[0], (0, 1), (mine, swap(mine, "sub")))
    received, mixed = lax.optimization_barrier((swap(sent, "narrow"), mixed))
    mine = hidden_half(total, received)
    mixed = down(down_weight, chunks[1], (0,), (mine,), mixed)
    out, *blocks = down(down_weight, chunks[1], (1,), (swap(mine, "sub"),), mixed, last=True)
    for apart in (3, 2, 1):
        block = blocks[apart_by.index(apart)]
        out = lax.optimization_barrier(out + across(block, apart).astype(F32))
    return out.astype(BF16).reshape(2, rows, -1).swapaxes(0, 1).reshape(rows, -1)


def solution(mesh):
    placed = (
        P(("groups", "wide"), ("narrow", "sub")),
        P(("narrow", "sub"), "wide"),
        P(("narrow", "sub"), "wide"),
        P("wide", ("narrow", "sub")),
    )
    sizes = tuple(mesh.shape[axis] for axis in ("groups", "wide", "narrow", "sub"))
    return jax.shard_map(
        chunked if sizes == (2, 4, 2, 2) else general,
        mesh=mesh,
        in_specs=placed,
        out_specs=P(("groups", "wide"), ("narrow", "sub")),
        check_vma=False,
    )
```

```python
import functools

import jax
import jax.numpy as jnp
from jax import lax
from jax.experimental import pallas as pl
from jax.experimental.pallas import tpu as pltpu
from jax.sharding import PartitionSpec as P

BF16 = jnp.bfloat16
F32 = jnp.float32


def activate(gate_sums, up_sums):
    return (jax.nn.silu(gate_sums) * up_sums).astype(BF16)


def general(tokens, gate_weight, up_weight, down_weight):
    section = lax.all_gather(tokens, "wide", axis=0, tiled=True)
    gate_part = jnp.dot(section, gate_weight, preferred_element_type=F32)
    up_part = jnp.dot(section, up_weight, preferred_element_type=F32)
    gate_sums = lax.psum(gate_part, ("narrow", "sub"))
    up_sums = lax.psum(up_part, ("narrow", "sub"))
    mixed = lax.psum_scatter(
        jnp.dot(activate(gate_sums, up_sums), down_weight, preferred_element_type=F32),
        "wide",
        scatter_dimension=0,
        tiled=True,
    )
    return mixed.astype(BF16)


def swap(x, axis):
    return lax.ppermute(x, axis, [(0, 1), (1, 0)])


BLOCK = 256
WIDE = 512
VMEM = pl.BlockSpec(memory_space=pltpu.VMEM)
ANY = pl.BlockSpec(memory_space=pl.ANY)
HBM = pl.BlockSpec(memory_space=pltpu.HBM)
GRANT = pltpu.CompilerParams(vmem_limit_bytes=6 * 2**20)


def held_in(x):
    return pltpu.with_memory_space_constraint(x, pltpu.VMEM)


def left_in_hbm(x):
    return pltpu.with_memory_space_constraint(x, pltpu.HBM)


def beside_kernel(*refs):
    refs[-1][...] = jnp.zeros_like(refs[-1])


def beside(weight, *operands):
    operands = [left_in_hbm(weight), *operands]
    return pl.pallas_call(
        beside_kernel,
        out_shape=jax.ShapeDtypeStruct((8, 128), F32),
        in_specs=[HBM] + [ANY] * (len(operands) - 1),
        out_specs=VMEM,
        compiler_params=GRANT,
        cost_estimate=pl.CostEstimate(flops=0, bytes_accessed=2 * weight.size, transcendentals=0),
        name="beside",
    )(*operands)


def half_sums_kernel(first, half, mine, tokens, gate, up, after, out, held, sems):
    core = lax.axis_index("sub")
    start = first + jnp.where(core == mine, 1, 0) * half

    def copy(block):
        at = pl.multiple_of(block * BLOCK, BLOCK)
        return pltpu.make_async_copy(
            up.at[:, pl.ds(pl.multiple_of(start + at, BLOCK), BLOCK)], held.at[:, pl.ds(at, BLOCK)], sems.at[block]
        )

    for block in range(half // BLOCK):
        copy(block).start()

    def steps(body):
        pl.loop(0, half // WIDE)(lambda step: body(pl.multiple_of(step * WIDE, WIDE), WIDE))
        if half % WIDE:
            body(half - half % WIDE, half % WIDE)

    def gate_sums(at, wide):
        columns = pl.ds(pl.multiple_of(start + at, BLOCK), wide)
        out[:, pl.ds(at, wide)] = jnp.dot(tokens[...], gate[:, columns], preferred_element_type=F32).astype(
            out.dtype
        )

    def up_sums(at, wide):
        for block in range(wide // BLOCK):
            copy(at // BLOCK + block).wait()
        out[:, pl.ds(half + at, wide)] = jnp.dot(
            tokens[...], held[:, pl.ds(at, wide)], preferred_element_type=F32
        ).astype(out.dtype)

    steps(gate_sums)
    steps(up_sums)


def half_sums(tokens, gate, up, chunk, mine, after):
    rows, depth = tokens.shape
    first, width = chunk
    half = width // 2
    return pl.pallas_call(
        functools.partial(half_sums_kernel, first, half, mine),
        out_shape=jax.ShapeDtypeStruct((rows, width), F32),
        in_specs=[VMEM, VMEM, HBM, ANY],
        out_specs=VMEM,
        scratch_shapes=[pltpu.VMEM((depth, half), BF16), pltpu.SemaphoreType.DMA((half // BLOCK,))],
        compiler_params=pltpu.CompilerParams(vmem_limit_bytes=2 * depth * half + 2 * 2**20),
        cost_estimate=pl.CostEstimate(
            flops=2 * rows * depth * width, bytes_accessed=2 * depth * width, transcendentals=0
        ),
        name="half_sums",
    )(tokens, held_in(gate), left_in_hbm(up), after)


def block_copies(first, half, step, gate, up, dst, sem):
    core = lax.axis_index("sub")
    mine = jnp.int32(step >= half // BLOCK)
    side = jnp.where(mine == 1, core, 1 - core)
    unit = first + side * half + (step - mine * (half // BLOCK)) * BLOCK
    columns = pl.ds(pl.multiple_of(unit, BLOCK), BLOCK)
    return [
        pltpu.make_async_copy(weight.at[:, columns], dst.at[:, pl.ds(i * BLOCK, BLOCK)], sem.at[i])
        for i, weight in enumerate((gate, up))
    ]


def pair(ref, at):
    return ref.at[:, pl.ds(pl.multiple_of(at * 2 * BLOCK, 2 * BLOCK), 2 * BLOCK)]


def stream_kernel(first, steps, tokens, gate, up, *refs):
    send, keep, streamed, sems = refs[-4:]
    held = refs[0] if steps else None
    half = send.shape[1] // 2
    blocks = half // BLOCK

    def copies(step):
        at = step - steps
        return block_copies(first, half, step, gate, up, pair(streamed, at), sems.at[at])

    for step in range(steps, 2 * blocks):
        for copy in copies(step):
            copy.start()

    def add(out, start, source, block):
        both = jnp.dot(tokens[...], source[...], preferred_element_type=F32).astype(out.dtype)
        for i in range(2):
            column = pl.multiple_of((i * blocks + block - start) * BLOCK, BLOCK)
            out[:, pl.ds(column, BLOCK)] = both[:, i * BLOCK : (i + 1) * BLOCK]

    for side, out in enumerate((send, keep)):
        start, end = side * blocks, (side + 1) * blocks

        middle = min(max(steps, start), end)
        if start < middle:

            @pl.loop(start, middle)
            def _(step):
                add(out, start, pair(held, step), step)

        if middle < end:

            @pl.loop(middle, end)
            def _(step):
                for copy in copies(step):
                    copy.wait()
                add(out, start, pair(streamed, step - steps), step)


def stream_sums(tokens, gate, up, chunk, held=None):
    rows, depth = tokens.shape
    first, width = chunk
    steps = 0 if held is None else held.shape[1] // (2 * BLOCK)
    streamed = width // BLOCK - steps
    return pl.pallas_call(
        functools.partial(stream_kernel, first, steps),
        out_shape=(jax.ShapeDtypeStruct((rows, width), BF16), jax.ShapeDtypeStruct((rows, width), F32)),
        in_specs=[VMEM, HBM, HBM] + [VMEM] * (steps > 0),
        out_specs=(VMEM, VMEM),
        scratch_shapes=[
            pltpu.VMEM((depth, streamed * 2 * BLOCK), BF16),
            pltpu.SemaphoreType.DMA((streamed, 2)),
        ],
        compiler_params=pltpu.CompilerParams(vmem_limit_bytes=4 * streamed * depth * BLOCK + 4 * 2**20),
        cost_estimate=pl.CostEstimate(
            flops=4 * rows * depth * width, bytes_accessed=4 * depth * width, transcendentals=0
        ),
        name="stream_sums",
    )(tokens, left_in_hbm(gate), left_in_hbm(up), *([held_in(held)] if steps else []))


def partial_sums(first, half, sides, hiddens, weight, columns):
    core = lax.axis_index("sub")
    part = 0.0
    for side, hidden in zip(sides, hiddens):
        start = pl.multiple_of(first + jnp.where(core == side, 0, half), BLOCK)
        part += jnp.dot(hidden[...], weight[pl.ds(start, half), columns], preferred_element_type=F32)
    return part


def down_kernel(first, half, sides, weight, *refs):
    hiddens, out = refs[: len(sides)], refs[-1]
    totals = refs[len(sides) : -1]
    for at in range(0, out.shape[1], WIDE):
        columns = pl.ds(at, WIDE)
        part = partial_sums(first, half, sides, hiddens, weight, columns)
        for total in totals:
            part += total[:, columns]
        out[:, columns] = part


def last_down_kernel(first, half, sides, weight, hidden, total, own, *sends):
    rows, columns = own.shape[0] // 2, own.shape[1]
    for at in range(0, columns, WIDE):
        parts = []
        for start in (at, columns + at):
            part = partial_sums(first, half, sides, [hidden], weight, pl.ds(start, WIDE))
            parts.append(part + total[:, pl.ds(start, WIDE)])
        for place, out in enumerate((own, *sends)):
            pieces = [part[place * rows : (place + 1) * rows] for part in parts]
            out[:, pl.ds(at, WIDE)] = jnp.concatenate(pieces, axis=0).astype(out.dtype)


def down(weight, chunk, sides, hiddens, total=None, last=False):
    rows, half = hiddens[0].shape
    features = weight.shape[1]
    if last:
        packed = (rows // 2, features // 2)
        out_shape = (jax.ShapeDtypeStruct(packed, F32),) + (jax.ShapeDtypeStruct(packed, BF16),) * 3
        kernel = last_down_kernel
    else:
        out_shape = jax.ShapeDtypeStruct((rows, features), F32)
        kernel = down_kernel
    operands = [held_in(weight), *hiddens] + ([] if total is None else [total])
    return pl.pallas_call(
        functools.partial(kernel, chunk[0], half, sides),
        out_shape=out_shape,
        in_specs=[VMEM] * len(operands),
        out_specs=(VMEM,) * 4 if last else VMEM,
        compiler_params=GRANT,
        cost_estimate=pl.CostEstimate(
            flops=2 * rows * features * half * len(sides),
            bytes_accessed=2 * features * half * len(sides),
            transcendentals=0,
        ),
        name="down",
    )(*operands)


def split(units):
    more = units // 512 * 8 // 13 * 512
    return (0, more), (more, units - more)


def across(x, apart):
    return lax.ppermute(x, "wide", [(i, i ^ apart) for i in range(4)])


def chunked(tokens, gate_weight, up_weight, down_weight):
    rows = tokens.shape[0]
    chunks = split(gate_weight.shape[1])
    apart_by = (3, 1, 2)
    section = tokens
    for apart in apart_by:
        section = lax.optimization_barrier(jnp.concatenate([section, across(tokens, apart)], axis=0))

    def core_sums(send, keep):
        total = keep + swap(send, "sub").astype(F32)
        return total, total.astype(BF16)

    def hidden_half(total, received):
        return activate(*jnp.split(total + received.astype(F32), 2, axis=1))

    ready = beside(gate_weight)
    send = half_sums(section, gate_weight, up_weight, chunks[0], 0, ready)
    keep = half_sums(section, gate_weight, up_weight, chunks[0], 1, send)
    total, sent = core_sums(send, keep)
    later, _ = lax.optimization_barrier((section, sent))
    send, keep = stream_sums(later, gate_weight, up_weight, chunks[1])
    received, keep = lax.optimization_barrier((swap(sent, "narrow"), keep))
    mine = hidden_half(total, received)
    total, sent = core_sums(send, keep)
    mixed = down(down_weight, chunks[0], (0, 1), (mine, swap(mine, "sub")))
    received, mixed = lax.optimization_barrier((swap(sent, "narrow"), mixed))
    mine = hidden_half(total, received)
    mixed = down(down_weight, chunks[1], (0,), (mine,), mixed)
    out, *blocks = down(down_weight, chunks[1], (1,), (swap(mine, "sub"),), mixed, last=True)
    for apart in (3, 2, 1):
        block = blocks[apart_by.index(apart)]
        out = lax.optimization_barrier(out + across(block, apart).astype(F32))
    return out.astype(BF16).reshape(2, rows, -1).swapaxes(0, 1).reshape(rows, -1)


def solution(mesh):
    placed = (
        P(("groups", "wide"), ("narrow", "sub")),
        P(("narrow", "sub"), "wide"),
        P(("narrow", "sub"), "wide"),
        P("wide", ("narrow", "sub")),
    )
    sizes = tuple(mesh.shape[axis] for axis in ("groups", "wide", "narrow", "sub"))
    return jax.shard_map(
        chunked if sizes == (2, 4, 2, 2) else general,
        mesh=mesh,
        in_specs=placed,
        out_specs=P(("groups", "wide"), ("narrow", "sub")),
        check_vma=False,
    )
```

```python
import functools

import jax
import jax.numpy as jnp
from jax import lax
from jax.experimental import pallas as pl
from jax.experimental.pallas import tpu as pltpu
from jax.sharding import PartitionSpec as P

BF16 = jnp.bfloat16
F32 = jnp.float32


def activate(gate_sums, up_sums):
    return (jax.nn.silu(gate_sums) * up_sums).astype(BF16)


def general(tokens, gate_weight, up_weight, down_weight):
    section = lax.all_gather(tokens, "wide", axis=0, tiled=True)
    gate_part = jnp.dot(section, gate_weight, preferred_element_type=F32)
    up_part = jnp.dot(section, up_weight, preferred_element_type=F32)
    gate_sums = lax.psum(gate_part, ("narrow", "sub"))
    up_sums = lax.psum(up_part, ("narrow", "sub"))
    mixed = lax.psum_scatter(
        jnp.dot(activate(gate_sums, up_sums), down_weight, preferred_element_type=F32),
        "wide",
        scatter_dimension=0,
        tiled=True,
    )
    return mixed.astype(BF16)


def swap(x, axis):
    return lax.ppermute(x, axis, [(0, 1), (1, 0)])


BLOCK = 256
WIDE = 512
VMEM = pl.BlockSpec(memory_space=pltpu.VMEM)
ANY = pl.BlockSpec(memory_space=pl.ANY)
HBM = pl.BlockSpec(memory_space=pltpu.HBM)
GRANT = pltpu.CompilerParams(vmem_limit_bytes=6 * 2**20)


def held_in(x):
    return pltpu.with_memory_space_constraint(x, pltpu.VMEM)


def left_in_hbm(x):
    return pltpu.with_memory_space_constraint(x, pltpu.HBM)


def beside_kernel(*refs):
    refs[-1][...] = jnp.zeros_like(refs[-1])


def beside(weight, *operands):
    operands = [left_in_hbm(weight), *operands]
    return pl.pallas_call(
        beside_kernel,
        out_shape=jax.ShapeDtypeStruct((8, 128), F32),
        in_specs=[HBM] + [ANY] * (len(operands) - 1),
        out_specs=VMEM,
        compiler_params=GRANT,
        cost_estimate=pl.CostEstimate(flops=0, bytes_accessed=2 * weight.size, transcendentals=0),
        name="beside",
    )(*operands)


def half_sums_kernel(first, half, mine, tokens, gate, up, after, out, held, sems):
    core = lax.axis_index("sub")
    start = first + jnp.where(core == mine, 1, 0) * half

    def copy(block):
        at = pl.multiple_of(block * BLOCK, BLOCK)
        return pltpu.make_async_copy(
            up.at[:, pl.ds(pl.multiple_of(start + at, BLOCK), BLOCK)], held.at[:, pl.ds(at, BLOCK)], sems.at[block]
        )

    for block in range(half // BLOCK):
        copy(block).start()

    def steps(body):
        pl.loop(0, half // WIDE)(lambda step: body(pl.multiple_of(step * WIDE, WIDE), WIDE))
        if half % WIDE:
            body(half - half % WIDE, half % WIDE)

    def gate_sums(at, wide):
        columns = pl.ds(pl.multiple_of(start + at, BLOCK), wide)
        out[:, pl.ds(at, wide)] = jnp.dot(tokens[...], gate[:, columns], preferred_element_type=F32).astype(
            out.dtype
        )

    def up_sums(at, wide):
        for block in range(wide // BLOCK):
            copy(at // BLOCK + block).wait()
        out[:, pl.ds(half + at, wide)] = jnp.dot(
            tokens[...], held[:, pl.ds(at, wide)], preferred_element_type=F32
        ).astype(out.dtype)

    steps(gate_sums)
    steps(up_sums)


def half_sums(tokens, gate, up, chunk, mine, after):
    rows, depth = tokens.shape
    first, width = chunk
    half = width // 2
    return pl.pallas_call(
        functools.partial(half_sums_kernel, first, half, mine),
        out_shape=jax.ShapeDtypeStruct((rows, width), F32),
        in_specs=[VMEM, VMEM, HBM, ANY],
        out_specs=VMEM,
        scratch_shapes=[pltpu.VMEM((depth, half), BF16), pltpu.SemaphoreType.DMA((half // BLOCK,))],
        compiler_params=pltpu.CompilerParams(vmem_limit_bytes=2 * depth * half + 2 * 2**20),
        cost_estimate=pl.CostEstimate(
            flops=2 * rows * depth * width, bytes_accessed=2 * depth * width, transcendentals=0
        ),
        name="half_sums",
    )(tokens, held_in(gate), left_in_hbm(up), after)


def block_copies(first, half, step, gate, up, dst, sem):
    core = lax.axis_index("sub")
    mine = jnp.int32(step >= half // BLOCK)
    side = jnp.where(mine == 1, core, 1 - core)
    unit = first + side * half + (step - mine * (half // BLOCK)) * BLOCK
    columns = pl.ds(pl.multiple_of(unit, BLOCK), BLOCK)
    return [
        pltpu.make_async_copy(weight.at[:, columns], dst.at[:, pl.ds(i * BLOCK, BLOCK)], sem.at[i])
        for i, weight in enumerate((gate, up))
    ]


def pair(ref, at):
    return ref.at[:, pl.ds(pl.multiple_of(at * 2 * BLOCK, 2 * BLOCK), 2 * BLOCK)]


def stream_kernel(first, steps, tokens, gate, up, *refs):
    send, keep, streamed, sems = refs[-4:]
    held = refs[0] if steps else None
    half = send.shape[1] // 2
    blocks = half // BLOCK

    def copies(step):
        at = step - steps
        return block_copies(first, half, step, gate, up, pair(streamed, at), sems.at[at])

    for step in range(steps, 2 * blocks):
        for copy in copies(step):
            copy.start()

    def add(out, start, source, block):
        both = jnp.dot(tokens[...], source[...], preferred_element_type=F32).astype(out.dtype)
        for i in range(2):
            column = pl.multiple_of((i * blocks + block - start) * BLOCK, BLOCK)
            out[:, pl.ds(column, BLOCK)] = both[:, i * BLOCK : (i + 1) * BLOCK]

    for side, out in enumerate((send, keep)):
        start, end = side * blocks, (side + 1) * blocks

        middle = min(max(steps, start), end)
        if start < middle:

            @pl.loop(start, middle)
            def _(step):
                add(out, start, pair(held, step), step)

        if middle < end:

            @pl.loop(middle, end)
            def _(step):
                for copy in copies(step):
                    copy.wait()
                add(out, start, pair(streamed, step - steps), step)


def stream_sums(tokens, gate, up, chunk, held=None):
    rows, depth = tokens.shape
    first, width = chunk
    steps = 0 if held is None else held.shape[1] // (2 * BLOCK)
    streamed = width // BLOCK - steps
    return pl.pallas_call(
        functools.partial(stream_kernel, first, steps),
        out_shape=(jax.ShapeDtypeStruct((rows, width), BF16), jax.ShapeDtypeStruct((rows, width), F32)),
        in_specs=[VMEM, HBM, HBM] + [VMEM] * (steps > 0),
        out_specs=(VMEM, VMEM),
        scratch_shapes=[
            pltpu.VMEM((depth, streamed * 2 * BLOCK), BF16),
            pltpu.SemaphoreType.DMA((streamed, 2)),
        ],
        compiler_params=pltpu.CompilerParams(vmem_limit_bytes=4 * streamed * depth * BLOCK + 4 * 2**20),
        cost_estimate=pl.CostEstimate(
            flops=4 * rows * depth * width, bytes_accessed=4 * depth * width, transcendentals=0
        ),
        name="stream_sums",
    )(tokens, left_in_hbm(gate), left_in_hbm(up), *([held_in(held)] if steps else []))


def partial_sums(first, half, sides, hiddens, weight, columns):
    core = lax.axis_index("sub")
    part = 0.0
    for side, hidden in zip(sides, hiddens):
        start = pl.multiple_of(first + jnp.where(core == side, 0, half), BLOCK)
        part += jnp.dot(hidden[...], weight[pl.ds(start, hidden.shape[1]), columns], preferred_element_type=F32)
    return part


def down_kernel(first, half, sides, weight, *refs):
    hiddens, out = refs[: len(sides)], refs[-1]
    totals = refs[len(sides) : -1]
    for at in range(0, out.shape[1], WIDE):
        columns = pl.ds(at, WIDE)
        part = partial_sums(first, half, sides, hiddens, weight, columns)
        for total in totals:
            part += total[:, columns]
        out[:, columns] = part


def last_down_kernel(first, half, sides, weight, hidden, total, own, *sends):
    rows, columns = own.shape[0] // 2, own.shape[1]
    for at in range(0, columns, WIDE):
        parts = []
        for start in (at, columns + at):
            part = partial_sums(first, half, sides, [hidden], weight, pl.ds(start, WIDE))
            parts.append(part + total[:, pl.ds(start, WIDE)])
        for place, out in enumerate((own, *sends)):
            pieces = [part[place * rows : (place + 1) * rows] for part in parts]
            out[:, pl.ds(at, WIDE)] = jnp.concatenate(pieces, axis=0).astype(out.dtype)


def down(weight, chunk, sides, hiddens, total=None, last=False, offset=0):
    rows, units = hiddens[0].shape
    half = chunk[1] // 2
    features = weight.shape[1]
    if last:
        packed = (rows // 2, features // 2)
        out_shape = (jax.ShapeDtypeStruct(packed, F32),) + (jax.ShapeDtypeStruct(packed, BF16),) * 3
        kernel = last_down_kernel
    else:
        out_shape = jax.ShapeDtypeStruct((rows, features), F32)
        kernel = down_kernel
    operands = [held_in(weight), *hiddens] + ([] if total is None else [total])
    return pl.pallas_call(
        functools.partial(kernel, chunk[0] + offset, half, sides),
        out_shape=out_shape,
        in_specs=[VMEM] * len(operands),
        out_specs=(VMEM,) * 4 if last else VMEM,
        compiler_params=GRANT,
        cost_estimate=pl.CostEstimate(
            flops=2 * rows * features * units * len(sides),
            bytes_accessed=2 * features * units * len(sides),
            transcendentals=0,
        ),
        name="down",
    )(*operands)


def split(units):
    more = units // 512 * 8 // 13 * 512
    return (0, more), (more, units - more)


def across(x, apart):
    return lax.ppermute(x, "wide", [(i, i ^ apart) for i in range(4)])


def chunked(tokens, gate_weight, up_weight, down_weight):
    rows = tokens.shape[0]
    chunks = split(gate_weight.shape[1])
    apart_by = (3, 1, 2)
    section = tokens
    for apart in apart_by:
        section = lax.optimization_barrier(jnp.concatenate([section, across(tokens, apart)], axis=0))

    def core_sums(send, keep):
        total = keep + swap(send, "sub").astype(F32)
        return total, total.astype(BF16)

    def hidden_half(total, received):
        return activate(*jnp.split(total + received.astype(F32), 2, axis=1))

    ready = beside(gate_weight)
    send = half_sums(section, gate_weight, up_weight, chunks[0], 0, ready)
    keep = half_sums(section, gate_weight, up_weight, chunks[0], 1, send)
    total, sent = core_sums(send, keep)
    later, _ = lax.optimization_barrier((section, sent))
    send, keep = stream_sums(later, gate_weight, up_weight, chunks[1])
    received, keep = lax.optimization_barrier((swap(sent, "narrow"), keep))
    mine = hidden_half(total, received)
    total, sent = core_sums(send, keep)
    mixed = down(down_weight, chunks[0], (0, 1), (mine, swap(mine, "sub")))
    half = chunks[1][1] // 2
    cut = half // BLOCK // 2 * BLOCK

    def part(x, start, end):
        return jnp.concatenate([x[:, start:end], x[:, half + start : half + end]], axis=1)

    received = [swap(part(sent, *ends), "narrow") for ends in ((0, cut), (cut, half))]
    received[0], mixed = lax.optimization_barrier((received[0], mixed))
    mine = hidden_half(part(total, 0, cut), received[0])
    mixed = down(down_weight, chunks[1], (0, 1), (mine, swap(mine, "sub")), mixed)
    received[1], mixed = lax.optimization_barrier((received[1], mixed))
    mine = hidden_half(part(total, cut, half), received[1])
    mixed = down(down_weight, chunks[1], (0,), (mine,), mixed, offset=cut)
    out, *blocks = down(
        down_weight, chunks[1], (1,), (swap(mine, "sub"),), mixed, last=True, offset=cut
    )
    for apart in (3, 2, 1):
        block = blocks[apart_by.index(apart)]
        out = lax.optimization_barrier(out + across(block, apart).astype(F32))
    return out.astype(BF16).reshape(2, rows, -1).swapaxes(0, 1).reshape(rows, -1)


def solution(mesh):
    placed = (
        P(("groups", "wide"), ("narrow", "sub")),
        P(("narrow", "sub"), "wide"),
        P(("narrow", "sub"), "wide"),
        P("wide", ("narrow", "sub")),
    )
    sizes = tuple(mesh.shape[axis] for axis in ("groups", "wide", "narrow", "sub"))
    return jax.shard_map(
        chunked if sizes == (2, 4, 2, 2) else general,
        mesh=mesh,
        in_specs=placed,
        out_specs=P(("groups", "wide"), ("narrow", "sub")),
        check_vma=False,
    )
```

```python
import functools

import jax
import jax.numpy as jnp
from jax import lax
from jax.experimental import pallas as pl
from jax.experimental.pallas import tpu as pltpu
from jax.sharding import PartitionSpec as P

BF16 = jnp.bfloat16
F32 = jnp.float32


def activate(gate_sums, up_sums):
    return (jax.nn.silu(gate_sums) * up_sums).astype(BF16)


def general(tokens, gate_weight, up_weight, down_weight):
    section = lax.all_gather(tokens, "wide", axis=0, tiled=True)
    gate_part = jnp.dot(section, gate_weight, preferred_element_type=F32)
    up_part = jnp.dot(section, up_weight, preferred_element_type=F32)
    gate_sums = lax.psum(gate_part, ("narrow", "sub"))
    up_sums = lax.psum(up_part, ("narrow", "sub"))
    mixed = lax.psum_scatter(
        jnp.dot(activate(gate_sums, up_sums), down_weight, preferred_element_type=F32),
        "wide",
        scatter_dimension=0,
        tiled=True,
    )
    return mixed.astype(BF16)


def swap(x, axis):
    return lax.ppermute(x, axis, [(0, 1), (1, 0)])


BLOCK = 256
WIDE = 512
VMEM = pl.BlockSpec(memory_space=pltpu.VMEM)
ANY = pl.BlockSpec(memory_space=pl.ANY)
HBM = pl.BlockSpec(memory_space=pltpu.HBM)
GRANT = pltpu.CompilerParams(vmem_limit_bytes=6 * 2**20)


def held_in(x):
    return pltpu.with_memory_space_constraint(x, pltpu.VMEM)


def left_in_hbm(x):
    return pltpu.with_memory_space_constraint(x, pltpu.HBM)


def beside_kernel(*refs):
    refs[-1][...] = jnp.zeros_like(refs[-1])


def beside(weight, *operands):
    operands = [left_in_hbm(weight), *operands]
    return pl.pallas_call(
        beside_kernel,
        out_shape=jax.ShapeDtypeStruct((8, 128), F32),
        in_specs=[HBM] + [ANY] * (len(operands) - 1),
        out_specs=VMEM,
        compiler_params=GRANT,
        cost_estimate=pl.CostEstimate(flops=0, bytes_accessed=2 * weight.size, transcendentals=0),
        name="beside",
    )(*operands)


def half_sums_kernel(first, half, mine, tokens, gate, up, after, out, held, sems):
    core = lax.axis_index("sub")
    start = first + jnp.where(core == mine, 1, 0) * half

    def copy(block):
        at = pl.multiple_of(block * BLOCK, BLOCK)
        return pltpu.make_async_copy(
            up.at[:, pl.ds(pl.multiple_of(start + at, BLOCK), BLOCK)], held.at[:, pl.ds(at, BLOCK)], sems.at[block]
        )

    for block in range(half // BLOCK):
        copy(block).start()

    def steps(body):
        pl.loop(0, half // WIDE)(lambda step: body(pl.multiple_of(step * WIDE, WIDE), WIDE))
        if half % WIDE:
            body(half - half % WIDE, half % WIDE)

    def gate_sums(at, wide):
        columns = pl.ds(pl.multiple_of(start + at, BLOCK), wide)
        out[:, pl.ds(at, wide)] = jnp.dot(tokens[...], gate[:, columns], preferred_element_type=F32).astype(
            out.dtype
        )

    def up_sums(at, wide):
        for block in range(wide // BLOCK):
            copy(at // BLOCK + block).wait()
        out[:, pl.ds(half + at, wide)] = jnp.dot(
            tokens[...], held[:, pl.ds(at, wide)], preferred_element_type=F32
        ).astype(out.dtype)

    steps(gate_sums)
    steps(up_sums)


def half_sums(tokens, gate, up, chunk, mine, after):
    rows, depth = tokens.shape
    first, width = chunk
    half = width // 2
    return pl.pallas_call(
        functools.partial(half_sums_kernel, first, half, mine),
        out_shape=jax.ShapeDtypeStruct((rows, width), F32),
        in_specs=[VMEM, VMEM, HBM, ANY],
        out_specs=VMEM,
        scratch_shapes=[pltpu.VMEM((depth, half), BF16), pltpu.SemaphoreType.DMA((half // BLOCK,))],
        compiler_params=pltpu.CompilerParams(vmem_limit_bytes=2 * depth * half + 2 * 2**20),
        cost_estimate=pl.CostEstimate(
            flops=2 * rows * depth * width, bytes_accessed=2 * depth * width, transcendentals=0
        ),
        name="half_sums",
    )(tokens, held_in(gate), left_in_hbm(up), after)


def block_copies(first, half, step, gate, up, dst, sem):
    core = lax.axis_index("sub")
    mine = jnp.int32(step >= half // BLOCK)
    side = jnp.where(mine == 1, core, 1 - core)
    unit = first + side * half + (step - mine * (half // BLOCK)) * BLOCK
    columns = pl.ds(pl.multiple_of(unit, BLOCK), BLOCK)
    return [
        pltpu.make_async_copy(weight.at[:, columns], dst.at[:, pl.ds(i * BLOCK, BLOCK)], sem.at[i])
        for i, weight in enumerate((gate, up))
    ]


def pair(ref, at):
    return ref.at[:, pl.ds(pl.multiple_of(at * 2 * BLOCK, 2 * BLOCK), 2 * BLOCK)]


def stream_kernel(first, steps, tokens, gate, up, *refs):
    send, keep, streamed, sems = refs[-4:]
    held = refs[0] if steps else None
    half = send.shape[1] // 2
    blocks = half // BLOCK

    def copies(step):
        at = step - steps
        return block_copies(first, half, step, gate, up, pair(streamed, at), sems.at[at])

    for step in range(steps, 2 * blocks):
        for copy in copies(step):
            copy.start()

    def add(out, start, source, block):
        both = jnp.dot(tokens[...], source[...], preferred_element_type=F32).astype(out.dtype)
        for i in range(2):
            column = pl.multiple_of((i * blocks + block - start) * BLOCK, BLOCK)
            out[:, pl.ds(column, BLOCK)] = both[:, i * BLOCK : (i + 1) * BLOCK]

    for side, out in enumerate((send, keep)):
        start, end = side * blocks, (side + 1) * blocks

        middle = min(max(steps, start), end)
        if start < middle:

            @pl.loop(start, middle)
            def _(step):
                add(out, start, pair(held, step), step)

        if middle < end:

            @pl.loop(middle, end)
            def _(step):
                for copy in copies(step):
                    copy.wait()
                add(out, start, pair(streamed, step - steps), step)


def stream_sums(tokens, gate, up, chunk, held=None):
    rows, depth = tokens.shape
    first, width = chunk
    steps = 0 if held is None else held.shape[1] // (2 * BLOCK)
    streamed = width // BLOCK - steps
    return pl.pallas_call(
        functools.partial(stream_kernel, first, steps),
        out_shape=(jax.ShapeDtypeStruct((rows, width), BF16), jax.ShapeDtypeStruct((rows, width), F32)),
        in_specs=[VMEM, HBM, HBM] + [VMEM] * (steps > 0),
        out_specs=(VMEM, VMEM),
        scratch_shapes=[
            pltpu.VMEM((depth, streamed * 2 * BLOCK), BF16),
            pltpu.SemaphoreType.DMA((streamed, 2)),
        ],
        compiler_params=pltpu.CompilerParams(vmem_limit_bytes=4 * streamed * depth * BLOCK + 4 * 2**20),
        cost_estimate=pl.CostEstimate(
            flops=4 * rows * depth * width, bytes_accessed=4 * depth * width, transcendentals=0
        ),
        name="stream_sums",
    )(tokens, left_in_hbm(gate), left_in_hbm(up), *([held_in(held)] if steps else []))


def partial_sums(first, half, sides, hiddens, weight, columns):
    core = lax.axis_index("sub")
    part = 0.0
    for side, hidden in zip(sides, hiddens):
        start = pl.multiple_of(first + jnp.where(core == side, 0, half), BLOCK)
        part += jnp.dot(hidden[...], weight[pl.ds(start, hidden.shape[1]), columns], preferred_element_type=F32)
    return part


def down_kernel(first, half, sides, weight, *refs):
    hiddens, out = refs[: len(sides)], refs[-1]
    totals = refs[len(sides) : -1]
    for at in range(0, out.shape[1], WIDE):
        columns = pl.ds(at, WIDE)
        part = partial_sums(first, half, sides, hiddens, weight, columns)
        for total in totals:
            part += total[:, columns]
        out[:, columns] = part


def last_down_kernel(first, half, sides, weight, hidden, total, own, *sends):
    rows, columns = own.shape[0] // 2, own.shape[1]
    for at in range(0, columns, WIDE):
        parts = []
        for start in (at, columns + at):
            part = partial_sums(first, half, sides, [hidden], weight, pl.ds(start, WIDE))
            parts.append(part + total[:, pl.ds(start, WIDE)])
        for place, out in enumerate((own, *sends)):
            pieces = [part[place * rows : (place + 1) * rows] for part in parts]
            out[:, pl.ds(at, WIDE)] = jnp.concatenate(pieces, axis=0).astype(out.dtype)


def down(weight, chunk, sides, hiddens, total=None, last=False, offset=0):
    rows, units = hiddens[0].shape
    half = chunk[1] // 2
    features = weight.shape[1]
    if last:
        packed = (rows // 2, features // 2)
        out_shape = (jax.ShapeDtypeStruct(packed, F32),) + (jax.ShapeDtypeStruct(packed, BF16),) * 3
        kernel = last_down_kernel
    else:
        out_shape = jax.ShapeDtypeStruct((rows, features), F32)
        kernel = down_kernel
    operands = [held_in(weight), *hiddens] + ([] if total is None else [total])
    return pl.pallas_call(
        functools.partial(kernel, chunk[0] + offset, half, sides),
        out_shape=out_shape,
        in_specs=[VMEM] * len(operands),
        out_specs=(VMEM,) * 4 if last else VMEM,
        compiler_params=GRANT,
        cost_estimate=pl.CostEstimate(
            flops=2 * rows * features * units * len(sides),
            bytes_accessed=2 * features * units * len(sides),
            transcendentals=0,
        ),
        name="down",
    )(*operands)


def split(units):
    more = units // 512 * 8 // 13 * 512
    return (0, more), (more, units - more)


def across(x, apart):
    return lax.ppermute(x, "wide", [(i, i ^ apart) for i in range(4)])


def chunked(tokens, gate_weight, up_weight, down_weight):
    rows = tokens.shape[0]
    chunks = split(gate_weight.shape[1])
    apart_by = (3, 1, 2)
    section = tokens
    for apart in apart_by:
        section = lax.optimization_barrier(jnp.concatenate([section, across(tokens, apart)], axis=0))

    def core_sums(send, keep):
        total = keep + swap(send, "sub").astype(F32)
        return total, total.astype(BF16)

    def hidden_half(total, received):
        return activate(*jnp.split(total + received.astype(F32), 2, axis=1))

    ready = beside(gate_weight)
    send = half_sums(section, gate_weight, up_weight, chunks[0], 0, ready)
    keep = half_sums(section, gate_weight, up_weight, chunks[0], 1, send)
    total, sent = core_sums(send, keep)
    later, _ = lax.optimization_barrier((section, sent))
    send, keep = stream_sums(later, gate_weight, up_weight, chunks[1])
    received, keep = lax.optimization_barrier((swap(sent, "narrow"), keep))
    mine = hidden_half(total, received)
    total, sent = core_sums(send, keep)
    other = swap(mine, "sub")
    mixed = down(down_weight, chunks[0], (0,), (mine,))
    half = chunks[1][1] // 2
    cut = half // BLOCK // 2 * BLOCK

    def part(x, start, end):
        return jnp.concatenate([x[:, start:end], x[:, half + start : half + end]], axis=1)

    received = [swap(part(sent, *ends), "narrow") for ends in ((0, cut), (cut, half))]
    received[0], mixed = lax.optimization_barrier((received[0], mixed))
    mine = hidden_half(part(total, 0, cut), received[0])
    mixed = down(down_weight, chunks[0], (1,), (other,), mixed)
    mixed = down(down_weight, chunks[1], (0, 1), (mine, swap(mine, "sub")), mixed)
    received[1], mixed = lax.optimization_barrier((received[1], mixed))
    mine = hidden_half(part(total, cut, half), received[1])
    mixed = down(down_weight, chunks[1], (0,), (mine,), mixed, offset=cut)
    out, *blocks = down(
        down_weight, chunks[1], (1,), (swap(mine, "sub"),), mixed, last=True, offset=cut
    )
    for apart in (3, 2, 1):
        block = blocks[apart_by.index(apart)]
        out = lax.optimization_barrier(out + across(block, apart).astype(F32))
    return out.astype(BF16).reshape(2, rows, -1).swapaxes(0, 1).reshape(rows, -1)


def solution(mesh):
    placed = (
        P(("groups", "wide"), ("narrow", "sub")),
        P(("narrow", "sub"), "wide"),
        P(("narrow", "sub"), "wide"),
        P("wide", ("narrow", "sub")),
    )
    sizes = tuple(mesh.shape[axis] for axis in ("groups", "wide", "narrow", "sub"))
    return jax.shard_map(
        chunked if sizes == (2, 4, 2, 2) else general,
        mesh=mesh,
        in_specs=placed,
        out_specs=P(("groups", "wide"), ("narrow", "sub")),
        check_vma=False,
    )
```
